256 devices in a mesh: exp: 32 (over y, x, core), tp: 8 (over z).
Axes of the slice: x: 4, y: 4, z: 8, core: 2. Of those that a mesh axis runs over, the one named last changes fastest.
Arguments:
- activations: bfloat16 [4096, 3584], P('exp'), may hold values from -6 to 6
- out_grad: bfloat16 [4096, 3584], P('exp'), may hold values from -6 to 6
- expert_ids: int32 [4096, 2], P('exp'), may hold values from 0 to 15, all different within a row; in each aligned block of 128 rows (0 to 127, 128 to 255, ...) at most 32 rows name the same one
- gate_values: float32 [4096, 2], P('exp'), may hold values from 0.1 to 0.9
- gate_proj: bfloat16 [32, 1536, 3584], P('exp', 'tp'), may hold values from -0.09375 to 0.09375
- up_proj: bfloat16 [32, 1536, 3584], P('exp', 'tp'), may hold values from -0.09375 to 0.09375
- down_proj: bfloat16 [32, 1536, 3584], P('exp', 'tp'), may hold values from -0.109375 to 0.109375
Outputs:
- in_grad: bfloat16 [4096, 3584], P('exp')
- gate_grad: bfloat16 [32, 1536, 3584], P('exp', 'tp')
- up_grad: bfloat16 [32, 1536, 3584], P('exp', 'tp')
- down_grad: bfloat16 [32, 1536, 3584], P('exp', 'tp')
The draws below stay inside these ranges and needn't reach their ends.
Inputs may be any that keep to these rules, and one draw needn't show every extreme that they name: `expert_ids`: each row names two different experts. Within the 128 rows of one index of exp no expert is named by more than 32 rows, and in some such block one expert is named by exactly 32 rows.
All inputs are finite; a program needn't handle non-finite values.
Results may differ from the reference program's by a relative error of at most 0.02.
Values may be sent and summed in bfloat16 or wider, within the bound.
No kernel may reach another device: no remote copies, remote signals or barrier semaphores. Data moves between devices by JAX's collectives and lax.ppermute only.
A program may use at most 128 MiB of HBM per device.

```python
import math
import jax
import jax.numpy as jnp
import numpy as np
from jax import lax

D = 3584
FF = 3072
TOK_EXP = 128
TOKENS = 4096
EXPERTS = 16
SLOTS = 32
N_EXP = 32
N_TP = 8


def block_scale(own_key, shape, shards, smallest, largest):
    def one(axis_at, parts):
        heights = jax.random.uniform(jax.random.fold_in(jax.random.fold_in(own_key, 6), axis_at), (parts,), jnp.float32, smallest / len(shards), largest / len(shards))
        return jnp.repeat(jnp.exp(heights), shape[axis_at] // parts).reshape((-1,) + (1,) * (len(shape) - axis_at - 1))

    gain = one(*shards[0])
    for cut in shards[1:]:
        gain = gain * one(*cut)
    return gain


def assign_block(key, own, number, rows, amount, top, bound, skew):
    order = jax.random.permutation(key, amount)
    crowded, usual = shares(amount, rows * top, bound, skew, True), shares(amount, rows * top, bound, skew, False)
    places = jnp.arange(amount)

    def named(sizes, turn):
        used = int((sizes > 0).sum())
        fixed = max(1, used // 4)
        shifted = fixed + (places - fixed + turn * (used - fixed)) % max(1, amount - fixed)
        return jnp.zeros((amount,), jnp.int32).at[order[jnp.where(places < fixed, places, shifted)]].set(jnp.asarray(sizes, jnp.int32))

    sizes = jnp.where(number % 4 == 0, named(crowded, number // 4), named(usual, number - number // 4 - 1))
    mixed = jax.random.permutation(jax.random.fold_in(own, 3), amount)
    source_of, receiver = mixed[0:amount // 2 * 2:2], mixed[1:amount // 2 * 2:2]
    margin = jnp.minimum(sizes[source_of] - 1, bound - sizes[receiver]) // 2
    margin = jnp.where((source_of == order[0]) | (receiver == order[0]) | (sizes[receiver] == 0), 0, jnp.maximum(margin, 0))
    shifted = jax.random.randint(jax.random.fold_in(own, 4), (amount // 2,), 0, 1 << 20) % (margin + 1)
    sizes = sizes.at[source_of].add(-shifted).at[receiver].add(shifted)
    members = jnp.searchsorted(jnp.cumsum(sizes), jnp.arange(rows * top), side="right").astype(jnp.int32)
    listing = members.reshape(top, rows).T
    listing = listing[jax.random.permutation(jax.random.fold_in(own, 1), rows)]
    turn = jax.random.randint(jax.random.fold_in(own, 2), (rows, 1), 0, top)
    return jnp.take_along_axis(listing, (jnp.arange(top)[None, :] + turn) % top, axis=1)


def shares(number_of, total, limit, skew, full):
    portions = [(1 << 20) // math.isqrt(grade ** skew) + 1 for grade in range(1, number_of + 1)]
    largest = limit if full else min(limit, max(-(-total // number_of), total * portions[0] // sum(portions)))
    least = 1 if total - largest >= number_of - 1 else 0
    holding, rest = [largest] + [least] * (number_of - 1), total - largest - least * (number_of - 1)
    while rest > 0:
        movable = [i for i in range(1, number_of) if holding[i] < largest] or [i for i in range(1, number_of) if holding[i] < limit]
        pool, left = sum([portions[i] for i in movable]), rest
        for i in movable:
            extra = min(limit - holding[i], max(1, left * portions[i] // pool), rest)
            holding[i] = holding[i] + extra
            rest = rest - extra
    return np.array(holding)


def gaussian(rng, shape, deviation, reach, cuts=(), kind=jnp.bfloat16):
    array = deviation * jax.random.normal(rng, shape, jnp.float32)
    if cuts:
        array = array * block_scale(rng, shape, cuts, -0.22, 0.18)
    return jnp.clip(array, -reach, reach).astype(kind)


def setup_inputs(seed: int = 0) -> dict:
    splits = jax.random.split(jax.random.key(seed), 8)
    activations = gaussian(splits[0], (TOKENS, D), 1.0, 6.0, ((0, 32),))
    out_grad = gaussian(splits[1], (TOKENS, D), 1.0, 6.0, ((0, 32),))
    expert_ids_keys = jax.random.split(jax.random.fold_in(splits[2], 1), TOKENS // TOK_EXP)
    expert_ids_turns = jax.random.permutation(jax.random.fold_in(splits[2], 3), TOKENS // TOK_EXP)
    expert_ids = jax.vmap(lambda own, number: assign_block(jax.random.fold_in(splits[2], 2), own, number, TOK_EXP, EXPERTS, 2, SLOTS, 2))(expert_ids_keys, expert_ids_turns).reshape((TOKENS, 2))
    gate_values = jnp.clip(0.1 + 0.79999997 * jax.random.uniform(splits[3], (TOKENS, 2), jnp.float32) ** block_scale(splits[3], (TOKENS, 2), ((0, 32),), -0.2, 0.2), 0.1, 0.9)
    gate_proj = gaussian(splits[4], (2 * EXPERTS, FF // 2, D), D ** -0.5, 0.09375, ((0, 32), (1, 8)))
    up_proj = gaussian(splits[5], (2 * EXPERTS, FF // 2, D), D ** -0.5, 0.09375, ((0, 32), (1, 8)))
    down_proj = gaussian(splits[6], (2 * EXPERTS, FF // 2, D), FF ** -0.5, 0.109375, ((0, 32), (1, 8)))
    return dict(activations=activations, out_grad=out_grad, expert_ids=expert_ids, gate_values=gate_values, gate_proj=gate_proj, up_proj=up_proj, down_proj=down_proj)


def route_tables(expert_ids, gate_values, experts, slot_count):
    tok_count = expert_ids.shape[0]
    flat_ids = expert_ids.reshape(-1)
    onehot = (flat_ids[:, None] == jnp.arange(experts, dtype=jnp.int32)[None, :]).astype(jnp.int32)
    before = jnp.cumsum(onehot, axis=0) - onehot
    ranking = jnp.sum(before * onehot, axis=1)
    slot_hot = (ranking[:, None] == jnp.arange(slot_count, dtype=jnp.int32)[None, :]).astype(jnp.float32)
    onehot_f = onehot.astype(jnp.float32)
    routing = jnp.einsum('pe,pc->pec', onehot_f, slot_hot).reshape(tok_count, 2, experts, slot_count)
    routing = jnp.transpose(jnp.sum(routing, axis=1), (1, 2, 0))
    weighted = jnp.sum(onehot_f.reshape(tok_count, 2, experts) * gate_values[:, :, None], axis=1)
    slot_gate = jnp.einsum('ect,te->ec', routing, weighted, precision=lax.Precision.HIGHEST)
    return routing, slot_gate


def dispatch(routing, slot_gate, activations, out_grad):
    select = routing.astype(jnp.bfloat16)
    sent_rows = jnp.einsum('ect,td->ecd', select, activations, preferred_element_type=jnp.float32).astype(jnp.bfloat16)
    picked = jnp.einsum('ect,td->ecd', select, out_grad, preferred_element_type=jnp.float32)
    sent_grads = (picked * slot_gate[:, :, None]).astype(jnp.bfloat16)
    return sent_rows, sent_grads


def expert_pass(rows_in, grads_in, gate_w, up_w, down_w, blocks):
    pre_gate = jnp.dot(rows_in, gate_w.T, preferred_element_type=jnp.float32)
    pre_up = jnp.dot(rows_in, up_w.T, preferred_element_type=jnp.float32)
    sigmoid_gate = jax.nn.sigmoid(pre_gate)
    silu_gate = pre_gate * sigmoid_gate
    hidden = (silu_gate * pre_up).astype(jnp.bfloat16)
    back = jnp.dot(grads_in, down_w.T, preferred_element_type=jnp.float32)
    d_gate = (back * pre_up * sigmoid_gate * (1.0 + pre_gate * (1.0 - sigmoid_gate))).astype(jnp.bfloat16)
    d_up = (back * silu_gate).astype(jnp.bfloat16)
    row_count = rows_in.shape[0]
    model_width = rows_in.shape[1]
    unit_count = gate_w.shape[0] // blocks
    gate_blocks = d_gate.astype(jnp.float32).reshape(row_count, blocks, unit_count)
    up_blocks = d_up.astype(jnp.float32).reshape(row_count, blocks, unit_count)
    gate_rows = gate_w.astype(jnp.float32).reshape(blocks, unit_count, model_width)
    up_rows = up_w.astype(jnp.float32).reshape(blocks, unit_count, model_width)
    pieces = jnp.einsum('sbu,bud->bsd', gate_blocks, gate_rows, precision=lax.Precision.HIGHEST)
    pieces = pieces + jnp.einsum('sbu,bud->bsd', up_blocks, up_rows, precision=lax.Precision.HIGHEST)
    summed = jnp.sum(pieces.astype(jnp.bfloat16).astype(jnp.float32), axis=0)
    gate_g = jnp.dot(d_gate.T, rows_in, preferred_element_type=jnp.float32).astype(jnp.bfloat16)
    up_g = jnp.dot(d_up.T, rows_in, preferred_element_type=jnp.float32).astype(jnp.bfloat16)
    down_g = jnp.dot(hidden.T, grads_in, preferred_element_type=jnp.float32).astype(jnp.bfloat16)
    return summed, gate_g, up_g, down_g


def reference(activations, out_grad, expert_ids, gate_values, gate_proj, up_proj, down_proj):
    blocks = 2 * N_TP
    acts_blocks = activations.reshape(N_EXP, TOK_EXP, D)
    grad_blocks = out_grad.reshape(N_EXP, TOK_EXP, D)
    id_blocks = expert_ids.reshape(N_EXP, TOK_EXP, 2)
    gate_blocks = gate_values.reshape(N_EXP, TOK_EXP, 2)

    def build(inputs):
        ids_here, gates_here, acts_here, grads_here = inputs
        routing, slot_gate = route_tables(ids_here, gates_here, EXPERTS, SLOTS)
        sent_rows, sent_grads = dispatch(routing, slot_gate, acts_here, grads_here)
        return routing, sent_rows, sent_grads

    routings, all_rows, all_grads = lax.map(build, (id_blocks, gate_blocks, acts_blocks, grad_blocks))
    all_rows = jnp.transpose(all_rows, (1, 0, 2, 3)).reshape(EXPERTS, N_EXP * SLOTS, D)
    all_grads = jnp.transpose(all_grads, (1, 0, 2, 3)).reshape(EXPERTS, N_EXP * SLOTS, D)
    gate_full = gate_proj.reshape(EXPERTS, FF, D)
    up_full = up_proj.reshape(EXPERTS, FF, D)
    down_full = down_proj.reshape(EXPERTS, FF, D)

    def per_expert(inputs):
        return expert_pass(inputs[0], inputs[1], inputs[2], inputs[3], inputs[4], blocks)

    terms, gate_g, up_g, down_g = lax.map(per_expert, (all_rows, all_grads, gate_full, up_full, down_full))
    terms = jnp.transpose(terms.reshape(EXPERTS, N_EXP, SLOTS, D), (1, 0, 2, 3))
    in_grad = jnp.einsum('bect,becd->btd', routings, terms, precision=lax.Precision.HIGHEST)
    in_grad = in_grad.reshape(TOKENS, D).astype(jnp.bfloat16)
    return (in_grad, gate_g.reshape(2 * EXPERTS, FF // 2, D), up_g.reshape(2 * EXPERTS, FF // 2, D),
            down_g.reshape(2 * EXPERTS, FF // 2, D))
```

```python
import functools

import jax
import jax.numpy as jnp
from jax import lax
from jax.experimental import pallas as pl
from jax.experimental.pallas import tpu as pltpu
from jax.sharding import PartitionSpec as P

F32 = jnp.float32
BF16 = jnp.bfloat16
VMEM = pltpu.VMEM
LIMIT = 48 * 1024 * 1024


def table(ids, experts):
    toks = ids.shape[1]
    expert = lax.broadcasted_iota(jnp.int32, (experts, toks), 0)
    first = ids[0:1, :] == expert
    second = ids[1:2, :] == expert
    named = jnp.where(first | second, 1.0, 0.0)
    earlier = lax.broadcasted_iota(jnp.int32, (toks, toks), 0)
    later = lax.broadcasted_iota(jnp.int32, (toks, toks), 1)
    before = jnp.where(earlier < later, 1.0, 0.0).astype(BF16)
    rank = jnp.dot(named.astype(BF16), before, preferred_element_type=F32)
    return first, second, jnp.where(named > 0.0, rank, -1.0)


def send_kernel(half, tp_ref, ids_ref, gate_ref, act_ref, grad_ref, far_ref, near_ref):
    experts = near_ref.shape[1] // 2
    toks = ids_ref.shape[1]
    first, second, rank = table(ids_ref[...], experts)
    gate = jnp.where(first, gate_ref[0:1, :], 0.0) + jnp.where(second, gate_ref[1:2, :], 0.0)
    acts = act_ref[...]
    grads = grad_ref[...]

    def select(slots, count):
        hit = (rank[:, None, :] == slots).reshape(experts * count, toks)
        weight = jnp.broadcast_to(gate[:, None, :], (experts, count, toks)).reshape(
            experts * count, toks
        )
        scale = jnp.sum(jnp.where(hit, weight, 0.0), axis=1, keepdims=True)
        mask = jnp.where(hit, 1.0, 0.0).astype(BF16)
        rows = jnp.dot(mask, acts, preferred_element_type=F32).astype(BF16)
        picked = jnp.dot(mask, grads, preferred_element_type=F32)
        return rows, (picked * scale).astype(BF16)

    slots = lax.broadcasted_iota(jnp.int32, (experts, half, toks), 1).astype(F32)
    rows, weighted = select(slots, half)
    far_ref[:, 0] = rows.reshape(far_ref.shape[0], half // 2, -1)
    far_ref[:, 1] = weighted.reshape(far_ref.shape[0], half // 2, -1)
    inner = lax.broadcasted_iota(jnp.int32, (experts, 8, toks), 1)
    slots = jnp.where(inner < 2, half + 2 * tp_ref[0] + inner, -2).astype(F32)
    rows, weighted = select(slots, 8)
    near_ref[0] = rows.reshape(experts, 8, -1)[:, :2].reshape(2 * experts, -1)
    near_ref[1] = weighted.reshape(experts, 8, -1)[:, :2].reshape(2 * experts, -1)


def make_send(tp_at, ids_t, gate_t, acts, grads, experts, half):
    toks, width = acts.shape
    tile = width // 7 if width % (7 * 128) == 0 else width
    return pl.pallas_call(
        functools.partial(send_kernel, half),
        grid=(width // tile,),
        in_specs=[
            pl.BlockSpec(memory_space=pltpu.SMEM),
            pl.BlockSpec((2, toks), lambda i: (0, 0)),
            pl.BlockSpec((2, toks), lambda i: (0, 0)),
            pl.BlockSpec((toks, tile), lambda i: (0, i)),
            pl.BlockSpec((toks, tile), lambda i: (0, i)),
        ],
        out_specs=[
            pl.BlockSpec((2 * experts, 2, half // 2, tile), lambda i: (0, 0, 0, i)),
            pl.BlockSpec((2, 2 * experts, tile), lambda i: (0, 0, i)),
        ],
        out_shape=[
            jax.ShapeDtypeStruct((2 * experts, 2, half // 2, width), BF16),
            jax.ShapeDtypeStruct((2, 2 * experts, width), BF16),
        ],
        compiler_params=pltpu.CompilerParams(vmem_limit_bytes=LIMIT),
    )(tp_at, ids_t, gate_t, acts, grads)


def expert_kernel(src_ref, pair_ref, down_ref, part_ref, side_ref, pre_acc, back_acc, dgu_ref):
    outer, _, inner, width = src_ref.shape
    rows = outer * inner
    units = down_ref.shape[0]
    quarter = part_ref.shape[2]
    contract = (((1,), (1,)), ((), ()))
    pre = jnp.zeros((rows, 2 * units), F32)
    back = jnp.zeros((rows, units), F32)
    pre_acc[...] = pre
    back_acc[...] = back
    step = quarter

    @pl.loop(0, width // step)
    def _(i):
        at = pl.ds(pl.multiple_of(i * step, step), step)
        x = src_ref[:, 0, :, at].reshape(rows, step)
        g = src_ref[:, 1, :, at].reshape(rows, step)
        pre_acc[...] += lax.dot_general(x, pair_ref[:, at], contract, preferred_element_type=F32)
        back_acc[...] += lax.dot_general(g, down_ref[:, at], contract, preferred_element_type=F32)

    pre_gate = pre_acc[:, :units]
    pre_up = pre_acc[:, units:]
    back = back_acc[...]
    sig = jax.nn.sigmoid(pre_gate)
    silu = pre_gate * sig
    hidden = (silu * pre_up).astype(BF16)
    d_gate = (back * pre_up * sig * (1.0 + pre_gate * (1.0 - sig))).astype(BF16)
    d_up = (back * silu).astype(BF16)
    dgu_ref[:, :units] = d_gate
    dgu_ref[:, units:] = d_up
    side_ref[:units, :] = d_gate.T
    side_ref[units : 2 * units, :] = d_up.T
    side_ref[2 * units :, :] = hidden.T

    @pl.loop(0, part_ref.shape[0])
    def _(q):
        at = pl.ds(pl.multiple_of(q * quarter, quarter), quarter)
        part_ref[q] = jnp.dot(
            dgu_ref[...], pair_ref[:, at], preferred_element_type=F32
        ).astype(BF16)


def expert_part(src, pair_w, down_w, quarters):
    outer, _, inner, width = src.shape
    rows = outer * inner
    units = down_w.shape[0]
    return pl.pallas_call(
        expert_kernel,
        in_specs=[pl.BlockSpec(memory_space=VMEM)] * 3,
        out_specs=[pl.BlockSpec(memory_space=VMEM)] * 2,
        out_shape=[
            jax.ShapeDtypeStruct((quarters, rows, width // quarters), BF16),
            jax.ShapeDtypeStruct((3 * units, rows), BF16),
        ],
        scratch_shapes=[
            VMEM((rows, 2 * units), F32),
            VMEM((rows, units), F32),
            VMEM((rows, 2 * units), BF16),
        ],
        compiler_params=pltpu.CompilerParams(vmem_limit_bytes=LIMIT),
        cost_estimate=pl.CostEstimate(
            flops=10 * rows * width * units,
            bytes_accessed=2 * (3 * rows * width + 3 * units * width),
            transcendentals=rows * units,
        ),
    )(src, pair_w, down_w)


def weight_kernel(count, *refs):
    sources, sides = refs[:count], refs[count : 2 * count]
    gate_ref, up_ref, down_ref = refs[2 * count :]
    units = gate_ref.shape[0]
    pair, down = None, None
    for src_ref, side_ref in zip(sources, sides):
        outer, _, inner, tile = src_ref.shape
        x = src_ref[:, 0].reshape(outer * inner, tile)
        g = src_ref[:, 1].reshape(outer * inner, tile)
        one = jnp.dot(side_ref[: 2 * units, :], x, preferred_element_type=F32)
        two = jnp.dot(side_ref[2 * units :, :], g, preferred_element_type=F32)
        pair = one if pair is None else pair + one
        down = two if down is None else down + two
    gate_ref[...] = pair[:units].astype(BF16)
    up_ref[...] = pair[units:].astype(BF16)
    down_ref[...] = down.astype(BF16)


def weight_grads(sources, sides):
    width = sources[0].shape[3]
    units = sides[0].shape[0] // 3
    rows = sum(side.shape[1] for side in sides)
    tile = 256 if width % 256 == 0 else width
    return pl.pallas_call(
        functools.partial(weight_kernel, len(sources)),
        grid=(width // tile,),
        in_specs=[
            pl.BlockSpec(src.shape[:3] + (tile,), lambda i: (0, 0, 0, i)) for src in sources
        ]
        + [pl.BlockSpec(side.shape, lambda i: (0, 0)) for side in sides],
        out_specs=[pl.BlockSpec((units, tile), lambda i: (0, i))] * 3,
        out_shape=[jax.ShapeDtypeStruct((units, width), BF16)] * 3,
        compiler_params=pltpu.CompilerParams(vmem_limit_bytes=LIMIT),
        cost_estimate=pl.CostEstimate(
            flops=6 * rows * width * units,
            bytes_accessed=2 * (2 * rows * width + 3 * units * width),
            transcendentals=0,
        ),
    )(*sources, *sides)


def combine_kernel(half, tp_ref, ids_ref, back_ref, out_ref):
    experts = back_ref.shape[0] // 2
    per_core = back_ref.shape[1]
    toks = ids_ref.shape[1]
    _, _, rank = table(ids_ref[...], experts)
    shape = (experts, 2 * per_core, toks)
    row = lax.broadcasted_iota(jnp.int32, shape, 1)
    core, inner = row // per_core, row % per_core
    slots = jnp.where(tp_ref[0] % 2 == 0, row, half + 2 * inner + core).astype(F32)
    hit = jnp.where(rank[:, None, :] == slots, 1.0, 0.0).astype(BF16)
    hit = hit.reshape(2 * experts * per_core, toks)
    out_ref[...] = lax.dot_general(
        hit,
        back_ref[...].reshape(2 * experts * per_core, -1),
        (((0,), (0,)), ((), ())),
        preferred_element_type=F32,
    ).astype(BF16)


def combine(tp_at, ids_t, returned, half):
    toks = ids_t.shape[1]
    return pl.pallas_call(
        functools.partial(combine_kernel, half),
        in_specs=[
            pl.BlockSpec(memory_space=pltpu.SMEM),
            pl.BlockSpec(memory_space=VMEM),
            pl.BlockSpec(memory_space=VMEM),
        ],
        out_specs=pl.BlockSpec(memory_space=VMEM),
        out_shape=jax.ShapeDtypeStruct((toks, returned.shape[2]), BF16),
        compiler_params=pltpu.CompilerParams(vmem_limit_bytes=LIMIT),
    )(tp_at, ids_t, returned)


def per_device(activations, out_grad, expert_ids, gate_values, gate_proj, up_proj, down_proj):
    devices = lax.axis_size("exp")
    planes = lax.axis_size("tp")
    experts = devices // 2
    toks, width = activations.shape
    slots = 8 * toks // devices
    half = slots // 2
    quarters = planes // 2
    tp_at = lax.axis_index("tp").astype(jnp.int32)[None]
    ids_t = expert_ids.T
    gate_t = gate_values.T
    swap = [(i, i ^ 1) for i in range(devices)]

    def trade(v):
        return lax.ppermute(v, "exp", swap)

    def spread(v):
        return lax.all_to_all(v, "exp", split_axis=0, concat_axis=0, tiled=True)

    far, near = make_send(tp_at, ids_t, gate_t, activations, out_grad, experts, half)
    near = spread(jnp.transpose(near, (1, 0, 2)))
    near, far = lax.optimization_barrier((near, far))
    near = jnp.transpose(near, (1, 0, 2))
    near = lax.all_gather(near, "tp", axis=0, tiled=False)
    far = spread(far.reshape(devices, half, width)).reshape(far.shape)
    pair_w = jnp.concatenate([gate_proj[0], up_proj[0]], axis=0)
    down_w = down_proj[0]
    far_other = trade(far)
    far_part, far_side = expert_part(far, pair_w, down_w, quarters)
    far_other_part, far_other_side = expert_part(far_other, pair_w, down_w, quarters)
    far_sent = trade(far_other_part)
    near_other = trade(near)
    near_other_part, near_other_side = expert_part(near_other, pair_w, down_w, quarters)
    near_sent = trade(near_other_part)
    near_part, near_side = expert_part(near, pair_w, down_w, quarters)
    far_sum = (far_part.astype(F32) + far_sent.astype(F32)).astype(BF16)
    near_sum = (near_part.astype(F32) + near_sent.astype(F32)).astype(BF16)
    both = jnp.stack([far_sum, near_sum], axis=1)
    both = both.reshape((planes,) + far_sum.shape[1:])
    mine = lax.psum_scatter(both, "tp", scatter_dimension=0, tiled=False)
    straight = mine.reshape(devices, half // 2, -1)
    turned = jnp.transpose(mine.reshape(half // 2, devices, -1), (1, 0, 2))
    returned = spread(jnp.where(tp_at[0] % 2 == 0, straight, turned))
    piece = combine(tp_at, ids_t, returned, half)
    gathered = lax.all_gather(piece, "tp", axis=0, tiled=False)
    gathered = gathered.reshape(quarters, 2, toks, width // quarters).astype(F32)
    in_grad = jnp.transpose((gathered[:, 0] + gathered[:, 1]).astype(BF16), (1, 0, 2))
    in_grad = in_grad.reshape(toks, width)
    gate_g, up_g, down_g = weight_grads(
        [far, far_other, near, near_other],
        [far_side, far_other_side, near_side, near_other_side],
    )
    return (in_grad, gate_g[None], up_g[None], down_g[None])


def solution(mesh):
    return jax.shard_map(
        per_device,
        mesh=mesh,
        in_specs=(
            P("exp", None),
            P("exp", None),
            P("exp", None),
            P("exp", None),
            P("exp", "tp", None),
            P("exp", "tp", None),
            P("exp", "tp", None),
        ),
        out_specs=(
            P("exp", None),
            P("exp", "tp", None),
            P("exp", "tp", None),
            P("exp", "tp", None),
        ),
        check_vma=False,
    )
```

```python
import functools

import jax
import jax.numpy as jnp
from jax import lax
from jax.experimental import pallas as pl
from jax.experimental.pallas import tpu as pltpu
from jax.sharding import PartitionSpec as P

F32 = jnp.float32
BF16 = jnp.bfloat16
VMEM = pltpu.VMEM
LIMIT = 48 * 1024 * 1024


def padded(columns):
    return -(-columns // 128) * 128


def fill_pieces(out_ref, total, wide):
    for j in range(out_ref.shape[0]):
        out_ref[j, :, :wide] = total[:, j * wide : (j + 1) * wide]
        if out_ref.shape[2] > wide:
            out_ref[j, :, wide:] = jnp.zeros_like(out_ref[j, :, wide:])


def table(ids, experts):
    toks = ids.shape[1]
    expert = lax.broadcasted_iota(jnp.int32, (experts, toks), 0)
    first = ids[0:1, :] == expert
    second = ids[1:2, :] == expert
    named = jnp.where(first | second, 1.0, 0.0)
    earlier = lax.broadcasted_iota(jnp.int32, (toks, toks), 0)
    later = lax.broadcasted_iota(jnp.int32, (toks, toks), 1)
    before = jnp.where(earlier < later, 1.0, 0.0).astype(BF16)
    rank = jnp.dot(named.astype(BF16), before, preferred_element_type=F32)
    return first, second, jnp.where(named > 0.0, rank, -1.0)


def send_kernel(half, tp_ref, ids_ref, gate_ref, act_ref, grad_ref, far_ref, near_ref):
    experts = near_ref.shape[1] // 2
    toks = ids_ref.shape[1]
    first, second, rank = table(ids_ref[...], experts)
    gate = jnp.where(first, gate_ref[0:1, :], 0.0) + jnp.where(second, gate_ref[1:2, :], 0.0)
    acts = act_ref[...]
    grads = grad_ref[...]

    def select(slots, count):
        hit = (rank[:, None, :] == slots).reshape(experts * count, toks)
        weight = jnp.broadcast_to(gate[:, None, :], (experts, count, toks)).reshape(
            experts * count, toks
        )
        scale = jnp.sum(jnp.where(hit, weight, 0.0), axis=1, keepdims=True)
        mask = jnp.where(hit, 1.0, 0.0).astype(BF16)
        rows = jnp.dot(mask, acts, preferred_element_type=F32).astype(BF16)
        picked = jnp.dot(mask, grads, preferred_element_type=F32)
        return rows, (picked * scale).astype(BF16)

    slots = lax.broadcasted_iota(jnp.int32, (experts, half, toks), 1).astype(F32)
    rows, weighted = select(slots, half)
    far_ref[:, 0] = rows.reshape(far_ref.shape[0], half // 2, -1)
    far_ref[:, 1] = weighted.reshape(far_ref.shape[0], half // 2, -1)
    inner = lax.broadcasted_iota(jnp.int32, (experts, 8, toks), 1)
    slots = jnp.where(inner < 2, half + 2 * tp_ref[0] + inner, -2).astype(F32)
    rows, weighted = select(slots, 8)
    near_ref[0] = rows.reshape(experts, 8, -1)[:, :2].reshape(2 * experts, -1)
    near_ref[1] = weighted.reshape(experts, 8, -1)[:, :2].reshape(2 * experts, -1)


def make_send(tp_at, ids_t, gate_t, acts, grads, experts, half):
    toks, width = acts.shape
    tile = width // 7 if width % (7 * 128) == 0 else width
    return pl.pallas_call(
        functools.partial(send_kernel, half),
        grid=(width // tile,),
        in_specs=[
            pl.BlockSpec(memory_space=pltpu.SMEM),
            pl.BlockSpec((2, toks), lambda i: (0, 0)),
            pl.BlockSpec((2, toks), lambda i: (0, 0)),
            pl.BlockSpec((toks, tile), lambda i: (0, i)),
            pl.BlockSpec((toks, tile), lambda i: (0, i)),
        ],
        out_specs=[
            pl.BlockSpec((2 * experts, 2, half // 2, tile), lambda i: (0, 0, 0, i)),
            pl.BlockSpec((2, 2 * experts, tile), lambda i: (0, 0, i)),
        ],
        out_shape=[
            jax.ShapeDtypeStruct((2 * experts, 2, half // 2, width), BF16),
            jax.ShapeDtypeStruct((2, 2 * experts, width), BF16),
        ],
        compiler_params=pltpu.CompilerParams(vmem_limit_bytes=LIMIT),
    )(tp_at, ids_t, gate_t, acts, grads)


def expert_kernel(turn, src_ref, pair_ref, down_ref, part_ref, side_ref, pre_acc, back_acc, dgu_ref):
    outer, _, inner, width = src_ref.shape
    rows = outer * inner
    units = down_ref.shape[0]
    contract = (((1,), (1,)), ((), ()))
    phase, at = pl.program_id(0), pl.program_id(1)

    @pl.when(phase == 0)
    def _():
        x = src_ref[:, 0].reshape(rows, width)
        g = src_ref[:, 1].reshape(rows, width)
        pre = lax.dot_general(x, pair_ref[...], contract, preferred_element_type=F32)
        back = lax.dot_general(g, down_ref[...], contract, preferred_element_type=F32)

        @pl.when(at == 0)
        def _():
            pre_acc[...] = pre
            back_acc[...] = back

        @pl.when(at > 0)
        def _():
            pre_acc[...] += pre
            back_acc[...] += back

    @pl.when((phase == 0) & (at == pl.num_programs(1) - 1))
    def _():
        pre_gate = pre_acc[:, :units]
        pre_up = pre_acc[:, units:]
        back = back_acc[...]
        sig = jax.nn.sigmoid(pre_gate)
        silu = pre_gate * sig
        hidden = (silu * pre_up).astype(BF16)
        d_gate = (back * pre_up * sig * (1.0 + pre_gate * (1.0 - sig))).astype(BF16)
        d_up = (back * silu).astype(BF16)
        side_ref[:units, :] = d_gate.T
        side_ref[units : 2 * units, :] = d_up.T
        side_ref[2 * units :, :] = hidden.T
        dgu_ref[:, :units] = d_gate
        dgu_ref[:, units:] = d_up
        if turn:
            to = lax.broadcasted_iota(jnp.int32, (rows, rows), 0)
            of = lax.broadcasted_iota(jnp.int32, (rows, rows), 1)
            moved = jnp.where(of == (to % outer) * inner + to // outer, 1.0, 0.0).astype(BF16)
            dgu_ref[...] = jnp.dot(moved, dgu_ref[...], preferred_element_type=F32).astype(BF16)

    @pl.when(phase == 1)
    def _():
        part = jnp.dot(dgu_ref[...], pair_ref[...], preferred_element_type=F32).astype(BF16)
        fill_pieces(part_ref, part, part.shape[1] // part_ref.shape[0])


def expert_part(src, pair_w, down_w, pieces, turn):
    outer, _, inner, width = src.shape
    rows = outer * inner
    units = down_w.shape[0]
    steps = 2
    tile = width // steps
    each = max(1, pieces // steps)
    last = steps - 1
    if pieces > 1:
        wide = padded(width // pieces)
        part_spec = pl.BlockSpec((each, rows, wide), lambda p, i: (p * i, 0, 0))
    else:
        wide = width
        part_spec = pl.BlockSpec((1, rows, tile), lambda p, i: (0, 0, p * i))
    return pl.pallas_call(
        functools.partial(expert_kernel, turn),
        grid=(2, steps),
        in_specs=[
            pl.BlockSpec((outer, 2, inner, tile), lambda p, i: (0, 0, 0, jnp.where(p == 0, i, last))),
            pl.BlockSpec((2 * units, tile), lambda p, i: (0, i)),
            pl.BlockSpec((units, tile), lambda p, i: (0, jnp.where(p == 0, i, last))),
        ],
        out_specs=[part_spec, pl.BlockSpec((3 * units, rows), lambda p, i: (0, 0))],
        out_shape=[
            jax.ShapeDtypeStruct((pieces, rows, wide), BF16),
            jax.ShapeDtypeStruct((3 * units, rows), BF16),
        ],
        scratch_shapes=[
            VMEM((rows, 2 * units), F32),
            VMEM((rows, units), F32),
            VMEM((rows, 2 * units), BF16),
        ],
        compiler_params=pltpu.CompilerParams(vmem_limit_bytes=LIMIT),
        cost_estimate=pl.CostEstimate(
            flops=40 * rows * width * units,
            bytes_accessed=2 * (3 * rows * width + 3 * units * width),
            transcendentals=rows * units,
        ),
    )(src, pair_w, down_w)


def weight_kernel(count, *refs):
    sources, sides = refs[:count], refs[count : 2 * count]
    gate_ref, up_ref, down_ref = refs[2 * count :]
    units = gate_ref.shape[0]
    tile = sources[0].shape[3]

    def stacked(kind):
        return jnp.concatenate([s[:, kind].reshape(-1, tile) for s in sources], axis=0)

    left = jnp.concatenate([s[: 2 * units] for s in sides], axis=1)
    pair = jnp.dot(left, stacked(0), preferred_element_type=F32)
    left = jnp.concatenate([s[2 * units :] for s in sides], axis=1)
    down = jnp.dot(left, stacked(1), preferred_element_type=F32)
    gate_ref[...] = pair[:units].astype(BF16)
    up_ref[...] = pair[units:].astype(BF16)
    down_ref[...] = down.astype(BF16)


def weight_grads(sources, sides):
    width = sources[0].shape[3]
    units = sides[0].shape[0] // 3
    rows = sum(side.shape[1] for side in sides)
    tile = width // 4
    return pl.pallas_call(
        functools.partial(weight_kernel, len(sources)),
        grid=(width // tile,),
        in_specs=[
            pl.BlockSpec(src.shape[:3] + (tile,), lambda i: (0, 0, 0, i)) for src in sources
        ]
        + [pl.BlockSpec(side.shape, lambda i: (0, 0)) for side in sides],
        out_specs=[pl.BlockSpec((units, tile), lambda i: (0, i))] * 3,
        out_shape=[jax.ShapeDtypeStruct((units, width), BF16)] * 3,
        compiler_params=pltpu.CompilerParams(vmem_limit_bytes=LIMIT),
        cost_estimate=pl.CostEstimate(
            flops=24 * rows * width * units,
            bytes_accessed=2 * (2 * rows * width + 3 * units * width),
            transcendentals=0,
        ),
    )(*sources, *sides)


def near_combine_kernel(half, ids_ref, back_ref, out_ref):
    experts, per_core = back_ref.shape[0] // 2, back_ref.shape[1]
    toks = ids_ref.shape[1]
    _, _, rank = table(ids_ref[...], experts)
    row = lax.broadcasted_iota(jnp.int32, (experts, 2 * per_core, toks), 1)
    slots = (half + 2 * (row % per_core) + row // per_core).astype(F32)
    total = gather_slots(rank, slots, back_ref[...])
    fill_pieces(out_ref, total.astype(BF16), total.shape[1] // out_ref.shape[0])


def far_combine_kernel(ids_ref, back_ref, near_ref, out_ref):
    experts, per_core = back_ref.shape[0] // 2, back_ref.shape[1]
    toks = ids_ref.shape[1]
    _, _, rank = table(ids_ref[...], experts)
    slots = lax.broadcasted_iota(jnp.int32, (experts, 2 * per_core, toks), 1).astype(F32)
    total = gather_slots(rank, slots, back_ref[...])
    out_ref[...] = (total + near_ref[...].astype(F32)).astype(BF16)


def gather_slots(rank, slots, rows):
    count = rows.shape[0] * rows.shape[1]
    hit = jnp.where(rank[:, None, :] == slots, 1.0, 0.0).astype(BF16).reshape(count, -1)
    return lax.dot_general(
        hit, rows.reshape(count, -1), (((0,), (0,)), ((), ())), preferred_element_type=F32
    )


def near_combine(ids_t, returned, pieces, half):
    toks = ids_t.shape[1]
    width = returned.shape[2]
    wide = padded(width // pieces)
    steps = 2
    return pl.pallas_call(
        functools.partial(near_combine_kernel, half),
        grid=(steps,),
        in_specs=[
            pl.BlockSpec(ids_t.shape, lambda i: (0, 0)),
            pl.BlockSpec(returned.shape[:2] + (width // steps,), lambda i: (0, 0, i)),
        ],
        out_specs=pl.BlockSpec((pieces // steps, toks, wide), lambda i: (i, 0, 0)),
        out_shape=jax.ShapeDtypeStruct((pieces, toks, wide), BF16),
        compiler_params=pltpu.CompilerParams(vmem_limit_bytes=LIMIT),
    )(ids_t, returned)


def far_combine(ids_t, returned, near):
    return pl.pallas_call(
        far_combine_kernel,
        in_specs=[pl.BlockSpec(memory_space=VMEM)] * 3,
        out_specs=pl.BlockSpec(memory_space=VMEM),
        out_shape=jax.ShapeDtypeStruct(near.shape, BF16),
        compiler_params=pltpu.CompilerParams(vmem_limit_bytes=LIMIT),
    )(ids_t, returned, near)


def per_device(activations, out_grad, expert_ids, gate_values, gate_proj, up_proj, down_proj):
    devices = lax.axis_size("exp")
    planes = lax.axis_size("tp")
    experts = devices // 2
    toks, width = activations.shape
    slots = 8 * toks // devices
    half = slots // 2
    tp_at = lax.axis_index("tp").astype(jnp.int32)[None]
    ids_t = expert_ids.T
    gate_t = gate_values.T
    swap = [(i, i ^ 1) for i in range(devices)]

    def trade(v):
        return lax.ppermute(v, "exp", swap)

    def spread(v):
        return lax.all_to_all(v, "exp", split_axis=0, concat_axis=0, tiled=True)

    far, near = make_send(tp_at, ids_t, gate_t, activations, out_grad, experts, half)
    near = spread(jnp.transpose(near, (1, 0, 2)))
    near, far = lax.optimization_barrier((near, far))
    near = jnp.transpose(near, (1, 0, 2))
    near = lax.all_gather(near, "tp", axis=0, tiled=False)
    far = spread(far.reshape(devices, half, width)).reshape(far.shape)
    pair_w = jnp.concatenate([gate_proj[0], up_proj[0]], axis=0)
    down_w = down_proj[0]
    far_other = trade(far)
    near_other = trade(near)
    far_part, far_side = expert_part(far, pair_w, down_w, planes, False)
    far_other, far_part = lax.optimization_barrier((far_other, far_part))
    far_other_part, far_other_side = expert_part(far_other, pair_w, down_w, planes, False)
    far_sum = (far_part.astype(F32) + trade(far_other_part).astype(F32)).astype(BF16)
    near_other, far_other_part = lax.optimization_barrier((near_other, far_other_part))
    near_other_part, near_other_side = expert_part(near_other, pair_w, down_w, 1, True)
    near_part, near_side = expert_part(near, pair_w, down_w, 1, True)
    near_sum = (near_part.astype(F32) + trade(near_other_part).astype(F32)).astype(BF16)
    far_mine = lax.psum_scatter(far_sum, "tp", scatter_dimension=0, tiled=False)
    near_back = spread(near_sum.reshape(devices, half // 2, width))
    near_mine = near_combine(ids_t, near_back, planes, half)
    near_mine = lax.psum_scatter(near_mine, "tp", scatter_dimension=0, tiled=False)
    far_back = spread(far_mine.reshape(devices, half // 2, -1))
    piece = far_combine(ids_t, far_back, near_mine)
    gathered = lax.all_gather(piece, "tp", axis=0, tiled=False)
    gathered = gathered[:, :, : width // planes]
    in_grad = jnp.transpose(gathered, (1, 0, 2)).reshape(toks, width)
    gate_g, up_g, down_g = weight_grads(
        [far, far_other, near, near_other],
        [far_side, far_other_side, near_side, near_other_side],
    )
    return (in_grad, gate_g[None], up_g[None], down_g[None])


def solution(mesh):
    return jax.shard_map(
        per_device,
        mesh=mesh,
        in_specs=(
            P("exp", None),
            P("exp", None),
            P("exp", None),
            P("exp", None),
            P("exp", "tp", None),
            P("exp", "tp", None),
            P("exp", "tp", None),
        ),
        out_specs=(
            P("exp", None),
            P("exp", "tp", None),
            P("exp", "tp", None),
            P("exp", "tp", None),
        ),
        check_vma=False,
    )
```

```python
import functools

import jax
import jax.numpy as jnp
from jax import lax
from jax.experimental import pallas as pl
from jax.experimental.pallas import tpu as pltpu
from jax.sharding import PartitionSpec as P

F32 = jnp.float32
BF16 = jnp.bfloat16
VMEM = pltpu.VMEM
LIMIT = 48 * 1024 * 1024


def table(ids, experts):
    toks = ids.shape[1]
    expert = lax.broadcasted_iota(jnp.int32, (experts, toks), 0)
    first = ids[0:1, :] == expert
    second = ids[1:2, :] == expert
    named = jnp.where(first | second, 1.0, 0.0)
    earlier = lax.broadcasted_iota(jnp.int32, (toks, toks), 0)
    later = lax.broadcasted_iota(jnp.int32, (toks, toks), 1)
    before = jnp.where(earlier < later, 1.0, 0.0).astype(BF16)
    rank = jnp.dot(named.astype(BF16), before, preferred_element_type=F32)
    return first, second, jnp.where(named > 0.0, rank, -1.0)


def select(ids_ref, gate_ref, act_ref, grad_ref, slots):
    experts, count, toks = slots.shape
    first, second, rank = table(ids_ref[...], experts)
    gate = jnp.where(first, gate_ref[0:1, :], 0.0) + jnp.where(second, gate_ref[1:2, :], 0.0)
    hit = (rank[:, None, :] == slots.astype(F32)).reshape(experts * count, toks)
    weight = jnp.broadcast_to(gate[:, None, :], slots.shape).reshape(experts * count, toks)
    scale = jnp.sum(jnp.where(hit, weight, 0.0), axis=1, keepdims=True)
    mask = jnp.where(hit, 1.0, 0.0).astype(BF16)
    rows = jnp.dot(mask, act_ref[...], preferred_element_type=F32).astype(BF16)
    picked = jnp.dot(mask, grad_ref[...], preferred_element_type=F32)
    return rows, (picked * scale).astype(BF16)


def far_kernel(ids_ref, gate_ref, act_ref, grad_ref, out_ref):
    experts, count, toks = out_ref.shape[0] // 2, 2 * out_ref.shape[2], ids_ref.shape[1]
    slots = lax.broadcasted_iota(jnp.int32, (experts, count, toks), 1)
    rows, weighted = select(ids_ref, gate_ref, act_ref, grad_ref, slots)
    out_ref[:, 0] = rows.reshape(2 * experts, count // 2, -1)
    out_ref[:, 1] = weighted.reshape(2 * experts, count // 2, -1)


def near_kernel(half, tp_ref, ids_ref, gate_ref, act_ref, grad_ref, out_ref):
    experts, toks = out_ref.shape[1] // 2, ids_ref.shape[1]
    inner = lax.broadcasted_iota(jnp.int32, (experts, 8, toks), 1)
    slots = jnp.where(inner < 2, half + 2 * tp_ref[0] + inner, -2)
    rows, weighted = select(ids_ref, gate_ref, act_ref, grad_ref, slots)
    out_ref[0] = rows.reshape(experts, 8, -1)[:, :2].reshape(2 * experts, -1)
    out_ref[1] = weighted.reshape(experts, 8, -1)[:, :2].reshape(2 * experts, -1)


def send_far(ids_t, gate_t, acts, grads, experts, half):
    toks, width = acts.shape
    tile = width // 4
    return pl.pallas_call(
        far_kernel,
        grid=(width // tile,),
        in_specs=[
            pl.BlockSpec((2, toks), lambda i: (0, 0)),
            pl.BlockSpec((2, toks), lambda i: (0, 0)),
            pl.BlockSpec((toks, tile), lambda i: (0, i)),
            pl.BlockSpec((toks, tile), lambda i: (0, i)),
        ],
        out_specs=pl.BlockSpec((2 * experts, 2, half // 2, tile), lambda i: (0, 0, 0, i)),
        out_shape=jax.ShapeDtypeStruct((2 * experts, 2, half // 2, width), BF16),
        compiler_params=pltpu.CompilerParams(vmem_limit_bytes=LIMIT),
        cost_estimate=pl.CostEstimate(
            flops=16 * experts * half * toks * width,
            bytes_accessed=4 * (toks + experts * half) * width,
            transcendentals=0,
        ),
    )(ids_t, gate_t, acts, grads)


def send_near(tp_at, ids_t, gate_t, acts, grads, experts, half):
    toks, width = acts.shape
    tile = width // 2
    return pl.pallas_call(
        functools.partial(near_kernel, half),
        grid=(width // tile,),
        in_specs=[
            pl.BlockSpec(memory_space=pltpu.SMEM),
            pl.BlockSpec((2, toks), lambda i: (0, 0)),
            pl.BlockSpec((2, toks), lambda i: (0, 0)),
            pl.BlockSpec((toks, tile), lambda i: (0, i)),
            pl.BlockSpec((toks, tile), lambda i: (0, i)),
        ],
        out_specs=pl.BlockSpec((2, 2 * experts, tile), lambda i: (0, 0, i)),
        out_shape=jax.ShapeDtypeStruct((2, 2 * experts, width), BF16),
        compiler_params=pltpu.CompilerParams(vmem_limit_bytes=LIMIT),
    )(tp_at, ids_t, gate_t, acts, grads)


def expert_kernel(
    turn, src_ref, gate_ref, up_ref, down_ref, part_ref, side_ref, pre_acc, back_acc, dgu_ref, kept
):
    outer, _, inner, width = src_ref.shape
    rows = outer * inner
    units = down_ref.shape[0]
    contract = (((1,), (1,)), ((), ()))
    phase, at = pl.program_id(0), pl.program_id(1)

    @pl.when(phase == 0)
    def _():
        x = src_ref[:, 0].reshape(rows, width)
        g = src_ref[:, 1].reshape(rows, width)
        kept[at, :units] = gate_ref[...]
        kept[at, units:] = up_ref[...]
        pre = lax.dot_general(x, kept[at], contract, preferred_element_type=F32)
        back = lax.dot_general(g, down_ref[...], contract, preferred_element_type=F32)

        @pl.when(at == 0)
        def _():
            pre_acc[...] = pre
            back_acc[...] = back

        @pl.when(at > 0)
        def _():
            pre_acc[...] += pre
            back_acc[...] += back

    @pl.when((phase == 0) & (at == pl.num_programs(1) - 1))
    def _():
        pre_gate = pre_acc[:, :units]
        pre_up = pre_acc[:, units:]
        back = back_acc[...]
        sig = jax.nn.sigmoid(pre_gate)
        silu = pre_gate * sig
        hidden = (silu * pre_up).astype(BF16)
        d_gate = (back * pre_up * sig * (1.0 + pre_gate * (1.0 - sig))).astype(BF16)
        d_up = (back * silu).astype(BF16)
        side_ref[:units, :] = d_gate.T
        side_ref[units : 2 * units, :] = d_up.T
        side_ref[2 * units :, :] = hidden.T
        dgu_ref[:, :units] = d_gate
        dgu_ref[:, units:] = d_up
        if turn:
            to = lax.broadcasted_iota(jnp.int32, (rows, rows), 0)
            of = lax.broadcasted_iota(jnp.int32, (rows, rows), 1)
            moved = jnp.where(of == (to % outer) * inner + to // outer, 1.0, 0.0).astype(BF16)
            dgu_ref[...] = jnp.dot(moved, dgu_ref[...], preferred_element_type=F32).astype(BF16)

    @pl.when(phase == 1)
    def _():
        part = jnp.dot(dgu_ref[...], kept[at], preferred_element_type=F32)
        part_ref[...] = part.astype(BF16)


def expert_part(src, gate_w, up_w, down_w, turn):
    outer, _, inner, width = src.shape
    rows = outer * inner
    units = down_w.shape[0]
    steps = 2
    tile = width // steps
    last = steps - 1

    def first_phase(p, i):
        return jnp.where(p == 0, i, last)

    weight_spec = pl.BlockSpec((units, tile), lambda p, i: (0, first_phase(p, i)))
    return pl.pallas_call(
        functools.partial(expert_kernel, turn),
        grid=(2, steps),
        in_specs=[
            pl.BlockSpec((outer, 2, inner, tile), lambda p, i: (0, 0, 0, first_phase(p, i))),
            weight_spec,
            weight_spec,
            weight_spec,
        ],
        out_specs=[
            pl.BlockSpec((rows, tile), lambda p, i: (0, p * i)),
            pl.BlockSpec((3 * units, rows), lambda p, i: (0, 0)),
        ],
        out_shape=[
            jax.ShapeDtypeStruct((rows, width), BF16),
            jax.ShapeDtypeStruct((3 * units, rows), BF16),
        ],
        scratch_shapes=[
            VMEM((rows, 2 * units), F32),
            VMEM((rows, units), F32),
            VMEM((rows, 2 * units), BF16),
            VMEM((steps, 2 * units, tile), BF16),
        ],
        compiler_params=pltpu.CompilerParams(vmem_limit_bytes=LIMIT),
        cost_estimate=pl.CostEstimate(
            flops=40 * rows * width * units,
            bytes_accessed=2 * (3 * rows * width + 3 * units * width),
            transcendentals=rows * units,
        ),
    )(src, gate_w, up_w, down_w)


def merge_kernel(far_ref, far_more_ref, near_ref, near_more_ref, out_ref):
    wide = out_ref.shape[2] // 2
    far = (far_ref[...].astype(F32) + far_more_ref[...].astype(F32)).astype(BF16)
    near = (near_ref[...].astype(F32) + near_more_ref[...].astype(F32)).astype(BF16)
    for j in range(out_ref.shape[0]):
        at = slice(j * wide, (j + 1) * wide)
        out_ref[j] = jnp.concatenate([far[:, at], near[:, at]], axis=1)


def merge(far, far_more, near, near_more, pieces):
    rows, width = far.shape
    steps = pieces // 2
    spec = pl.BlockSpec((rows, width // steps), lambda i: (0, i))
    return pl.pallas_call(
        merge_kernel,
        grid=(steps,),
        in_specs=[spec] * 4,
        out_specs=pl.BlockSpec((2, rows, 2 * width // pieces), lambda i: (i, 0, 0)),
        out_shape=jax.ShapeDtypeStruct((pieces, rows, 2 * width // pieces), BF16),
        compiler_params=pltpu.CompilerParams(vmem_limit_bytes=LIMIT),
    )(far, far_more, near, near_more)


def weight_kernel(count, *refs):
    sources, sides = refs[:count], refs[count : 2 * count]
    gate_ref, up_ref, down_ref = refs[2 * count :]
    units = gate_ref.shape[0]
    tile = sources[0].shape[3]

    def stacked(kind):
        return jnp.concatenate([s[:, kind].reshape(-1, tile) for s in sources], axis=0)

    left = jnp.concatenate([s[: 2 * units] for s in sides], axis=1)
    pair = jnp.dot(left, stacked(0), preferred_element_type=F32)
    left = jnp.concatenate([s[2 * units :] for s in sides], axis=1)
    down = jnp.dot(left, stacked(1), preferred_element_type=F32)
    gate_ref[...] = pair[:units].astype(BF16)
    up_ref[...] = pair[units:].astype(BF16)
    down_ref[...] = down.astype(BF16)


def weight_grads(sources, sides):
    width = sources[0].shape[3]
    units = sides[0].shape[0] // 3
    rows = sum(side.shape[1] for side in sides)
    tile = width // 4
    return pl.pallas_call(
        functools.partial(weight_kernel, len(sources)),
        grid=(width // tile,),
        in_specs=[
            pl.BlockSpec(src.shape[:3] + (tile,), lambda i: (0, 0, 0, i)) for src in sources
        ]
        + [pl.BlockSpec(side.shape, lambda i: (0, 0)) for side in sides],
        out_specs=[pl.BlockSpec((units, tile), lambda i: (0, i))] * 3,
        out_shape=[jax.ShapeDtypeStruct((units, width), BF16)] * 3,
        compiler_params=pltpu.CompilerParams(vmem_limit_bytes=LIMIT),
        cost_estimate=pl.CostEstimate(
            flops=24 * rows * width * units,
            bytes_accessed=2 * (2 * rows * width + 3 * units * width),
            transcendentals=0,
        ),
    )(*sources, *sides)


def combine_kernel(half, ids_ref, back_ref, out_ref):
    experts, per_core = back_ref.shape[0] // 2, back_ref.shape[1]
    toks = ids_ref.shape[1]
    wide = out_ref.shape[1]
    _, _, rank = table(ids_ref[...], experts)
    row = lax.broadcasted_iota(jnp.int32, (experts, 2 * per_core, toks), 1)
    late = half + 2 * (row % per_core) + row // per_core
    rows = back_ref[...].reshape(2 * experts * per_core, 2 * wide)
    total = gather_slots(rank, row.astype(F32), rows)[:, :wide]
    total += gather_slots(rank, late.astype(F32), rows)[:, wide:]
    out_ref[...] = total.astype(BF16)


def gather_slots(rank, slots, rows):
    hit = jnp.where(rank[:, None, :] == slots, 1.0, 0.0).astype(BF16).reshape(rows.shape[0], -1)
    return lax.dot_general(hit, rows, (((0,), (0,)), ((), ())), preferred_element_type=F32)


def combine(ids_t, returned, half):
    toks = ids_t.shape[1]
    return pl.pallas_call(
        functools.partial(combine_kernel, half),
        in_specs=[pl.BlockSpec(memory_space=VMEM)] * 2,
        out_specs=pl.BlockSpec(memory_space=VMEM),
        out_shape=jax.ShapeDtypeStruct((toks, returned.shape[2] // 2), BF16),
        compiler_params=pltpu.CompilerParams(vmem_limit_bytes=LIMIT),
    )(ids_t, returned)


def per_device(activations, out_grad, expert_ids, gate_values, gate_proj, up_proj, down_proj):
    devices = lax.axis_size("exp")
    planes = lax.axis_size("tp")
    experts = devices // 2
    toks, width = activations.shape
    slots = 8 * toks // devices
    half = slots // 2
    tp_at = lax.axis_index("tp").astype(jnp.int32)[None]
    ids_t = expert_ids.T
    gate_t = gate_values.T
    swap = [(i, i ^ 1) for i in range(devices)]

    def trade(v):
        return lax.ppermute(v, "exp", swap)

    def spread(v):
        return lax.all_to_all(v, "exp", split_axis=0, concat_axis=0, tiled=True)

    near = send_near(tp_at, ids_t, gate_t, activations, out_grad, experts, half)
    near = spread(jnp.transpose(near, (1, 0, 2)))
    far = send_far(ids_t, gate_t, activations, out_grad, experts, half)
    near, far = lax.optimization_barrier((near, far))
    near = jnp.transpose(near, (1, 0, 2))
    near = lax.all_gather(near, "tp", axis=0, tiled=False)
    far = spread(far.reshape(devices, half, width)).reshape(far.shape)
    weights = (gate_proj[0], up_proj[0], down_proj[0])
    far_other = trade(far)
    near_other = trade(near)
    far_part, far_side = expert_part(far, *weights, False)
    far_other, far_part = lax.optimization_barrier((far_other, far_part))
    far_other_part, far_other_side = expert_part(far_other, *weights, False)
    far_sent = trade(far_other_part)
    near_other, far_other_part = lax.optimization_barrier((near_other, far_other_part))
    near_other_part, near_other_side = expert_part(near_other, *weights, True)
    near_sent = trade(near_other_part)
    near, near_other_part = lax.optimization_barrier((near, near_other_part))
    near_part, near_side = expert_part(near, *weights, True)
    both = merge(far_part, far_sent, near_part, near_sent, planes)
    mine = lax.psum_scatter(both, "tp", scatter_dimension=0, tiled=False)
    returned = spread(mine.reshape(devices, half // 2, -1))
    piece = combine(ids_t, returned, half)
    gathered = lax.all_gather(piece, "tp", axis=0, tiled=False)
    in_grad = jnp.transpose(gathered, (1, 0, 2)).reshape(toks, width)
    gate_g, up_g, down_g = weight_grads(
        [far, far_other, near, near_other],
        [far_side, far_other_side, near_side, near_other_side],
    )
    return (in_grad, gate_g[None], up_g[None], down_g[None])


def solution(mesh):
    return jax.shard_map(
        per_device,
        mesh=mesh,
        in_specs=(
            P("exp", None),
            P("exp", None),
            P("exp", None),
            P("exp", None),
            P("exp", "tp", None),
            P("exp", "tp", None),
            P("exp", "tp", None),
        ),
        out_specs=(
            P("exp", None),
            P("exp", "tp", None),
            P("exp", "tp", None),
            P("exp", "tp", None),
        ),
        check_vma=False,
    )
```

```python
import functools

import jax
import jax.numpy as jnp
from jax import lax
from jax.experimental import pallas as pl
from jax.experimental.pallas import tpu as pltpu
from jax.sharding import PartitionSpec as P

F32 = jnp.float32
BF16 = jnp.bfloat16
VMEM = pltpu.VMEM
LIMIT = 28 * 1024 * 1024
WHOLE = 60 * 1024 * 1024


def table(ids, experts):
    toks = ids.shape[1]
    expert = lax.broadcasted_iota(jnp.int32, (experts, toks), 0)
    first = ids[0:1, :] == expert
    second = ids[1:2, :] == expert
    named = jnp.where(first | second, 1.0, 0.0)
    earlier = lax.broadcasted_iota(jnp.int32, (toks, toks), 0)
    later = lax.broadcasted_iota(jnp.int32, (toks, toks), 1)
    before = jnp.where(earlier < later, 1.0, 0.0).astype(BF16)
    rank = jnp.dot(named.astype(BF16), before, preferred_element_type=F32)
    return first, second, jnp.where(named > 0.0, rank, -1.0)


def choose(ids, gate, slots):
    experts, count, toks = slots.shape
    first, second, rank = table(ids, experts)
    gate = jnp.where(first, gate[0:1, :], 0.0) + jnp.where(second, gate[1:2, :], 0.0)
    hit = (rank[:, None, :] == slots.astype(F32)).reshape(experts * count, toks)
    weight = jnp.broadcast_to(gate[:, None, :], slots.shape).reshape(experts * count, toks)
    scale = jnp.sum(jnp.where(hit, weight, 0.0), axis=1, keepdims=True)
    return jnp.where(hit, 1.0, 0.0), scale


def far_kernel(ids_ref, gate_ref, act_ref, grad_ref, out_ref):
    experts, count, toks = out_ref.shape[0] // 2, 2 * out_ref.shape[2], ids_ref.shape[1]
    slots = lax.broadcasted_iota(jnp.int32, (experts, count, toks), 1)
    mask, scale = choose(ids_ref[...], gate_ref[...], slots)
    mask = mask.astype(BF16)
    rows = jnp.dot(mask, act_ref[...], preferred_element_type=F32).astype(BF16)
    picked = jnp.dot(mask, grad_ref[...], preferred_element_type=F32)
    out_ref[:, 0] = rows.reshape(2 * experts, count // 2, -1)
    out_ref[:, 1] = (picked * scale).astype(BF16).reshape(2 * experts, count // 2, -1)


def near_kernel(
    half, tp_ref, ids_hbm, gate_hbm, act_hbm, grad_hbm, out_ref, ids_ref, gate_ref, act_ref, grad_ref, sems
):
    pairs = ((ids_hbm, ids_ref), (gate_hbm, gate_ref), (act_hbm, act_ref), (grad_hbm, grad_ref))
    copies = [pltpu.make_async_copy(a, b, sems.at[i]) for i, (a, b) in enumerate(pairs)]
    for copy in copies:
        copy.start()
    experts, toks = out_ref.shape[0], ids_ref.shape[1]
    inner = lax.broadcasted_iota(jnp.int32, (experts, 8, toks), 1)
    slots = jnp.where(inner < 4, half + 2 * tp_ref[0] + inner // 2, -2)
    copies[0].wait()
    copies[1].wait()
    mask, scale = choose(ids_ref[...], gate_ref[...], slots)
    kind = (inner % 2).reshape(mask.shape)
    of_rows = jnp.where(kind == 0, mask, 0.0).astype(BF16)
    of_grads = jnp.where(kind == 1, mask, 0.0).astype(BF16)
    copies[2].wait()
    copies[3].wait()
    rows = jnp.dot(of_rows, act_ref[...], preferred_element_type=F32)
    picked = jnp.dot(of_grads, grad_ref[...], preferred_element_type=F32)
    both = (rows + picked * scale).reshape(experts, 8, -1)
    out_ref[:, 0] = both[:, 0:2].astype(BF16)
    out_ref[:, 1] = both[:, 2:4].astype(BF16)


def send_far(ids_t, gate_t, acts, grads, experts, half):
    toks, width = acts.shape
    tile = width // 4
    return pl.pallas_call(
        far_kernel,
        grid=(width // tile,),
        in_specs=[
            pl.BlockSpec((2, toks), lambda i: (0, 0)),
            pl.BlockSpec((2, toks), lambda i: (0, 0)),
            pl.BlockSpec((toks, tile), lambda i: (0, i)),
            pl.BlockSpec((toks, tile), lambda i: (0, i)),
        ],
        out_specs=pl.BlockSpec((2 * experts, 2, half // 2, tile), lambda i: (0, 0, 0, i)),
        out_shape=jax.ShapeDtypeStruct((2 * experts, 2, half // 2, width), BF16),
        compiler_params=pltpu.CompilerParams(vmem_limit_bytes=WHOLE),
        cost_estimate=pl.CostEstimate(
            flops=16 * experts * half * toks * width,
            bytes_accessed=4 * (toks + experts * half) * width,
            transcendentals=0,
        ),
    )(ids_t, gate_t, acts, grads)


def send_near(tp_at, ids_t, gate_t, acts, grads, experts, half):
    toks, width = acts.shape
    return pl.pallas_call(
        functools.partial(near_kernel, half),
        in_specs=[pl.BlockSpec(memory_space=pltpu.SMEM)]
        + [pl.BlockSpec(memory_space=pltpu.HBM)] * 4,
        out_specs=pl.BlockSpec(memory_space=VMEM),
        out_shape=jax.ShapeDtypeStruct((experts, 2, 2, width), BF16),
        scratch_shapes=[
            VMEM((2, toks), ids_t.dtype),
            VMEM((2, toks), gate_t.dtype),
            VMEM((toks, width), acts.dtype),
            VMEM((toks, width), grads.dtype),
            pltpu.SemaphoreType.DMA((4,)),
        ],
        compiler_params=pltpu.CompilerParams(vmem_limit_bytes=WHOLE),
    )(tp_at, ids_t, gate_t, acts, grads)


def expert_kernel(
    turn, src_ref, gate_ref, up_ref, down_ref, part_ref, side_ref, pre_acc, back_acc, dgu_ref, kept
):
    outer, _, inner, width = src_ref.shape
    rows = outer * inner
    units = down_ref.shape[0]
    contract = (((1,), (1,)), ((), ()))
    phase, at = pl.program_id(0), pl.program_id(1)

    @pl.when(phase == 0)
    def _():
        x = src_ref[:, 0].reshape(rows, width)
        g = src_ref[:, 1].reshape(rows, width)
        kept[at, :units] = gate_ref[...]
        kept[at, units:] = up_ref[...]
        pre = lax.dot_general(x, kept[at], contract, preferred_element_type=F32)
        back = lax.dot_general(g, down_ref[...], contract, preferred_element_type=F32)

        @pl.when(at == 0)
        def _():
            pre_acc[...] = pre
            back_acc[...] = back

        @pl.when(at > 0)
        def _():
            pre_acc[...] += pre
            back_acc[...] += back

    @pl.when((phase == 0) & (at == pl.num_programs(1) - 1))
    def _():
        pre_gate = pre_acc[:, :units]
        pre_up = pre_acc[:, units:]
        back = back_acc[...]
        sig = jax.nn.sigmoid(pre_gate)
        silu = pre_gate * sig
        hidden = (silu * pre_up).astype(BF16)
        d_gate = (back * pre_up * sig * (1.0 + pre_gate * (1.0 - sig))).astype(BF16)
        d_up = (back * silu).astype(BF16)
        side_ref[:units, :] = d_gate.T
        side_ref[units : 2 * units, :] = d_up.T
        side_ref[2 * units :, :] = hidden.T
        dgu_ref[:, :units] = d_gate
        dgu_ref[:, units:] = d_up
        if turn:
            to = lax.broadcasted_iota(jnp.int32, (rows, rows), 0)
            of = lax.broadcasted_iota(jnp.int32, (rows, rows), 1)
            moved = jnp.where(of == (to % outer) * inner + to // outer, 1.0, 0.0).astype(BF16)
            dgu_ref[...] = jnp.dot(moved, dgu_ref[...], preferred_element_type=F32).astype(BF16)

    @pl.when(phase == 1)
    def _():
        part = jnp.dot(dgu_ref[...], kept[at], preferred_element_type=F32)
        part_ref[...] = part.astype(BF16)


def expert_part(src, gate_w, up_w, down_w, turn):
    outer, _, inner, width = src.shape
    rows = outer * inner
    units = down_w.shape[0]
    steps = 1
    tile = width // steps
    last = steps - 1

    def first_phase(p, i):
        return jnp.where(p == 0, i, last)

    weight_spec = pl.BlockSpec((units, tile), lambda p, i: (0, first_phase(p, i)))
    return pl.pallas_call(
        functools.partial(expert_kernel, turn),
        grid=(2, steps),
        in_specs=[
            pl.BlockSpec((outer, 2, inner, tile), lambda p, i: (0, 0, 0, first_phase(p, i))),
            weight_spec,
            weight_spec,
            weight_spec,
        ],
        out_specs=[
            pl.BlockSpec((rows, tile), lambda p, i: (0, p * i)),
            pl.BlockSpec((3 * units, rows), lambda p, i: (0, 0)),
        ],
        out_shape=[
            jax.ShapeDtypeStruct((rows, width), BF16),
            jax.ShapeDtypeStruct((3 * units, rows), BF16),
        ],
        scratch_shapes=[
            VMEM((rows, 2 * units), F32),
            VMEM((rows, units), F32),
            VMEM((rows, 2 * units), BF16),
            VMEM((steps, 2 * units, tile), BF16),
        ],
        compiler_params=pltpu.CompilerParams(vmem_limit_bytes=LIMIT),
        cost_estimate=pl.CostEstimate(
            flops=40 * rows * width * units,
            bytes_accessed=2 * (3 * rows * width + 3 * units * width),
            transcendentals=rows * units,
        ),
    )(src, gate_w, up_w, down_w)


def merge_kernel(far_ref, far_more_ref, near_ref, near_more_ref, out_ref):
    wide = out_ref.shape[2] // 2
    far = (far_ref[...].astype(F32) + far_more_ref[...].astype(F32)).astype(BF16)
    near = (near_ref[...].astype(F32) + near_more_ref[...].astype(F32)).astype(BF16)
    for j in range(out_ref.shape[0]):
        at = slice(j * wide, (j + 1) * wide)
        out_ref[j] = jnp.concatenate([far[:, at], near[:, at]], axis=1)


def merge(far, far_more, near, near_more, pieces):
    rows, width = far.shape
    steps = pieces // 2
    spec = pl.BlockSpec((rows, width // steps), lambda i: (0, i))
    return pl.pallas_call(
        merge_kernel,
        grid=(steps,),
        in_specs=[spec] * 4,
        out_specs=pl.BlockSpec((2, rows, 2 * width // pieces), lambda i: (i, 0, 0)),
        out_shape=pltpu.HBM((pieces, rows, 2 * width // pieces), BF16),
        compiler_params=pltpu.CompilerParams(vmem_limit_bytes=LIMIT),
    )(far, far_more, near, near_more)


def weight_kernel(count, *refs):
    sources, sides = refs[:count], refs[count : 2 * count]
    gate_ref, up_ref, down_ref = refs[2 * count :]
    units = gate_ref.shape[0]
    tile = sources[0].shape[3]

    def stacked(kind):
        return jnp.concatenate([s[:, kind].reshape(-1, tile) for s in sources], axis=0)

    left = jnp.concatenate([s[: 2 * units] for s in sides], axis=1)
    pair = jnp.dot(left, stacked(0), preferred_element_type=F32)
    left = jnp.concatenate([s[2 * units :] for s in sides], axis=1)
    down = jnp.dot(left, stacked(1), preferred_element_type=F32)
    gate_ref[...] = pair[:units].astype(BF16)
    up_ref[...] = pair[units:].astype(BF16)
    down_ref[...] = down.astype(BF16)


def weight_grads(sources, sides):
    width = sources[0].shape[3]
    units = sides[0].shape[0] // 3
    rows = sum(side.shape[1] for side in sides)
    tile = width // 4
    return pl.pallas_call(
        functools.partial(weight_kernel, len(sources)),
        grid=(width // tile,),
        in_specs=[
            pl.BlockSpec(src.shape[:3] + (tile,), lambda i: (0, 0, 0, i)) for src in sources
        ]
        + [pl.BlockSpec(side.shape, lambda i: (0, 0)) for side in sides],
        out_specs=[pl.BlockSpec((units, tile), lambda i: (0, i))] * 3,
        out_shape=[jax.ShapeDtypeStruct((units, width), BF16)] * 3,
        compiler_params=pltpu.CompilerParams(vmem_limit_bytes=LIMIT),
        cost_estimate=pl.CostEstimate(
            flops=24 * rows * width * units,
            bytes_accessed=2 * (2 * rows * width + 3 * units * width),
            transcendentals=0,
        ),
    )(*sources, *sides)


def combine_kernel(half, ids_ref, back_ref, out_ref):
    experts, per_core = back_ref.shape[0] // 2, back_ref.shape[1]
    toks = ids_ref.shape[1]
    wide = out_ref.shape[1]
    _, _, rank = table(ids_ref[...], experts)
    row = lax.broadcasted_iota(jnp.int32, (experts, 2 * per_core, toks), 1)
    late = half + 2 * (row % per_core) + row // per_core
    rows = back_ref[...].reshape(2 * experts * per_core, 2 * wide)
    total = gather_slots(rank, row.astype(F32), rows)[:, :wide]
    total += gather_slots(rank, late.astype(F32), rows)[:, wide:]
    out_ref[...] = total.astype(BF16)


def gather_slots(rank, slots, rows):
    hit = jnp.where(rank[:, None, :] == slots, 1.0, 0.0).astype(BF16).reshape(rows.shape[0], -1)
    return lax.dot_general(hit, rows, (((0,), (0,)), ((), ())), preferred_element_type=F32)


def combine(ids_t, returned, half):
    toks = ids_t.shape[1]
    return pl.pallas_call(
        functools.partial(combine_kernel, half),
        in_specs=[pl.BlockSpec(memory_space=VMEM)] * 2,
        out_specs=pl.BlockSpec(memory_space=VMEM),
        out_shape=jax.ShapeDtypeStruct((toks, returned.shape[2] // 2), BF16),
        compiler_params=pltpu.CompilerParams(vmem_limit_bytes=LIMIT),
    )(ids_t, returned)


def per_device(activations, out_grad, expert_ids, gate_values, gate_proj, up_proj, down_proj):
    devices = lax.axis_size("exp")
    planes = lax.axis_size("tp")
    experts = devices // 2
    toks, width = activations.shape
    slots = 8 * toks // devices
    half = slots // 2
    tp_at = lax.axis_index("tp").astype(jnp.int32)[None]
    ids_t = expert_ids.T
    gate_t = gate_values.T
    swap = [(i, i ^ 1) for i in range(devices)]

    def trade(v):
        return lax.ppermute(v, "exp", swap)

    def spread(v):
        return lax.all_to_all(v, "exp", split_axis=0, concat_axis=0, tiled=True)

    near = send_near(tp_at, ids_t, gate_t, activations, out_grad, experts, half)
    near = spread(near.reshape(devices, 2, width))
    far = send_far(ids_t, gate_t, activations, out_grad, experts, half)
    near, far = lax.optimization_barrier((near, far))
    near = jnp.transpose(near, (1, 0, 2))
    near = lax.all_gather(near, "tp", axis=0, tiled=False)
    far = spread(far.reshape(devices, half, width)).reshape(far.shape)
    weights = (gate_proj[0], up_proj[0], down_proj[0])
    far_other = trade(far)
    near_other = trade(near)
    far_part, far_side = expert_part(far, *weights, False)
    far_other, far_part = lax.optimization_barrier((far_other, far_part))
    far_other_part, far_other_side = expert_part(far_other, *weights, False)
    far_sent = trade(far_other_part)
    near_other, far_other_part = lax.optimization_barrier((near_other, far_other_part))
    near_other_part, near_other_side = expert_part(near_other, *weights, True)
    near_sent = trade(near_other_part)
    near, near_other_part = lax.optimization_barrier((near, near_other_part))
    near_part, near_side = expert_part(near, *weights, True)
    both = merge(far_part, far_sent, near_part, near_sent, planes)
    both, far = lax.optimization_barrier((both, far))
    gate_g, up_g, down_g = weight_grads(
        [far, far_other, near, near_other],
        [far_side, far_other_side, near_side, near_other_side],
    )
    mine = lax.psum_scatter(both, "tp", scatter_dimension=0, tiled=False)
    mine, gate_g, up_g, down_g = lax.optimization_barrier((mine, gate_g, up_g, down_g))
    returned = spread(mine.reshape(devices, half // 2, -1))
    piece = combine(ids_t, returned, half)
    gathered = lax.all_gather(piece, "tp", axis=0, tiled=False)
    in_grad = jnp.transpose(gathered, (1, 0, 2)).reshape(toks, width)
    return (in_grad, gate_g[None], up_g[None], down_g[None])


def solution(mesh):
    return jax.shard_map(
        per_device,
        mesh=mesh,
        in_specs=(
            P("exp", None),
            P("exp", None),
            P("exp", None),
            P("exp", None),
            P("exp", "tp", None),
            P("exp", "tp", None),
            P("exp", "tp", None),
        ),
        out_specs=(
            P("exp", None),
            P("exp", "tp", None),
            P("exp", "tp", None),
            P("exp", "tp", None),
        ),
        check_vma=False,
    )
```

```python
import functools

import jax
import jax.numpy as jnp
from jax import lax
from jax.experimental import pallas as pl
from jax.experimental.pallas import tpu as pltpu
from jax.sharding import PartitionSpec as P

F32 = jnp.float32
BF16 = jnp.bfloat16
VMEM = pltpu.VMEM
LIMIT = 28 * 1024 * 1024
WHOLE = 60 * 1024 * 1024


def table(ids, experts):
    toks = ids.shape[1]
    expert = lax.broadcasted_iota(jnp.int32, (experts, toks), 0)
    first = ids[0:1, :] == expert
    second = ids[1:2, :] == expert
    named = jnp.where(first | second, 1.0, 0.0)
    earlier = lax.broadcasted_iota(jnp.int32, (toks, toks), 0)
    later = lax.broadcasted_iota(jnp.int32, (toks, toks), 1)
    before = jnp.where(earlier < later, 1.0, 0.0).astype(BF16)
    rank = jnp.dot(named.astype(BF16), before, preferred_element_type=F32)
    return first, second, jnp.where(named > 0.0, rank, -1.0)


def choose(ids, gate, slots):
    experts, count, toks = slots.shape
    first, second, rank = table(ids, experts)
    gate = jnp.where(first, gate[0:1, :], 0.0) + jnp.where(second, gate[1:2, :], 0.0)
    hit = (rank[:, None, :] == slots.astype(F32)).reshape(experts * count, toks)
    weight = jnp.broadcast_to(gate[:, None, :], slots.shape).reshape(experts * count, toks)
    scale = jnp.sum(jnp.where(hit, weight, 0.0), axis=1, keepdims=True)
    return jnp.where(hit, 1.0, 0.0), scale


def far_kernel(ids_ref, gate_ref, act_ref, grad_ref, out_ref):
    experts, _, count, tile = out_ref.shape
    toks = ids_ref.shape[1]
    slots = lax.broadcasted_iota(jnp.int32, (experts, count, toks), 1)
    mask, scale = choose(ids_ref[...], gate_ref[...], slots)
    mask = mask.astype(BF16)
    rows = jnp.dot(mask, act_ref[...], preferred_element_type=F32).astype(BF16)
    picked = jnp.dot(mask, grad_ref[...], preferred_element_type=F32)
    out_ref[:, 0] = rows.reshape(experts, count, tile)
    out_ref[:, 1] = (picked * scale).astype(BF16).reshape(experts, count, tile)


def near_kernel(
    half, tp_ref, ids_hbm, gate_hbm, act_hbm, grad_hbm, out_ref, ids_ref, gate_ref, act_ref, grad_ref, sems
):
    pairs = ((ids_hbm, ids_ref), (gate_hbm, gate_ref), (act_hbm, act_ref), (grad_hbm, grad_ref))
    copies = [pltpu.make_async_copy(a, b, sems.at[i]) for i, (a, b) in enumerate(pairs)]
    for copy in copies:
        copy.start()
    experts, toks = out_ref.shape[0], ids_ref.shape[1]
    inner = lax.broadcasted_iota(jnp.int32, (experts, 8, toks), 1)
    slots = jnp.where(inner < 4, half + 2 * tp_ref[0] + inner % 2, -2)
    copies[0].wait()
    copies[1].wait()
    mask, scale = choose(ids_ref[...], gate_ref[...], slots)
    kind = (inner // 2).reshape(mask.shape)
    of_rows = jnp.where(kind == 0, mask, 0.0).astype(BF16)
    of_grads = jnp.where(kind == 1, mask, 0.0).astype(BF16)
    copies[2].wait()
    copies[3].wait()
    rows = jnp.dot(of_rows, act_ref[...], preferred_element_type=F32)
    picked = jnp.dot(of_grads, grad_ref[...], preferred_element_type=F32)
    both = (rows + picked * scale).reshape(experts, 8, -1)
    out_ref[...] = both[:, :4].astype(BF16)


def send_far(ids_t, gate_t, acts, grads, experts, half):
    toks, width = acts.shape
    tile = width // 4
    return pl.pallas_call(
        far_kernel,
        grid=(width // tile,),
        in_specs=[
            pl.BlockSpec((2, toks), lambda i: (0, 0)),
            pl.BlockSpec((2, toks), lambda i: (0, 0)),
            pl.BlockSpec((toks, tile), lambda i: (0, i)),
            pl.BlockSpec((toks, tile), lambda i: (0, i)),
        ],
        out_specs=pl.BlockSpec((experts, 2, half, tile), lambda i: (0, 0, 0, i)),
        out_shape=jax.ShapeDtypeStruct((experts, 2, half, width), BF16),
        compiler_params=pltpu.CompilerParams(vmem_limit_bytes=WHOLE),
        cost_estimate=pl.CostEstimate(
            flops=16 * experts * half * toks * width,
            bytes_accessed=4 * (toks + experts * half) * width,
            transcendentals=0,
        ),
    )(ids_t, gate_t, acts, grads)


def send_near(tp_at, ids_t, gate_t, acts, grads, experts, half):
    toks, width = acts.shape
    return pl.pallas_call(
        functools.partial(near_kernel, half),
        in_specs=[pl.BlockSpec(memory_space=pltpu.SMEM)]
        + [pl.BlockSpec(memory_space=pltpu.HBM)] * 4,
        out_specs=pl.BlockSpec(memory_space=VMEM),
        out_shape=jax.ShapeDtypeStruct((experts, 4, width), BF16),
        scratch_shapes=[
            VMEM((2, toks), ids_t.dtype),
            VMEM((2, toks), gate_t.dtype),
            VMEM((toks, width), acts.dtype),
            VMEM((toks, width), grads.dtype),
            pltpu.SemaphoreType.DMA((4,)),
        ],
        compiler_params=pltpu.CompilerParams(vmem_limit_bytes=WHOLE),
    )(tp_at, ids_t, gate_t, acts, grads)


def sort_kernel(in_ref, out_ref):
    every = in_ref[...].astype(F32)
    for kind in range(2):
        some = every[:, 2 * kind : 2 * kind + 2].reshape(out_ref.shape[1], -1)
        out_ref[kind] = some.astype(BF16)


def sort_kinds(near):
    chips, _, width = near.shape
    tile = width // 2
    return pl.pallas_call(
        sort_kernel,
        grid=(width // tile,),
        in_specs=[pl.BlockSpec((chips, 4, tile), lambda i: (0, 0, i))],
        out_specs=pl.BlockSpec((2, 2 * chips, tile), lambda i: (0, 0, i)),
        out_shape=pltpu.HBM((2, 2 * chips, width), BF16),
        compiler_params=pltpu.CompilerParams(vmem_limit_bytes=LIMIT),
    )(near)


def expert_kernel(
    turn, src_ref, gate_ref, up_ref, down_ref, part_ref, side_ref, pre_acc, back_acc, dgu_ref, kept
):
    outer, _, inner, width = src_ref.shape
    rows = outer * inner
    units = down_ref.shape[0]
    contract = (((1,), (1,)), ((), ()))
    phase, at = pl.program_id(0), pl.program_id(1)

    @pl.when(phase == 0)
    def _():
        x = src_ref[:, 0].reshape(rows, width)
        g = src_ref[:, 1].reshape(rows, width)
        kept[at, :units] = gate_ref[...]
        kept[at, units:] = up_ref[...]
        pre = lax.dot_general(x, kept[at], contract, preferred_element_type=F32)
        back = lax.dot_general(g, down_ref[...], contract, preferred_element_type=F32)

        @pl.when(at == 0)
        def _():
            pre_acc[...] = pre
            back_acc[...] = back

        @pl.when(at > 0)
        def _():
            pre_acc[...] += pre
            back_acc[...] += back

    @pl.when((phase == 0) & (at == pl.num_programs(1) - 1))
    def _():
        pre_gate = pre_acc[:, :units]
        pre_up = pre_acc[:, units:]
        back = back_acc[...]
        sig = jax.nn.sigmoid(pre_gate)
        silu = pre_gate * sig
        hidden = (silu * pre_up).astype(BF16)
        d_gate = (back * pre_up * sig * (1.0 + pre_gate * (1.0 - sig))).astype(BF16)
        d_up = (back * silu).astype(BF16)
        side_ref[:units, :] = d_gate.T
        side_ref[units : 2 * units, :] = d_up.T
        side_ref[2 * units :, :] = hidden.T
        dgu_ref[:, :units] = d_gate
        dgu_ref[:, units:] = d_up
        if turn:
            to = lax.broadcasted_iota(jnp.int32, (rows, rows), 0)
            of = lax.broadcasted_iota(jnp.int32, (rows, rows), 1)
            chip, place = to // (2 * outer), to % (2 * outer)
            moved = of == (place // 2) * inner + 2 * chip + place % 2
            moved = jnp.where(moved, 1.0, 0.0).astype(BF16)
            dgu_ref[...] = jnp.dot(moved, dgu_ref[...], preferred_element_type=F32).astype(BF16)

    @pl.when(phase == 1)
    def _():
        part = jnp.dot(dgu_ref[...], kept[at], preferred_element_type=F32)
        part_ref[...] = part.astype(BF16)


def expert_part(src, gate_w, up_w, down_w, turn):
    outer, _, inner, width = src.shape
    rows = outer * inner
    units = down_w.shape[0]
    steps = 1
    tile = width // steps
    last = steps - 1

    def first_phase(p, i):
        return jnp.where(p == 0, i, last)

    weight_spec = pl.BlockSpec((units, tile), lambda p, i: (0, first_phase(p, i)))
    return pl.pallas_call(
        functools.partial(expert_kernel, turn),
        grid=(2, steps),
        in_specs=[
            pl.BlockSpec((outer, 2, inner, tile), lambda p, i: (0, 0, 0, first_phase(p, i))),
            weight_spec,
            weight_spec,
            weight_spec,
        ],
        out_specs=[
            pl.BlockSpec((rows, tile), lambda p, i: (0, p * i)),
            pl.BlockSpec((3 * units, rows), lambda p, i: (0, 0)),
        ],
        out_shape=[
            jax.ShapeDtypeStruct((rows, width), BF16),
            jax.ShapeDtypeStruct((3 * units, rows), BF16),
        ],
        scratch_shapes=[
            VMEM((rows, 2 * units), F32),
            VMEM((rows, units), F32),
            VMEM((rows, 2 * units), BF16),
            VMEM((steps, 2 * units, tile), BF16),
        ],
        compiler_params=pltpu.CompilerParams(vmem_limit_bytes=LIMIT),
        cost_estimate=pl.CostEstimate(
            flops=40 * rows * width * units,
            bytes_accessed=2 * (3 * rows * width + 3 * units * width),
            transcendentals=rows * units,
        ),
    )(src, gate_w, up_w, down_w)


def merge_kernel(far_ref, far_more_ref, near_ref, near_more_ref, out_ref):
    wide = out_ref.shape[2] // 2
    far = (far_ref[...].astype(F32) + far_more_ref[...].astype(F32)).astype(BF16)
    near = (near_ref[...].astype(F32) + near_more_ref[...].astype(F32)).astype(BF16)
    for j in range(out_ref.shape[0]):
        at = slice(j * wide, (j + 1) * wide)
        out_ref[j] = jnp.concatenate([far[:, at], near[:, at]], axis=1)


def merge(far, far_more, near, near_more, pieces):
    rows, width = far.shape
    steps = pieces // 2
    spec = pl.BlockSpec((rows, width // steps), lambda i: (0, i))
    return pl.pallas_call(
        merge_kernel,
        grid=(steps,),
        in_specs=[spec] * 4,
        out_specs=pl.BlockSpec((2, rows, 2 * width // pieces), lambda i: (i, 0, 0)),
        out_shape=pltpu.HBM((pieces, rows, 2 * width // pieces), BF16),
        compiler_params=pltpu.CompilerParams(vmem_limit_bytes=LIMIT),
    )(far, far_more, near, near_more)


def weight_kernel(count, *refs):
    sources, sides = refs[:count], refs[count : 2 * count]
    gate_ref, up_ref, down_ref = refs[2 * count :]
    units = gate_ref.shape[0]
    tile = sources[0].shape[3]

    def stacked(kind):
        return jnp.concatenate([s[:, kind].reshape(-1, tile) for s in sources], axis=0)

    left = jnp.concatenate([s[: 2 * units] for s in sides], axis=1)
    pair = jnp.dot(left, stacked(0), preferred_element_type=F32)
    left = jnp.concatenate([s[2 * units :] for s in sides], axis=1)
    down = jnp.dot(left, stacked(1), preferred_element_type=F32)
    gate_ref[...] = pair[:units].astype(BF16)
    up_ref[...] = pair[units:].astype(BF16)
    down_ref[...] = down.astype(BF16)


def weight_grads(sources, sides):
    width = sources[0].shape[3]
    units = sides[0].shape[0] // 3
    rows = sum(side.shape[1] for side in sides)
    tile = width // 4
    return pl.pallas_call(
        functools.partial(weight_kernel, len(sources)),
        grid=(width // tile,),
        in_specs=[
            pl.BlockSpec(src.shape[:3] + (tile,), lambda i: (0, 0, 0, i)) for src in sources
        ]
        + [pl.BlockSpec(side.shape, lambda i: (0, 0)) for side in sides],
        out_specs=[pl.BlockSpec((units, tile), lambda i: (0, i))] * 3,
        out_shape=[jax.ShapeDtypeStruct((units, width), BF16)] * 3,
        compiler_params=pltpu.CompilerParams(vmem_limit_bytes=LIMIT),
        cost_estimate=pl.CostEstimate(
            flops=24 * rows * width * units,
            bytes_accessed=2 * (2 * rows * width + 3 * units * width),
            transcendentals=0,
        ),
    )(*sources, *sides)


def combine_kernel(ids_ref, back_ref, out_ref):
    experts, half = back_ref.shape[0], back_ref.shape[1]
    toks = ids_ref.shape[1]
    wide = out_ref.shape[1]
    _, _, rank = table(ids_ref[...], experts)
    slots = lax.broadcasted_iota(jnp.int32, (experts, half, toks), 1)
    rows = back_ref[...].reshape(experts * half, 2 * wide)
    total = gather_slots(rank, slots.astype(F32), rows)[:, :wide]
    total += gather_slots(rank, (slots + half).astype(F32), rows)[:, wide:]
    out_ref[...] = total.astype(BF16)


def gather_slots(rank, slots, rows):
    hit = jnp.where(rank[:, None, :] == slots, 1.0, 0.0).astype(BF16).reshape(rows.shape[0], -1)
    return lax.dot_general(hit, rows, (((0,), (0,)), ((), ())), preferred_element_type=F32)


def combine(ids_t, returned):
    toks = ids_t.shape[1]
    return pl.pallas_call(
        combine_kernel,
        in_specs=[pl.BlockSpec(memory_space=VMEM)] * 2,
        out_specs=pl.BlockSpec(memory_space=VMEM),
        out_shape=jax.ShapeDtypeStruct((toks, returned.shape[2] // 2), BF16),
        compiler_params=pltpu.CompilerParams(vmem_limit_bytes=LIMIT),
    )(ids_t, returned)


def per_device(activations, out_grad, expert_ids, gate_values, gate_proj, up_proj, down_proj):
    devices = lax.axis_size("exp")
    planes = lax.axis_size("tp")
    experts = devices // 2
    toks, width = activations.shape
    slots = 8 * toks // devices
    half = slots // 2
    tp_at = lax.axis_index("tp").astype(jnp.int32)[None]
    ids_t = expert_ids.T
    gate_t = gate_values.T
    swap = [(i, i ^ 1) for i in range(devices)]

    def trade(v):
        return lax.ppermute(v, "exp", swap)

    sides = [list(range(core, devices, 2)) for core in range(2)]

    def spread(v):
        return lax.all_to_all(
            v, "exp", split_axis=0, concat_axis=0, tiled=True, axis_index_groups=sides
        )

    near = send_near(tp_at, ids_t, gate_t, activations, out_grad, experts, half)
    near = spread(near)
    far = send_far(ids_t, gate_t, activations, out_grad, experts, half)
    near, far = lax.optimization_barrier((near, far))
    near = sort_kinds(near)
    near = lax.all_gather(near, "tp", axis=0, tiled=False)
    far = spread(far.reshape(experts, 2 * half, width)).reshape(far.shape)
    weights = (gate_proj[0], up_proj[0], down_proj[0])
    far_other = trade(far)
    near_other = trade(near)
    far_part, far_side = expert_part(far, *weights, False)
    near, far_part = lax.optimization_barrier((near, far_part))
    near_part, near_side = expert_part(near, *weights, True)
    far_other, near_part = lax.optimization_barrier((far_other, near_part))
    far_other_part, far_other_side = expert_part(far_other, *weights, False)
    far_sent = trade(far_other_part)
    near_other, far_other_part = lax.optimization_barrier((near_other, far_other_part))
    near_other_part, near_other_side = expert_part(near_other, *weights, True)
    near_sent = trade(near_other_part)
    both = merge(far_part, far_sent, near_part, near_sent, planes)
    both, far = lax.optimization_barrier((both, far))
    gate_g, up_g, down_g = weight_grads(
        [far, far_other, near, near_other],
        [far_side, far_other_side, near_side, near_other_side],
    )
    mine = lax.psum_scatter(both, "tp", scatter_dimension=0, tiled=False)
    mine, gate_g, up_g, down_g = lax.optimization_barrier((mine, gate_g, up_g, down_g))
    returned = spread(mine.reshape(experts, half, -1))
    piece = combine(ids_t, returned)
    gathered = lax.all_gather(piece, "tp", axis=0, tiled=False)
    in_grad = jnp.transpose(gathered, (1, 0, 2)).reshape(toks, width)
    return (in_grad, gate_g[None], up_g[None], down_g[None])


def solution(mesh):
    return jax.shard_map(
        per_device,
        mesh=mesh,
        in_specs=(
            P("exp", None),
            P("exp", None),
            P("exp", None),
            P("exp", None),
            P("exp", "tp", None),
            P("exp", "tp", None),
            P("exp", "tp", None),
        ),
        out_specs=(
            P("exp", None),
            P("exp", "tp", None),
            P("exp", "tp", None),
            P("exp", "tp", None),
        ),
        check_vma=False,
    )
```

```python
import functools

import jax
import jax.numpy as jnp
from jax import lax
from jax.experimental import pallas as pl
from jax.experimental.pallas import tpu as pltpu
from jax.sharding import PartitionSpec as P

F32 = jnp.float32
BF16 = jnp.bfloat16
VMEM = pltpu.VMEM
LIMIT = 28 * 1024 * 1024
WHOLE = 60 * 1024 * 1024
PASS = 62 * 1024 * 1024


def table(ids, experts):
    toks = ids.shape[1]
    expert = lax.broadcasted_iota(jnp.int32, (experts, toks), 0)
    first = ids[0:1, :] == expert
    second = ids[1:2, :] == expert
    named = jnp.where(first | second, 1.0, 0.0)
    earlier = lax.broadcasted_iota(jnp.int32, (toks, toks), 0)
    later = lax.broadcasted_iota(jnp.int32, (toks, toks), 1)
    before = jnp.where(earlier < later, 1.0, 0.0).astype(BF16)
    rank = jnp.dot(named.astype(BF16), before, preferred_element_type=F32)
    return first, second, jnp.where(named > 0.0, rank, -1.0)


def choose(ids, gate, slots):
    experts, count, toks = slots.shape
    first, second, rank = table(ids, experts)
    gate = jnp.where(first, gate[0:1, :], 0.0) + jnp.where(second, gate[1:2, :], 0.0)
    hit = (rank[:, None, :] == slots.astype(F32)).reshape(experts * count, toks)
    weight = jnp.broadcast_to(gate[:, None, :], slots.shape).reshape(experts * count, toks)
    scale = jnp.sum(jnp.where(hit, weight, 0.0), axis=1, keepdims=True)
    return jnp.where(hit, 1.0, 0.0), scale


def far_kernel(ids_ref, gate_ref, act_ref, grad_ref, out_ref):
    experts, _, count, tile = out_ref.shape
    toks = ids_ref.shape[1]
    slots = lax.broadcasted_iota(jnp.int32, (experts, count, toks), 1)
    mask, scale = choose(ids_ref[...], gate_ref[...], slots)
    mask = mask.astype(BF16)
    rows = jnp.dot(mask, act_ref[...], preferred_element_type=F32).astype(BF16)
    picked = jnp.dot(mask, grad_ref[...], preferred_element_type=F32)
    out_ref[:, 0] = rows.reshape(experts, count, tile)
    out_ref[:, 1] = (picked * scale).astype(BF16).reshape(experts, count, tile)


def near_kernel(
    half, tp_ref, ids_hbm, gate_hbm, act_hbm, grad_hbm, out_ref, ids_ref, gate_ref, act_ref, grad_ref, sems
):
    pairs = ((ids_hbm, ids_ref), (gate_hbm, gate_ref), (act_hbm, act_ref), (grad_hbm, grad_ref))
    copies = [pltpu.make_async_copy(a, b, sems.at[i]) for i, (a, b) in enumerate(pairs)]
    for copy in copies:
        copy.start()
    experts, toks = out_ref.shape[0], ids_ref.shape[1]
    inner = lax.broadcasted_iota(jnp.int32, (experts, 8, toks), 1)
    slots = jnp.where(inner < 4, half + 2 * tp_ref[0] + inner % 2, -2)
    copies[0].wait()
    copies[1].wait()
    mask, scale = choose(ids_ref[...], gate_ref[...], slots)
    kind = (inner // 2).reshape(mask.shape)
    of_rows = jnp.where(kind == 0, mask, 0.0).astype(BF16)
    of_grads = jnp.where(kind == 1, mask, 0.0).astype(BF16)
    copies[2].wait()
    copies[3].wait()
    rows = jnp.dot(of_rows, act_ref[...], preferred_element_type=F32)
    picked = jnp.dot(of_grads, grad_ref[...], preferred_element_type=F32)
    both = (rows + picked * scale).reshape(experts, 8, -1)
    out_ref[...] = both[:, :4].astype(BF16)


def send_far(ids_t, gate_t, acts, grads, experts, half):
    toks, width = acts.shape
    tile = width // 4
    return pl.pallas_call(
        far_kernel,
        grid=(width // tile,),
        in_specs=[
            pl.BlockSpec((2, toks), lambda i: (0, 0)),
            pl.BlockSpec((2, toks), lambda i: (0, 0)),
            pl.BlockSpec((toks, tile), lambda i: (0, i)),
            pl.BlockSpec((toks, tile), lambda i: (0, i)),
        ],
        out_specs=pl.BlockSpec((experts, 2, half, tile), lambda i: (0, 0, 0, i)),
        out_shape=jax.ShapeDtypeStruct((experts, 2, half, width), BF16),
        compiler_params=pltpu.CompilerParams(vmem_limit_bytes=WHOLE),
        cost_estimate=pl.CostEstimate(
            flops=16 * experts * half * toks * width,
            bytes_accessed=4 * (toks + experts * half) * width,
            transcendentals=0,
        ),
    )(ids_t, gate_t, acts, grads)


def send_near(tp_at, ids_t, gate_t, acts, grads, experts, half):
    toks, width = acts.shape
    return pl.pallas_call(
        functools.partial(near_kernel, half),
        in_specs=[pl.BlockSpec(memory_space=pltpu.SMEM)]
        + [pl.BlockSpec(memory_space=pltpu.HBM)] * 4,
        out_specs=pl.BlockSpec(memory_space=VMEM),
        out_shape=jax.ShapeDtypeStruct((experts, 4, width), BF16),
        scratch_shapes=[
            VMEM((2, toks), ids_t.dtype),
            VMEM((2, toks), gate_t.dtype),
            VMEM((toks, width), acts.dtype),
            VMEM((toks, width), grads.dtype),
            pltpu.SemaphoreType.DMA((4,)),
        ],
        compiler_params=pltpu.CompilerParams(vmem_limit_bytes=WHOLE),
    )(tp_at, ids_t, gate_t, acts, grads)


def sort_kernel(in_ref, out_ref):
    every = in_ref[...].astype(F32)
    for kind in range(2):
        some = every[:, 2 * kind : 2 * kind + 2].reshape(out_ref.shape[1], -1)
        out_ref[kind] = some.astype(BF16)


def sort_kinds(near):
    chips, _, width = near.shape
    tile = width // 2
    return pl.pallas_call(
        sort_kernel,
        grid=(width // tile,),
        in_specs=[pl.BlockSpec((chips, 4, tile), lambda i: (0, 0, i))],
        out_specs=pl.BlockSpec((2, 2 * chips, tile), lambda i: (0, 0, i)),
        out_shape=pltpu.HBM((2, 2 * chips, width), BF16),
        compiler_params=pltpu.CompilerParams(vmem_limit_bytes=LIMIT),
    )(near)


def expert_kernel(
    far_ref, near_ref, g0, u0, g1, u1, d0, d1, part_ref, side_ref, pre_acc, back_acc, both_ref, kept
):
    units = g0.shape[0]
    half = pre_acc.shape[0] // 2
    contract = (((1,), (1,)), ((), ()))
    phase, at = pl.program_id(0), pl.program_id(1)

    @pl.when(phase == 0)
    def _():
        for i, ref in enumerate((g0, u0, g1, u1)):
            kept[at, i * units : (i + 1) * units] = ref[...]
        down = jnp.concatenate([d0[...], d1[...]], axis=0)
        for i, ref in enumerate((far_ref, near_ref)):
            rows = slice(i * half, (i + 1) * half)
            x = ref[:, 0].reshape(half, -1)
            g = ref[:, 1].reshape(half, -1)
            pre = lax.dot_general(x, kept[at], contract, preferred_element_type=F32)
            back = lax.dot_general(g, down, contract, preferred_element_type=F32)

            @pl.when(at == 0)
            def _():
                pre_acc[rows] = pre
                back_acc[rows] = back

            @pl.when(at > 0)
            def _():
                pre_acc[rows] += pre
                back_acc[rows] += back

    @pl.when((phase == 0) & (at == pl.num_programs(1) - 1))
    def _():
        for i in range(2):
            pre_gate = pre_acc[:, 2 * i * units : (2 * i + 1) * units]
            pre_up = pre_acc[:, (2 * i + 1) * units : (2 * i + 2) * units]
            back = back_acc[:, i * units : (i + 1) * units]
            sig = jax.nn.sigmoid(pre_gate)
            silu = pre_gate * sig
            hidden = (silu * pre_up).astype(BF16)
            d_gate = (back * pre_up * sig * (1.0 + pre_gate * (1.0 - sig))).astype(BF16)
            d_up = (back * silu).astype(BF16)
            base = 3 * i * units
            side_ref[base : base + units] = d_gate.T
            side_ref[base + units : base + 2 * units] = d_up.T
            side_ref[base + 2 * units : base + 3 * units] = hidden.T
            both_ref[:, 2 * i * units : (2 * i + 1) * units] = d_gate
            both_ref[:, (2 * i + 1) * units : (2 * i + 2) * units] = d_up
        outer, inner = near_ref.shape[0], near_ref.shape[2]
        to = lax.broadcasted_iota(jnp.int32, (half, half), 0)
        of = lax.broadcasted_iota(jnp.int32, (half, half), 1)
        chip, place = to // (2 * outer), to % (2 * outer)
        moved = of == (place // 2) * inner + 2 * chip + place % 2
        moved = jnp.where(moved, 1.0, 0.0).astype(BF16)
        both_ref[half:] = jnp.dot(moved, both_ref[half:], preferred_element_type=F32).astype(BF16)

    @pl.when(phase == 1)
    def _():
        part = jnp.dot(both_ref[...], kept[at], preferred_element_type=F32).astype(BF16)
        wide = part_ref.shape[2] // 2
        for j in range(part_ref.shape[0]):
            cut = part[:, j * wide : (j + 1) * wide]
            part_ref[j] = jnp.concatenate([cut[:half], cut[half:]], axis=1)


def expert_part(far, near, weights, pieces):
    width = far.shape[3]
    half = far.shape[0] * far.shape[2]
    units = weights[0].shape[0]
    steps = 2
    tile = width // steps
    last = steps - 1

    def first_phase(p, i):
        return jnp.where(p == 0, i, last)

    return pl.pallas_call(
        expert_kernel,
        grid=(2, steps),
        in_specs=[
            pl.BlockSpec(src.shape[:3] + (tile,), lambda p, i: (0, 0, 0, first_phase(p, i)))
            for src in (far, near)
        ]
        + [pl.BlockSpec((units, tile), lambda p, i: (0, first_phase(p, i)))] * 6,
        out_specs=[
            pl.BlockSpec((pieces // steps, half, 2 * width // pieces), lambda p, i: (p * i, 0, 0)),
            pl.BlockSpec((6 * units, 2 * half), lambda p, i: (0, 0)),
        ],
        out_shape=[
            pltpu.HBM((pieces, half, 2 * width // pieces), BF16),
            jax.ShapeDtypeStruct((6 * units, 2 * half), BF16),
        ],
        scratch_shapes=[
            VMEM((2 * half, 4 * units), F32),
            VMEM((2 * half, 2 * units), F32),
            VMEM((2 * half, 4 * units), BF16),
            VMEM((steps, 4 * units, tile), BF16),
        ],
        compiler_params=pltpu.CompilerParams(vmem_limit_bytes=PASS),
        cost_estimate=pl.CostEstimate(
            flops=40 * half * width * units,
            bytes_accessed=2 * (6 * half * width + 6 * units * width),
            transcendentals=4 * half * units,
        ),
    )(far, near, *weights)


def weight_kernel(base, far_ref, near_ref, side_ref, *refs):
    tile = far_ref.shape[3]
    units = side_ref.shape[0] // 6
    base = base * units

    def stacked(kind):
        return jnp.concatenate(
            [ref[:, kind].reshape(-1, tile) for ref in (far_ref, near_ref)], axis=0
        )

    pair = jnp.dot(side_ref[base : base + 2 * units], stacked(0), preferred_element_type=F32)
    down = jnp.dot(
        side_ref[base + 2 * units : base + 3 * units], stacked(1), preferred_element_type=F32
    )
    if len(refs) == 1:
        refs[0][: 2 * units] = pair.astype(BF16)
        refs[0][2 * units :] = down.astype(BF16)
    else:
        more_ref, gate_ref, up_ref, down_ref = refs
        pair += more_ref[: 2 * units].astype(F32)
        down += more_ref[2 * units :].astype(F32)
        gate_ref[...] = pair[:units].astype(BF16)
        up_ref[...] = pair[units:].astype(BF16)
        down_ref[...] = down.astype(BF16)


def weight_grads(far, near, side, more):
    width = far.shape[3]
    units = side.shape[0] // 6
    tile = width // 4
    specs = [
        pl.BlockSpec(far.shape[:3] + (tile,), lambda i: (0, 0, 0, i)),
        pl.BlockSpec(near.shape[:3] + (tile,), lambda i: (0, 0, 0, i)),
        pl.BlockSpec(side.shape, lambda i: (0, 0)),
    ]
    three = pl.BlockSpec((3 * units, tile), lambda i: (0, i))
    one = pl.BlockSpec((units, tile), lambda i: (0, i))
    if more is None:
        base, operands = 3, (far, near, side)
        out_specs, out_shape = three, jax.ShapeDtypeStruct((3 * units, width), BF16)
    else:
        base, operands = 0, (far, near, side, more)
        specs = specs + [three]
        out_specs, out_shape = [one] * 3, [jax.ShapeDtypeStruct((units, width), BF16)] * 3
    return pl.pallas_call(
        functools.partial(weight_kernel, base),
        grid=(width // tile,),
        in_specs=specs,
        out_specs=out_specs,
        out_shape=out_shape,
        compiler_params=pltpu.CompilerParams(vmem_limit_bytes=LIMIT),
        cost_estimate=pl.CostEstimate(
            flops=6 * side.shape[1] * width * units,
            bytes_accessed=2 * (2 * side.shape[1] * width + 6 * units * width),
            transcendentals=0,
        ),
    )(*operands)


def combine_kernel(ids_ref, back_ref, out_ref):
    experts, half = back_ref.shape[0], back_ref.shape[1]
    toks = ids_ref.shape[1]
    wide = out_ref.shape[1]
    _, _, rank = table(ids_ref[...], experts)
    slots = lax.broadcasted_iota(jnp.int32, (experts, half, toks), 1)
    rows = back_ref[...].reshape(experts * half, 2 * wide)
    total = gather_slots(rank, slots.astype(F32), rows)[:, :wide]
    total += gather_slots(rank, (slots + half).astype(F32), rows)[:, wide:]
    out_ref[...] = total.astype(BF16)


def gather_slots(rank, slots, rows):
    hit = jnp.where(rank[:, None, :] == slots, 1.0, 0.0).astype(BF16).reshape(rows.shape[0], -1)
    return lax.dot_general(hit, rows, (((0,), (0,)), ((), ())), preferred_element_type=F32)


def combine(ids_t, returned):
    toks = ids_t.shape[1]
    return pl.pallas_call(
        combine_kernel,
        in_specs=[pl.BlockSpec(memory_space=VMEM)] * 2,
        out_specs=pl.BlockSpec(memory_space=VMEM),
        out_shape=jax.ShapeDtypeStruct((toks, returned.shape[2] // 2), BF16),
        compiler_params=pltpu.CompilerParams(vmem_limit_bytes=LIMIT),
    )(ids_t, returned)


def per_device(activations, out_grad, expert_ids, gate_values, gate_proj, up_proj, down_proj):
    devices = lax.axis_size("exp")
    planes = lax.axis_size("tp")
    experts = devices // 2
    toks, width = activations.shape
    slots = 8 * toks // devices
    half = slots // 2
    tp_at = lax.axis_index("tp").astype(jnp.int32)[None]
    ids_t = expert_ids.T
    gate_t = gate_values.T
    swap = [(i, i ^ 1) for i in range(devices)]

    def trade(v):
        return lax.ppermute(v, "exp", swap)

    sides = [list(range(core, devices, 2)) for core in range(2)]

    def spread(v):
        return lax.all_to_all(
            v, "exp", split_axis=0, concat_axis=0, tiled=True, axis_index_groups=sides
        )

    near = send_near(tp_at, ids_t, gate_t, activations, out_grad, experts, half)
    near = spread(near)
    far = send_far(ids_t, gate_t, activations, out_grad, experts, half)
    near, far = lax.optimization_barrier((near, far))
    near = sort_kinds(near)
    near = lax.all_gather(near, "tp", axis=0, tiled=False)
    far = spread(far.reshape(experts, 2 * half, width)).reshape(far.shape)
    own = (gate_proj[0], up_proj[0], down_proj[0])
    other = tuple(trade(v) for v in own)
    weights = (own[0], own[1], other[0], other[1], own[2], other[2])
    both, side = expert_part(far, near, weights, planes)
    both, side = lax.optimization_barrier((both, side))
    shared = trade(weight_grads(far, near, side, None))
    gate_g, up_g, down_g = weight_grads(far, near, side, shared)
    mine = lax.psum_scatter(both, "tp", scatter_dimension=0, tiled=False)
    mine, gate_g, up_g, down_g = lax.optimization_barrier((mine, gate_g, up_g, down_g))
    returned = spread(mine.reshape(experts, half, -1))
    piece = combine(ids_t, returned)
    gathered = lax.all_gather(piece, "tp", axis=0, tiled=False)
    in_grad = jnp.transpose(gathered, (1, 0, 2)).reshape(toks, width)
    return (in_grad, gate_g[None], up_g[None], down_g[None])


def solution(mesh):
    return jax.shard_map(
        per_device,
        mesh=mesh,
        in_specs=(
            P("exp", None),
            P("exp", None),
            P("exp", None),
            P("exp", None),
            P("exp", "tp", None),
            P("exp", "tp", None),
            P("exp", "tp", None),
        ),
        out_specs=(
            P("exp", None),
            P("exp", "tp", None),
            P("exp", "tp", None),
            P("exp", "tp", None),
        ),
        check_vma=False,
    )
```

```python
import functools

import jax
import jax.numpy as jnp
from jax import lax
from jax.experimental import pallas as pl
from jax.experimental.pallas import tpu as pltpu
from jax.sharding import PartitionSpec as P

F32 = jnp.float32
BF16 = jnp.bfloat16
VMEM = pltpu.VMEM
LIMIT = 28 * 1024 * 1024
WHOLE = 60 * 1024 * 1024
PASS = 62 * 1024 * 1024


def table(ids, experts):
    toks = ids.shape[1]
    expert = lax.broadcasted_iota(jnp.int32, (experts, toks), 0)
    first = ids[0:1, :] == expert
    second = ids[1:2, :] == expert
    named = jnp.where(first | second, 1.0, 0.0)
    earlier = lax.broadcasted_iota(jnp.int32, (toks, toks), 0)
    later = lax.broadcasted_iota(jnp.int32, (toks, toks), 1)
    before = jnp.where(earlier < later, 1.0, 0.0).astype(BF16)
    rank = jnp.dot(named.astype(BF16), before, preferred_element_type=F32)
    return first, second, jnp.where(named > 0.0, rank, -1.0)


def choose(ids, gate, slots):
    experts, count, toks = slots.shape
    first, second, rank = table(ids, experts)
    gate = jnp.where(first, gate[0:1, :], 0.0) + jnp.where(second, gate[1:2, :], 0.0)
    hit = (rank[:, None, :] == slots.astype(F32)).reshape(experts * count, toks)
    weight = jnp.broadcast_to(gate[:, None, :], slots.shape).reshape(experts * count, toks)
    scale = jnp.sum(jnp.where(hit, weight, 0.0), axis=1, keepdims=True)
    return jnp.where(hit, 1.0, 0.0), scale


def far_kernel(ids_ref, gate_ref, act_ref, grad_ref, out_ref):
    experts, _, count, tile = out_ref.shape
    toks = ids_ref.shape[1]
    slots = lax.broadcasted_iota(jnp.int32, (experts, count, toks), 1)
    mask, scale = choose(ids_ref[...], gate_ref[...], slots)
    mask = mask.astype(BF16)
    rows = jnp.dot(mask, act_ref[...], preferred_element_type=F32).astype(BF16)
    picked = jnp.dot(mask, grad_ref[...], preferred_element_type=F32)
    out_ref[:, 0] = rows.reshape(experts, count, tile)
    out_ref[:, 1] = (picked * scale).astype(BF16).reshape(experts, count, tile)


def near_kernel(
    half, tp_ref, ids_hbm, gate_hbm, act_hbm, grad_hbm, out_ref, ids_ref, gate_ref, act_ref, grad_ref, sems
):
    pairs = ((ids_hbm, ids_ref), (gate_hbm, gate_ref), (act_hbm, act_ref), (grad_hbm, grad_ref))
    copies = [pltpu.make_async_copy(a, b, sems.at[i]) for i, (a, b) in enumerate(pairs)]
    for copy in copies:
        copy.start()
    experts, toks = out_ref.shape[0], ids_ref.shape[1]
    inner = lax.broadcasted_iota(jnp.int32, (experts, 8, toks), 1)
    slots = jnp.where(inner < 4, half + 2 * tp_ref[0] + inner % 2, -2)
    copies[0].wait()
    copies[1].wait()
    mask, scale = choose(ids_ref[...], gate_ref[...], slots)
    kind = (inner // 2).reshape(mask.shape)
    of_rows = jnp.where(kind == 0, mask, 0.0).astype(BF16)
    of_grads = jnp.where(kind == 1, mask, 0.0).astype(BF16)
    copies[2].wait()
    copies[3].wait()
    rows = jnp.dot(of_rows, act_ref[...], preferred_element_type=F32)
    picked = jnp.dot(of_grads, grad_ref[...], preferred_element_type=F32)
    both = (rows + picked * scale).reshape(experts, 8, -1)
    out_ref[...] = both[:, :4].astype(BF16)


def send_far(ids_t, gate_t, acts, grads, experts, half):
    toks, width = acts.shape
    tile = width // 4
    return pl.pallas_call(
        far_kernel,
        grid=(width // tile,),
        in_specs=[
            pl.BlockSpec((2, toks), lambda i: (0, 0)),
            pl.BlockSpec((2, toks), lambda i: (0, 0)),
            pl.BlockSpec((toks, tile), lambda i: (0, i)),
            pl.BlockSpec((toks, tile), lambda i: (0, i)),
        ],
        out_specs=pl.BlockSpec((experts, 2, half, tile), lambda i: (0, 0, 0, i)),
        out_shape=jax.ShapeDtypeStruct((experts, 2, half, width), BF16),
        compiler_params=pltpu.CompilerParams(vmem_limit_bytes=WHOLE),
        cost_estimate=pl.CostEstimate(
            flops=16 * experts * half * toks * width,
            bytes_accessed=4 * (toks + experts * half) * width,
            transcendentals=0,
        ),
    )(ids_t, gate_t, acts, grads)


def send_near(tp_at, ids_t, gate_t, acts, grads, experts, half):
    toks, width = acts.shape
    return pl.pallas_call(
        functools.partial(near_kernel, half),
        in_specs=[pl.BlockSpec(memory_space=pltpu.SMEM)]
        + [pl.BlockSpec(memory_space=pltpu.HBM)] * 4,
        out_specs=pl.BlockSpec(memory_space=VMEM),
        out_shape=jax.ShapeDtypeStruct((experts, 4, width), BF16),
        scratch_shapes=[
            VMEM((2, toks), ids_t.dtype),
            VMEM((2, toks), gate_t.dtype),
            VMEM((toks, width), acts.dtype),
            VMEM((toks, width), grads.dtype),
            pltpu.SemaphoreType.DMA((4,)),
        ],
        compiler_params=pltpu.CompilerParams(vmem_limit_bytes=WHOLE),
    )(tp_at, ids_t, gate_t, acts, grads)


def sort_kernel(in_ref, out_ref):
    every = in_ref[...].astype(F32)
    for kind in range(2):
        some = every[:, 2 * kind : 2 * kind + 2].reshape(out_ref.shape[1], -1)
        out_ref[kind] = some.astype(BF16)


def sort_kinds(near):
    chips, _, width = near.shape
    tile = width // 2
    return pl.pallas_call(
        sort_kernel,
        grid=(width // tile,),
        in_specs=[pl.BlockSpec((chips, 4, tile), lambda i: (0, 0, i))],
        out_specs=pl.BlockSpec((2, 2 * chips, tile), lambda i: (0, 0, i)),
        out_shape=pltpu.HBM((2, 2 * chips, width), BF16),
        compiler_params=pltpu.CompilerParams(vmem_limit_bytes=LIMIT),
    )(near)


def expert_kernel(
    far_ref, near_ref, g0, u0, g1, u1, d0, d1, part_ref, side_ref, pre_acc, back_acc, both_ref, kept
):
    units = g0.shape[0]
    half = pre_acc.shape[0] // 2
    contract = (((1,), (1,)), ((), ()))
    phase, at = pl.program_id(0), pl.program_id(1)

    @pl.when(phase == 0)
    def _():
        for i, ref in enumerate((g0, u0, g1, u1)):
            kept[at, i * units : (i + 1) * units] = ref[...]
        down = jnp.concatenate([d0[...], d1[...]], axis=0)
        for i, ref in enumerate((far_ref, near_ref)):
            rows = slice(i * half, (i + 1) * half)
            x = ref[:, 0].reshape(half, -1)
            g = ref[:, 1].reshape(half, -1)
            pre = lax.dot_general(x, kept[at], contract, preferred_element_type=F32)
            back = lax.dot_general(g, down, contract, preferred_element_type=F32)

            @pl.when(at == 0)
            def _():
                pre_acc[rows] = pre
                back_acc[rows] = back

            @pl.when(at > 0)
            def _():
                pre_acc[rows] += pre
                back_acc[rows] += back

    @pl.when((phase == 0) & (at == pl.num_programs(1) - 1))
    def _():
        for i in range(2):
            pre_gate = pre_acc[:, 2 * i * units : (2 * i + 1) * units]
            pre_up = pre_acc[:, (2 * i + 1) * units : (2 * i + 2) * units]
            back = back_acc[:, i * units : (i + 1) * units]
            sig = jax.nn.sigmoid(pre_gate)
            silu = pre_gate * sig
            hidden = (silu * pre_up).astype(BF16)
            d_gate = (back * pre_up * sig * (1.0 + pre_gate * (1.0 - sig))).astype(BF16)
            d_up = (back * silu).astype(BF16)
            base = 3 * i * units
            side_ref[base : base + units] = d_gate.T
            side_ref[base + units : base + 2 * units] = d_up.T
            side_ref[base + 2 * units : base + 3 * units] = hidden.T
            both_ref[:, 2 * i * units : (2 * i + 1) * units] = d_gate
            both_ref[:, (2 * i + 1) * units : (2 * i + 2) * units] = d_up
        outer, inner = near_ref.shape[0], near_ref.shape[2]
        to = lax.broadcasted_iota(jnp.int32, (half, half), 0)
        of = lax.broadcasted_iota(jnp.int32, (half, half), 1)
        chip, place = to // (2 * outer), to % (2 * outer)
        moved = of == (place // 2) * inner + 2 * chip + place % 2
        moved = jnp.where(moved, 1.0, 0.0).astype(BF16)
        both_ref[half:] = jnp.dot(moved, both_ref[half:], preferred_element_type=F32).astype(BF16)

    @pl.when(phase == 1)
    def _():
        part = jnp.dot(both_ref[...], kept[at], preferred_element_type=F32).astype(BF16)
        wide = part_ref.shape[2] // 2
        for j in range(part_ref.shape[0]):
            cut = part[:, j * wide : (j + 1) * wide]
            part_ref[j] = jnp.concatenate([cut[:half], cut[half:]], axis=1)


def expert_part(far, near, weights, pieces):
    width = far.shape[3]
    half = far.shape[0] * far.shape[2]
    units = weights[0].shape[0]
    steps = 2
    tile = width // steps
    last = steps - 1

    def first_phase(p, i):
        return jnp.where(p == 0, i, last)

    return pl.pallas_call(
        expert_kernel,
        grid=(2, steps),
        in_specs=[
            pl.BlockSpec(src.shape[:3] + (tile,), lambda p, i: (0, 0, 0, first_phase(p, i)))
            for src in (far, near)
        ]
        + [pl.BlockSpec((units, tile), lambda p, i: (0, first_phase(p, i)))] * 6,
        out_specs=[
            pl.BlockSpec((pieces // steps, half, 2 * width // pieces), lambda p, i: (p * i, 0, 0)),
            pl.BlockSpec((6 * units, 2 * half), lambda p, i: (0, 0)),
        ],
        out_shape=[
            pltpu.HBM((pieces, half, 2 * width // pieces), BF16),
            jax.ShapeDtypeStruct((6 * units, 2 * half), BF16),
        ],
        scratch_shapes=[
            VMEM((2 * half, 4 * units), F32),
            VMEM((2 * half, 2 * units), F32),
            VMEM((2 * half, 4 * units), BF16),
            VMEM((steps, 4 * units, tile), BF16),
        ],
        compiler_params=pltpu.CompilerParams(vmem_limit_bytes=PASS),
        cost_estimate=pl.CostEstimate(
            flops=40 * half * width * units,
            bytes_accessed=2 * (6 * half * width + 6 * units * width),
            transcendentals=4 * half * units,
        ),
    )(far, near, *weights)


def weight_kernel(base, far_ref, near_ref, side_ref, *refs):
    tile = far_ref.shape[3]
    units = side_ref.shape[0] // 6
    base = base * units

    def stacked(kind):
        return jnp.concatenate(
            [ref[:, kind].reshape(-1, tile) for ref in (far_ref, near_ref)], axis=0
        )

    pair = jnp.dot(side_ref[base : base + 2 * units], stacked(0), preferred_element_type=F32)
    down = jnp.dot(
        side_ref[base + 2 * units : base + 3 * units], stacked(1), preferred_element_type=F32
    )
    if len(refs) == 1:
        refs[0][: 2 * units] = pair.astype(BF16)
        refs[0][2 * units :] = down.astype(BF16)
    else:
        more_ref, gate_ref, up_ref, down_ref = refs
        pair += more_ref[: 2 * units].astype(F32)
        down += more_ref[2 * units :].astype(F32)
        gate_ref[...] = pair[:units].astype(BF16)
        up_ref[...] = pair[units:].astype(BF16)
        down_ref[...] = down.astype(BF16)


def weight_grads(far, near, side, more):
    width = far.shape[3]
    units = side.shape[0] // 6
    tile = width // 4
    specs = [
        pl.BlockSpec(far.shape[:3] + (tile,), lambda i: (0, 0, 0, i)),
        pl.BlockSpec(near.shape[:3] + (tile,), lambda i: (0, 0, 0, i)),
        pl.BlockSpec(side.shape, lambda i: (0, 0)),
    ]
    three = pl.BlockSpec((3 * units, tile), lambda i: (0, i))
    one = pl.BlockSpec((units, tile), lambda i: (0, i))
    if more is None:
        base, operands = 3, (far, near, side)
        out_specs, out_shape = three, jax.ShapeDtypeStruct((3 * units, width), BF16)
    else:
        base, operands = 0, (far, near, side, more)
        specs = specs + [three]
        out_specs, out_shape = [one] * 3, [jax.ShapeDtypeStruct((units, width), BF16)] * 3
    return pl.pallas_call(
        functools.partial(weight_kernel, base),
        grid=(width // tile,),
        in_specs=specs,
        out_specs=out_specs,
        out_shape=out_shape,
        compiler_params=pltpu.CompilerParams(vmem_limit_bytes=LIMIT),
        cost_estimate=pl.CostEstimate(
            flops=6 * side.shape[1] * width * units,
            bytes_accessed=2 * (2 * side.shape[1] * width + 6 * units * width),
            transcendentals=0,
        ),
    )(*operands)


def combine_kernel(ids_ref, back_ref, out_ref):
    experts, half = back_ref.shape[0], back_ref.shape[1]
    toks = ids_ref.shape[1]
    wide = out_ref.shape[1]
    _, _, rank = table(ids_ref[...], experts)
    slots = lax.broadcasted_iota(jnp.int32, (experts, half, toks), 1)
    rows = back_ref[...].reshape(experts * half, 2 * wide)
    total = gather_slots(rank, slots.astype(F32), rows)[:, :wide]
    total += gather_slots(rank, (slots + half).astype(F32), rows)[:, wide:]
    out_ref[...] = total.astype(BF16)


def gather_slots(rank, slots, rows):
    hit = jnp.where(rank[:, None, :] == slots, 1.0, 0.0).astype(BF16).reshape(rows.shape[0], -1)
    return lax.dot_general(hit, rows, (((0,), (0,)), ((), ())), preferred_element_type=F32)


def combine(ids_t, returned):
    toks = ids_t.shape[1]
    return pl.pallas_call(
        combine_kernel,
        in_specs=[pl.BlockSpec(memory_space=VMEM)] * 2,
        out_specs=pl.BlockSpec(memory_space=VMEM),
        out_shape=jax.ShapeDtypeStruct((toks, returned.shape[2] // 2), BF16),
        compiler_params=pltpu.CompilerParams(vmem_limit_bytes=LIMIT),
    )(ids_t, returned)


def per_device(activations, out_grad, expert_ids, gate_values, gate_proj, up_proj, down_proj):
    devices = lax.axis_size("exp")
    planes = lax.axis_size("tp")
    experts = devices // 2
    toks, width = activations.shape
    slots = 8 * toks // devices
    half = slots // 2
    tp_at = lax.axis_index("tp").astype(jnp.int32)[None]
    ids_t = expert_ids.T
    gate_t = gate_values.T
    swap = [(i, i ^ 1) for i in range(devices)]

    def trade(v):
        return lax.ppermute(v, "exp", swap)

    sides = [list(range(core, devices, 2)) for core in range(2)]

    def spread(v):
        return lax.all_to_all(
            v, "exp", split_axis=0, concat_axis=0, tiled=True, axis_index_groups=sides
        )

    near = send_near(tp_at, ids_t, gate_t, activations, out_grad, experts, half)
    own = (gate_proj[0], up_proj[0], down_proj[0])
    other = tuple(trade(v) for v in own)
    other, ids_t = lax.optimization_barrier((other, ids_t))
    near = spread(near)
    far = send_far(ids_t, gate_t, activations, out_grad, experts, half)
    near, far = lax.optimization_barrier((near, far))
    near = sort_kinds(near)
    near = lax.all_gather(near, "tp", axis=0, tiled=False)
    far = spread(far.reshape(experts, 2 * half, width)).reshape(far.shape)
    weights = (own[0], own[1], other[0], other[1], own[2], other[2])
    both, side = expert_part(far, near, weights, planes)
    both, side = lax.optimization_barrier((both, side))
    shared = trade(weight_grads(far, near, side, None))
    gate_g, up_g, down_g = weight_grads(far, near, side, shared)
    mine = lax.psum_scatter(both, "tp", scatter_dimension=0, tiled=False)
    mine, gate_g, up_g, down_g = lax.optimization_barrier((mine, gate_g, up_g, down_g))
    returned = spread(mine.reshape(experts, half, -1))
    piece = combine(ids_t, returned)
    gathered = lax.all_gather(piece, "tp", axis=0, tiled=False)
    in_grad = jnp.transpose(gathered, (1, 0, 2)).reshape(toks, width)
    return (in_grad, gate_g[None], up_g[None], down_g[None])


def solution(mesh):
    return jax.shard_map(
        per_device,
        mesh=mesh,
        in_specs=(
            P("exp", None),
            P("exp", None),
            P("exp", None),
            P("exp", None),
            P("exp", "tp", None),
            P("exp", "tp", None),
            P("exp", "tp", None),
        ),
        out_specs=(
            P("exp", None),
            P("exp", "tp", None),
            P("exp", "tp", None),
            P("exp", "tp", None),
        ),
        check_vma=False,
    )
```

```python
import functools

import jax
import jax.numpy as jnp
from jax import lax
from jax.experimental import pallas as pl
from jax.experimental.pallas import tpu as pltpu
from jax.sharding import PartitionSpec as P

F32 = jnp.float32
BF16 = jnp.bfloat16
VMEM = pltpu.VMEM
LIMIT = 28 * 1024 * 1024
WHOLE = 60 * 1024 * 1024
PASS = 53 * 1024 * 1024


def table(ids, experts):
    toks = ids.shape[1]
    expert = lax.broadcasted_iota(jnp.int32, (experts, toks), 0)
    first = ids[0:1, :] == expert
    second = ids[1:2, :] == expert
    named = jnp.where(first | second, 1.0, 0.0)
    earlier = lax.broadcasted_iota(jnp.int32, (toks, toks), 0)
    later = lax.broadcasted_iota(jnp.int32, (toks, toks), 1)
    before = jnp.where(earlier < later, 1.0, 0.0).astype(BF16)
    rank = jnp.dot(named.astype(BF16), before, preferred_element_type=F32)
    return first, second, jnp.where(named > 0.0, rank, -1.0)


def choose(ids, gate, slots):
    experts, count, toks = slots.shape
    first, second, rank = table(ids, experts)
    gate = jnp.where(first, gate[0:1, :], 0.0) + jnp.where(second, gate[1:2, :], 0.0)
    hit = (rank[:, None, :] == slots.astype(F32)).reshape(experts * count, toks)
    weight = jnp.broadcast_to(gate[:, None, :], slots.shape).reshape(experts * count, toks)
    scale = jnp.sum(jnp.where(hit, weight, 0.0), axis=1, keepdims=True)
    return jnp.where(hit, 1.0, 0.0), scale


def far_kernel(ids_ref, gate_ref, act_ref, grad_ref, out_ref):
    experts, _, count, tile = out_ref.shape
    toks = ids_ref.shape[1]
    slots = lax.broadcasted_iota(jnp.int32, (experts, count, toks), 1)
    mask, scale = choose(ids_ref[...], gate_ref[...], slots)
    mask = mask.astype(BF16)
    rows = jnp.dot(mask, act_ref[...], preferred_element_type=F32).astype(BF16)
    picked = jnp.dot(mask, grad_ref[...], preferred_element_type=F32)
    out_ref[:, 0] = rows.reshape(experts, count, tile)
    out_ref[:, 1] = (picked * scale).astype(BF16).reshape(experts, count, tile)


def near_kernel(
    half, tp_ref, ids_hbm, gate_hbm, act_hbm, grad_hbm, out_ref, ids_ref, gate_ref, act_ref, grad_ref, sems
):
    pairs = ((ids_hbm, ids_ref), (gate_hbm, gate_ref), (act_hbm, act_ref), (grad_hbm, grad_ref))
    copies = [pltpu.make_async_copy(a, b, sems.at[i]) for i, (a, b) in enumerate(pairs)]
    for copy in copies:
        copy.start()
    experts, toks = out_ref.shape[0], ids_ref.shape[1]
    inner = lax.broadcasted_iota(jnp.int32, (experts, 8, toks), 1)
    slots = jnp.where(inner < 4, half + 2 * tp_ref[0] + inner % 2, -2)
    copies[0].wait()
    copies[1].wait()
    mask, scale = choose(ids_ref[...], gate_ref[...], slots)
    kind = (inner // 2).reshape(mask.shape)
    of_rows = jnp.where(kind == 0, mask, 0.0).astype(BF16)
    of_grads = jnp.where(kind == 1, mask, 0.0).astype(BF16)
    copies[2].wait()
    copies[3].wait()
    rows = jnp.dot(of_rows, act_ref[...], preferred_element_type=F32)
    picked = jnp.dot(of_grads, grad_ref[...], preferred_element_type=F32)
    both = (rows + picked * scale).reshape(experts, 8, -1)
    out_ref[...] = both[:, :4].astype(BF16)


def send_far(ids_t, gate_t, acts, grads, experts, half):
    toks, width = acts.shape
    tile = width // 4
    return pl.pallas_call(
        far_kernel,
        grid=(width // tile,),
        in_specs=[
            pl.BlockSpec((2, toks), lambda i: (0, 0)),
            pl.BlockSpec((2, toks), lambda i: (0, 0)),
            pl.BlockSpec((toks, tile), lambda i: (0, i)),
            pl.BlockSpec((toks, tile), lambda i: (0, i)),
        ],
        out_specs=pl.BlockSpec((experts, 2, half, tile), lambda i: (0, 0, 0, i)),
        out_shape=jax.ShapeDtypeStruct((experts, 2, half, width), BF16),
        compiler_params=pltpu.CompilerParams(vmem_limit_bytes=WHOLE),
        cost_estimate=pl.CostEstimate(
            flops=16 * experts * half * toks * width,
            bytes_accessed=4 * (toks + experts * half) * width,
            transcendentals=0,
        ),
    )(ids_t, gate_t, acts, grads)


def send_near(tp_at, ids_t, gate_t, acts, grads, experts, half):
    toks, width = acts.shape
    return pl.pallas_call(
        functools.partial(near_kernel, half),
        in_specs=[pl.BlockSpec(memory_space=pltpu.SMEM)]
        + [pl.BlockSpec(memory_space=pltpu.HBM)] * 4,
        out_specs=pl.BlockSpec(memory_space=VMEM),
        out_shape=jax.ShapeDtypeStruct((experts, 4, width), BF16),
        scratch_shapes=[
            VMEM((2, toks), ids_t.dtype),
            VMEM((2, toks), gate_t.dtype),
            VMEM((toks, width), acts.dtype),
            VMEM((toks, width), grads.dtype),
            pltpu.SemaphoreType.DMA((4,)),
        ],
        compiler_params=pltpu.CompilerParams(vmem_limit_bytes=WHOLE),
    )(tp_at, ids_t, gate_t, acts, grads)


def sort_kernel(in_ref, out_ref):
    every = in_ref[...].astype(F32)
    for kind in range(2):
        some = every[:, 2 * kind : 2 * kind + 2].reshape(out_ref.shape[1], -1)
        out_ref[kind] = some.astype(BF16)


def sort_kinds(near):
    chips, _, width = near.shape
    tile = width // 2
    return pl.pallas_call(
        sort_kernel,
        grid=(width // tile,),
        in_specs=[pl.BlockSpec((chips, 4, tile), lambda i: (0, 0, i))],
        out_specs=pl.BlockSpec((2, 2 * chips, tile), lambda i: (0, 0, i)),
        out_shape=pltpu.HBM((2, 2 * chips, width), BF16),
        compiler_params=pltpu.CompilerParams(vmem_limit_bytes=LIMIT),
    )(near)


def expert_kernel(
    far_ref, near_ref, g0, u0, g1, u1, d0, d1, part_ref, side_ref, pre_acc, back_acc, both_ref, kept
):
    units = g0.shape[0]
    half = pre_acc.shape[0] // 2
    contract = (((1,), (1,)), ((), ()))
    phase, at = pl.program_id(0), pl.program_id(1)

    @pl.when(phase == 0)
    def _():
        for i, ref in enumerate((g0, u0, g1, u1)):
            kept[at, i * units : (i + 1) * units] = ref[...]
        down = jnp.concatenate([d0[...], d1[...]], axis=0)
        x, g = [
            jnp.concatenate([ref[:, k].reshape(half, -1) for ref in (far_ref, near_ref)], axis=0)
            for k in range(2)
        ]
        pre = lax.dot_general(x, kept[at], contract, preferred_element_type=F32)
        back = lax.dot_general(g, down, contract, preferred_element_type=F32)

        @pl.when(at == 0)
        def _():
            pre_acc[...] = pre
            back_acc[...] = back

        @pl.when(at > 0)
        def _():
            pre_acc[...] += pre
            back_acc[...] += back

    @pl.when((phase == 0) & (at == pl.num_programs(1) - 1))
    def _():
        for i in range(2):
            pre_gate = pre_acc[:, 2 * i * units : (2 * i + 1) * units]
            pre_up = pre_acc[:, (2 * i + 1) * units : (2 * i + 2) * units]
            back = back_acc[:, i * units : (i + 1) * units]
            sig = jax.nn.sigmoid(pre_gate)
            silu = pre_gate * sig
            hidden = (silu * pre_up).astype(BF16)
            d_gate = (back * pre_up * sig * (1.0 + pre_gate * (1.0 - sig))).astype(BF16)
            d_up = (back * silu).astype(BF16)
            base = 3 * i * units
            side_ref[:, base : base + units] = d_gate
            side_ref[:, base + units : base + 2 * units] = d_up
            side_ref[:, base + 2 * units : base + 3 * units] = hidden
            both_ref[:, 2 * i * units : (2 * i + 1) * units] = d_gate
            both_ref[:, (2 * i + 1) * units : (2 * i + 2) * units] = d_up
        outer, inner = near_ref.shape[0], near_ref.shape[2]
        to = lax.broadcasted_iota(jnp.int32, (half, half), 0)
        of = lax.broadcasted_iota(jnp.int32, (half, half), 1)
        chip, place = to // (2 * outer), to % (2 * outer)
        moved = of == (place // 2) * inner + 2 * chip + place % 2
        moved = jnp.where(moved, 1.0, 0.0).astype(BF16)
        both_ref[half:] = jnp.dot(moved, both_ref[half:], preferred_element_type=F32).astype(BF16)

    @pl.when(phase == 1)
    def _():
        part = jnp.dot(both_ref[...], kept[at], preferred_element_type=F32).astype(BF16)
        wide = part_ref.shape[2] // 2
        for j in range(part_ref.shape[0]):
            cut = part[:, j * wide : (j + 1) * wide]
            part_ref[j] = jnp.concatenate([cut[:half], cut[half:]], axis=1)


def expert_part(far, near, weights, pieces):
    width = far.shape[3]
    half = far.shape[0] * far.shape[2]
    units = weights[0].shape[0]
    steps = 2
    tile = width // steps
    last = steps - 1

    def first_phase(p, i):
        return jnp.where(p == 0, i, last)

    return pl.pallas_call(
        expert_kernel,
        grid=(2, steps),
        in_specs=[
            pl.BlockSpec(src.shape[:3] + (tile,), lambda p, i: (0, 0, 0, first_phase(p, i)))
            for src in (far, near)
        ]
        + [pl.BlockSpec((units, tile), lambda p, i: (0, first_phase(p, i)))] * 6,
        out_specs=[
            pl.BlockSpec((pieces // steps, half, 2 * width // pieces), lambda p, i: (p * i, 0, 0)),
            pl.BlockSpec((2 * half, 6 * units), lambda p, i: (0, 0)),
        ],
        out_shape=[
            pltpu.HBM((pieces, half, 2 * width // pieces), BF16),
            jax.ShapeDtypeStruct((2 * half, 6 * units), BF16),
        ],
        scratch_shapes=[
            VMEM((2 * half, 4 * units), F32),
            VMEM((2 * half, 2 * units), F32),
            VMEM((2 * half, 4 * units), BF16),
            VMEM((steps, 4 * units, tile), BF16),
        ],
        compiler_params=pltpu.CompilerParams(vmem_limit_bytes=PASS),
        cost_estimate=pl.CostEstimate(
            flops=40 * half * width * units,
            bytes_accessed=2 * (6 * half * width + 6 * units * width),
            transcendentals=4 * half * units,
        ),
    )(far, near, *weights)


def weight_kernel(base, far_ref, near_ref, side_ref, *refs):
    tile = far_ref.shape[3]
    units = side_ref.shape[1] // 6
    contract = (((0,), (0,)), ((), ()))
    base = base * units

    def stacked(kind):
        return jnp.concatenate(
            [ref[:, kind].reshape(-1, tile) for ref in (far_ref, near_ref)], axis=0
        )

    left = side_ref[:, base : base + 2 * units]
    pair = lax.dot_general(left, stacked(0), contract, preferred_element_type=F32)
    left = side_ref[:, base + 2 * units : base + 3 * units]
    down = lax.dot_general(left, stacked(1), contract, preferred_element_type=F32)
    if len(refs) == 1:
        refs[0][: 2 * units] = pair.astype(BF16)
        refs[0][2 * units :] = down.astype(BF16)
    else:
        more_ref, gate_ref, up_ref, down_ref = refs
        pair += more_ref[: 2 * units].astype(F32)
        down += more_ref[2 * units :].astype(F32)
        gate_ref[...] = pair[:units].astype(BF16)
        up_ref[...] = pair[units:].astype(BF16)
        down_ref[...] = down.astype(BF16)


def weight_grads(far, near, side, more):
    width = far.shape[3]
    units = side.shape[1] // 6
    tile = width // 4
    specs = [
        pl.BlockSpec(far.shape[:3] + (tile,), lambda i: (0, 0, 0, i)),
        pl.BlockSpec(near.shape[:3] + (tile,), lambda i: (0, 0, 0, i)),
        pl.BlockSpec(side.shape, lambda i: (0, 0)),
    ]
    three = pl.BlockSpec((3 * units, tile), lambda i: (0, i))
    one = pl.BlockSpec((units, tile), lambda i: (0, i))
    if more is None:
        base, operands = 3, (far, near, side)
        out_specs, out_shape = three, jax.ShapeDtypeStruct((3 * units, width), BF16)
    else:
        base, operands = 0, (far, near, side, more)
        specs = specs + [three]
        out_specs, out_shape = [one] * 3, [jax.ShapeDtypeStruct((units, width), BF16)] * 3
    return pl.pallas_call(
        functools.partial(weight_kernel, base),
        grid=(width // tile,),
        in_specs=specs,
        out_specs=out_specs,
        out_shape=out_shape,
        compiler_params=pltpu.CompilerParams(vmem_limit_bytes=LIMIT),
        cost_estimate=pl.CostEstimate(
            flops=6 * side.shape[0] * width * units,
            bytes_accessed=2 * (2 * side.shape[0] * width + 6 * units * width),
            transcendentals=0,
        ),
    )(*operands)


def combine_kernel(ids_ref, back_ref, out_ref):
    experts, half = back_ref.shape[0], back_ref.shape[1]
    toks = ids_ref.shape[1]
    wide = out_ref.shape[1]
    _, _, rank = table(ids_ref[...], experts)
    slots = lax.broadcasted_iota(jnp.int32, (experts, half, toks), 1)
    rows = back_ref[...].reshape(experts * half, 2 * wide)
    total = gather_slots(rank, slots.astype(F32), rows)[:, :wide]
    total += gather_slots(rank, (slots + half).astype(F32), rows)[:, wide:]
    out_ref[...] = total.astype(BF16)


def gather_slots(rank, slots, rows):
    hit = jnp.where(rank[:, None, :] == slots, 1.0, 0.0).astype(BF16).reshape(rows.shape[0], -1)
    return lax.dot_general(hit, rows, (((0,), (0,)), ((), ())), preferred_element_type=F32)


def combine(ids_t, returned):
    toks = ids_t.shape[1]
    return pl.pallas_call(
        combine_kernel,
        in_specs=[pl.BlockSpec(memory_space=VMEM)] * 2,
        out_specs=pl.BlockSpec(memory_space=VMEM),
        out_shape=jax.ShapeDtypeStruct((toks, returned.shape[2] // 2), BF16),
        compiler_params=pltpu.CompilerParams(vmem_limit_bytes=LIMIT),
    )(ids_t, returned)


def per_device(activations, out_grad, expert_ids, gate_values, gate_proj, up_proj, down_proj):
    devices = lax.axis_size("exp")
    planes = lax.axis_size("tp")
    experts = devices // 2
    toks, width = activations.shape
    slots = 8 * toks // devices
    half = slots // 2
    tp_at = lax.axis_index("tp").astype(jnp.int32)[None]
    ids_t = expert_ids.T
    gate_t = gate_values.T
    swap = [(i, i ^ 1) for i in range(devices)]

    def trade(v):
        return lax.ppermute(v, "exp", swap)

    sides = [list(range(core, devices, 2)) for core in range(2)]

    def spread(v):
        return lax.all_to_all(
            v, "exp", split_axis=0, concat_axis=0, tiled=True, axis_index_groups=sides
        )

    near = send_near(tp_at, ids_t, gate_t, activations, out_grad, experts, half)
    own = (gate_proj[0], up_proj[0], down_proj[0])
    other = tuple(trade(v) for v in own)
    other, ids_t = lax.optimization_barrier((other, ids_t))
    near = spread(near)
    far = send_far(ids_t, gate_t, activations, out_grad, experts, half)
    near, far = lax.optimization_barrier((near, far))
    near = sort_kinds(near)
    near = lax.all_gather(near, "tp", axis=0, tiled=False)
    far = spread(far.reshape(experts, 2 * half, width)).reshape(far.shape)
    weights = (own[0], own[1], other[0], other[1], own[2], other[2])
    both, side = expert_part(far, near, weights, planes)
    both, side = lax.optimization_barrier((both, side))
    shared = trade(weight_grads(far, near, side, None))
    gate_g, up_g, down_g = weight_grads(far, near, side, shared)
    mine = lax.psum_scatter(both, "tp", scatter_dimension=0, tiled=False)
    mine, gate_g, up_g, down_g = lax.optimization_barrier((mine, gate_g, up_g, down_g))
    returned = spread(mine.reshape(experts, half, -1))
    piece = combine(ids_t, returned)
    gathered = lax.all_gather(piece, "tp", axis=0, tiled=False)
    in_grad = jnp.transpose(gathered, (1, 0, 2)).reshape(toks, width)
    return (in_grad, gate_g[None], up_g[None], down_g[None])


def solution(mesh):
    return jax.shard_map(
        per_device,
        mesh=mesh,
        in_specs=(
            P("exp", None),
            P("exp", None),
            P("exp", None),
            P("exp", None),
            P("exp", "tp", None),
            P("exp", "tp", None),
            P("exp", "tp", None),
        ),
        out_specs=(
            P("exp", None),
            P("exp", "tp", None),
            P("exp", "tp", None),
            P("exp", "tp", None),
        ),
        check_vma=False,
    )
```

```python
import functools

import jax
import jax.numpy as jnp
from jax import lax
from jax.experimental import pallas as pl
from jax.experimental.pallas import tpu as pltpu
from jax.sharding import PartitionSpec as P

F32 = jnp.float32
BF16 = jnp.bfloat16
VMEM = pltpu.VMEM
LIMIT = 28 * 1024 * 1024
WHOLE = 60 * 1024 * 1024
PASS = 53 * 1024 * 1024


def table(ids, experts):
    toks = ids.shape[1]
    expert = lax.broadcasted_iota(jnp.int32, (experts, toks), 0)
    first = ids[0:1, :] == expert
    second = ids[1:2, :] == expert
    named = jnp.where(first | second, 1.0, 0.0)
    earlier = lax.broadcasted_iota(jnp.int32, (toks, toks), 0)
    later = lax.broadcasted_iota(jnp.int32, (toks, toks), 1)
    before = jnp.where(earlier < later, 1.0, 0.0).astype(BF16)
    rank = jnp.dot(named.astype(BF16), before, preferred_element_type=F32)
    return first, second, jnp.where(named > 0.0, rank, -1.0)


def choose(ids, gate, slots):
    experts, count, toks = slots.shape
    first, second, rank = table(ids, experts)
    gate = jnp.where(first, gate[0:1, :], 0.0) + jnp.where(second, gate[1:2, :], 0.0)
    hit = (rank[:, None, :] == slots.astype(F32)).reshape(experts * count, toks)
    weight = jnp.broadcast_to(gate[:, None, :], slots.shape).reshape(experts * count, toks)
    scale = jnp.sum(jnp.where(hit, weight, 0.0), axis=1, keepdims=True)
    return jnp.where(hit, 1.0, 0.0), scale


def far_kernel(ids_ref, gate_ref, act_ref, grad_ref, out_ref):
    experts, _, count, tile = out_ref.shape
    toks = ids_ref.shape[1]
    slots = lax.broadcasted_iota(jnp.int32, (experts, count, toks), 1)
    mask, scale = choose(ids_ref[...], gate_ref[...], slots)
    mask = mask.astype(BF16)
    rows = jnp.dot(mask, act_ref[...], preferred_element_type=F32).astype(BF16)
    picked = jnp.dot(mask, grad_ref[...], preferred_element_type=F32)
    out_ref[:, 0] = rows.reshape(experts, count, tile)
    out_ref[:, 1] = (picked * scale).astype(BF16).reshape(experts, count, tile)


def near_kernel(
    half, tp_ref, ids_hbm, gate_hbm, act_hbm, grad_hbm, out_ref, ids_ref, gate_ref, act_ref, grad_ref, sems
):
    pairs = ((ids_hbm, ids_ref), (gate_hbm, gate_ref), (act_hbm, act_ref), (grad_hbm, grad_ref))
    copies = [pltpu.make_async_copy(a, b, sems.at[i]) for i, (a, b) in enumerate(pairs)]
    for copy in copies:
        copy.start()
    experts, toks = out_ref.shape[0], ids_ref.shape[1]
    inner = lax.broadcasted_iota(jnp.int32, (experts, 8, toks), 1)
    slots = jnp.where(inner < 4, half + 2 * tp_ref[0] + inner % 2, -2)
    copies[0].wait()
    copies[1].wait()
    mask, scale = choose(ids_ref[...], gate_ref[...], slots)
    kind = (inner // 2).reshape(mask.shape)
    of_rows = jnp.where(kind == 0, mask, 0.0).astype(BF16)
    of_grads = jnp.where(kind == 1, mask, 0.0).astype(BF16)
    copies[2].wait()
    copies[3].wait()
    rows = jnp.dot(of_rows, act_ref[...], preferred_element_type=F32)
    picked = jnp.dot(of_grads, grad_ref[...], preferred_element_type=F32)
    both = (rows + picked * scale).reshape(experts, 8, -1)
    out_ref[...] = both[:, :4].astype(BF16)


def send_far(ids_t, gate_t, acts, grads, experts, half):
    toks, width = acts.shape
    tile = width // 4
    return pl.pallas_call(
        far_kernel,
        grid=(width // tile,),
        in_specs=[
            pl.BlockSpec((2, toks), lambda i: (0, 0)),
            pl.BlockSpec((2, toks), lambda i: (0, 0)),
            pl.BlockSpec((toks, tile), lambda i: (0, i)),
            pl.BlockSpec((toks, tile), lambda i: (0, i)),
        ],
        out_specs=pl.BlockSpec((experts, 2, half, tile), lambda i: (0, 0, 0, i)),
        out_shape=jax.ShapeDtypeStruct((experts, 2, half, width), BF16),
        compiler_params=pltpu.CompilerParams(vmem_limit_bytes=WHOLE),
        cost_estimate=pl.CostEstimate(
            flops=16 * experts * half * toks * width,
            bytes_accessed=4 * (toks + experts * half) * width,
            transcendentals=0,
        ),
    )(ids_t, gate_t, acts, grads)


def send_near(tp_at, ids_t, gate_t, acts, grads, experts, half):
    toks, width = acts.shape
    return pl.pallas_call(
        functools.partial(near_kernel, half),
        in_specs=[pl.BlockSpec(memory_space=pltpu.SMEM)]
        + [pl.BlockSpec(memory_space=pltpu.HBM)] * 4,
        out_specs=pl.BlockSpec(memory_space=VMEM),
        out_shape=jax.ShapeDtypeStruct((experts, 4, width), BF16),
        scratch_shapes=[
            VMEM((2, toks), ids_t.dtype),
            VMEM((2, toks), gate_t.dtype),
            VMEM((toks, width), acts.dtype),
            VMEM((toks, width), grads.dtype),
            pltpu.SemaphoreType.DMA((4,)),
        ],
        compiler_params=pltpu.CompilerParams(vmem_limit_bytes=WHOLE),
    )(tp_at, ids_t, gate_t, acts, grads)


def sort_kernel(in_ref, out_ref):
    every = in_ref[...].astype(F32)
    for kind in range(2):
        some = every[:, 2 * kind : 2 * kind + 2].reshape(out_ref.shape[1], -1)
        out_ref[kind] = some.astype(BF16)


def sort_kinds(near):
    chips, _, width = near.shape
    tile = width // 2
    return pl.pallas_call(
        sort_kernel,
        grid=(width // tile,),
        in_specs=[pl.BlockSpec((chips, 4, tile), lambda i: (0, 0, i))],
        out_specs=pl.BlockSpec((2, 2 * chips, tile), lambda i: (0, 0, i)),
        out_shape=pltpu.HBM((2, 2 * chips, width), BF16),
        compiler_params=pltpu.CompilerParams(vmem_limit_bytes=LIMIT),
    )(near)


def expert_kernel(
    far_ref, near_ref, g0, u0, g1, u1, d0, d1, part_ref, side_ref, pre_acc, back_acc, both_ref, kept
):
    units = g0.shape[0]
    half = pre_acc.shape[0] // 2
    contract = (((1,), (1,)), ((), ()))
    phase, at = pl.program_id(0), pl.program_id(1)

    @pl.when(phase == 0)
    def _():
        for i, ref in enumerate((g0, u0, g1, u1)):
            kept[at, i * units : (i + 1) * units] = ref[...]
        down = jnp.concatenate([d0[...], d1[...]], axis=0)
        x, g = [
            jnp.concatenate([ref[:, k].reshape(half, -1) for ref in (far_ref, near_ref)], axis=0)
            for k in range(2)
        ]
        pre = lax.dot_general(x, kept[at], contract, preferred_element_type=F32)
        back = lax.dot_general(g, down, contract, preferred_element_type=F32)

        @pl.when(at == 0)
        def _():
            pre_acc[...] = pre
            back_acc[...] = back

        @pl.when(at > 0)
        def _():
            pre_acc[...] += pre
            back_acc[...] += back

    @pl.when((phase == 0) & (at == pl.num_programs(1) - 1))
    def _():
        for i in range(2):
            pre_gate = pre_acc[:, 2 * i * units : (2 * i + 1) * units]
            pre_up = pre_acc[:, (2 * i + 1) * units : (2 * i + 2) * units]
            back = back_acc[:, i * units : (i + 1) * units]
            sig = jax.nn.sigmoid(pre_gate)
            silu = pre_gate * sig
            hidden = (silu * pre_up).astype(BF16)
            d_gate = (back * pre_up * sig * (1.0 + pre_gate * (1.0 - sig))).astype(BF16)
            d_up = (back * silu).astype(BF16)
            base = 3 * i * units
            side_ref[:, base : base + units] = d_gate
            side_ref[:, base + units : base + 2 * units] = d_up
            side_ref[:, base + 2 * units : base + 3 * units] = hidden
            both_ref[:, 2 * i * units : (2 * i + 1) * units] = d_gate
            both_ref[:, (2 * i + 1) * units : (2 * i + 2) * units] = d_up
        outer, inner = near_ref.shape[0], near_ref.shape[2]
        to = lax.broadcasted_iota(jnp.int32, (half, half), 0)
        of = lax.broadcasted_iota(jnp.int32, (half, half), 1)
        chip, place = to // (2 * outer), to % (2 * outer)
        moved = of == (place // 2) * inner + 2 * chip + place % 2
        moved = jnp.where(moved, 1.0, 0.0).astype(BF16)
        both_ref[half:] = jnp.dot(moved, both_ref[half:], preferred_element_type=F32).astype(BF16)

    @pl.when(phase == 1)
    def _():
        part = jnp.dot(both_ref[...], kept[at], preferred_element_type=F32).astype(BF16)
        wide = part_ref.shape[2] // 2
        for j in range(part_ref.shape[0]):
            cut = part[:, j * wide : (j + 1) * wide]
            part_ref[j] = jnp.concatenate([cut[:half], cut[half:]], axis=1)


def expert_part(far, near, weights, pieces):
    width = far.shape[3]
    half = far.shape[0] * far.shape[2]
    units = weights[0].shape[0]
    steps = 2
    tile = width // steps
    last = steps - 1

    def first_phase(p, i):
        return jnp.where(p == 0, i, last)

    return pl.pallas_call(
        expert_kernel,
        grid=(2, steps),
        in_specs=[
            pl.BlockSpec(src.shape[:3] + (tile,), lambda p, i: (0, 0, 0, first_phase(p, i)))
            for src in (far, near)
        ]
        + [pl.BlockSpec((units, tile), lambda p, i: (0, first_phase(p, i)))] * 6,
        out_specs=[
            pl.BlockSpec((pieces // steps, half, 2 * width // pieces), lambda p, i: (p * i, 0, 0)),
            pl.BlockSpec((2 * half, 6 * units), lambda p, i: (0, 0)),
        ],
        out_shape=[
            pltpu.HBM((pieces, half, 2 * width // pieces), BF16),
            jax.ShapeDtypeStruct((2 * half, 6 * units), BF16),
        ],
        scratch_shapes=[
            VMEM((2 * half, 4 * units), F32),
            VMEM((2 * half, 2 * units), F32),
            VMEM((2 * half, 4 * units), BF16),
            VMEM((steps, 4 * units, tile), BF16),
        ],
        compiler_params=pltpu.CompilerParams(vmem_limit_bytes=PASS),
        cost_estimate=pl.CostEstimate(
            flops=40 * half * width * units,
            bytes_accessed=2 * (6 * half * width + 6 * units * width),
            transcendentals=4 * half * units,
        ),
    )(far, near, *weights)


def weight_kernel(base, far_ref, near_ref, side_ref, *refs):
    tile = far_ref.shape[3]
    units = side_ref.shape[1] // 6
    contract = (((0,), (0,)), ((), ()))
    base = base * units

    def stacked(kind):
        return jnp.concatenate(
            [ref[:, kind].reshape(-1, tile) for ref in (far_ref, near_ref)], axis=0
        )

    left = side_ref[:, base : base + 2 * units]
    pair = lax.dot_general(left, stacked(0), contract, preferred_element_type=F32)
    left = side_ref[:, base + 2 * units : base + 3 * units]
    down = lax.dot_general(left, stacked(1), contract, preferred_element_type=F32)
    if len(refs) == 1:
        refs[0][: 2 * units] = pair.astype(BF16)
        refs[0][2 * units :] = down.astype(BF16)
    else:
        more_ref, gate_ref, up_ref, down_ref = refs
        pair += more_ref[: 2 * units].astype(F32)
        down += more_ref[2 * units :].astype(F32)
        gate_ref[...] = pair[:units].astype(BF16)
        up_ref[...] = pair[units:].astype(BF16)
        down_ref[...] = down.astype(BF16)


def weight_grads(far, near, side, more):
    width = far.shape[3]
    units = side.shape[1] // 6
    tile = width // 4
    specs = [
        pl.BlockSpec(far.shape[:3] + (tile,), lambda i: (0, 0, 0, i)),
        pl.BlockSpec(near.shape[:3] + (tile,), lambda i: (0, 0, 0, i)),
        pl.BlockSpec(side.shape, lambda i: (0, 0)),
    ]
    three = pl.BlockSpec((3 * units, tile), lambda i: (0, i))
    one = pl.BlockSpec((units, tile), lambda i: (0, i))
    if more is None:
        base, operands = 3, (far, near, side)
        out_specs, out_shape = three, jax.ShapeDtypeStruct((3 * units, width), BF16)
    else:
        base, operands = 0, (far, near, side, more)
        specs = specs + [three]
        out_specs, out_shape = [one] * 3, [jax.ShapeDtypeStruct((units, width), BF16)] * 3
    return pl.pallas_call(
        functools.partial(weight_kernel, base),
        grid=(width // tile,),
        in_specs=specs,
        out_specs=out_specs,
        out_shape=out_shape,
        compiler_params=pltpu.CompilerParams(vmem_limit_bytes=LIMIT),
        cost_estimate=pl.CostEstimate(
            flops=6 * side.shape[0] * width * units,
            bytes_accessed=2 * (2 * side.shape[0] * width + 6 * units * width),
            transcendentals=0,
        ),
    )(*operands)


def combine_kernel(ids_ref, back_ref, out_ref):
    experts, half = back_ref.shape[0], back_ref.shape[1]
    toks = ids_ref.shape[1]
    wide = out_ref.shape[1]
    _, _, rank = table(ids_ref[...], experts)
    slots = lax.broadcasted_iota(jnp.int32, (experts, half, toks), 1)
    rows = back_ref[...].reshape(experts * half, 2 * wide)
    total = gather_slots(rank, slots.astype(F32), rows)[:, :wide]
    total += gather_slots(rank, (slots + half).astype(F32), rows)[:, wide:]
    out_ref[...] = total.astype(BF16)


def gather_slots(rank, slots, rows):
    hit = jnp.where(rank[:, None, :] == slots, 1.0, 0.0).astype(BF16).reshape(rows.shape[0], -1)
    return lax.dot_general(hit, rows, (((0,), (0,)), ((), ())), preferred_element_type=F32)


def combine(ids_t, returned):
    toks = ids_t.shape[1]
    return pl.pallas_call(
        combine_kernel,
        in_specs=[pl.BlockSpec(memory_space=VMEM)] * 2,
        out_specs=pl.BlockSpec(memory_space=VMEM),
        out_shape=jax.ShapeDtypeStruct((toks, returned.shape[2] // 2), BF16),
        compiler_params=pltpu.CompilerParams(vmem_limit_bytes=LIMIT),
    )(ids_t, returned)


def order_kernel(tp_ref, *refs):
    pieces, out_ref, kept = refs[:-2], refs[-2], refs[-1]
    count, toks, wide = kept.shape
    reach = count // 2 - 1
    me = tp_ref[0]
    kept[me] = pieces[0][...]
    for step in range(1, reach + 1):
        kept[lax.rem(me + count - step, count)] = pieces[2 * step - 1][...]
        kept[lax.rem(me + step, count)] = pieces[2 * step][...]
    far = lax.rem(me + count // 2, count)
    kept[far, : toks // 2] = pieces[-2][...]
    kept[far, toks // 2 :] = pieces[-1][...]
    for k in range(0, count, 2):
        out_ref[:, k * wide : (k + 2) * wide] = jnp.concatenate([kept[k], kept[k + 1]], axis=1)


def gather_columns(tp_at, piece, count):
    toks, wide = piece.shape
    up = [(i, (i + 1) % count) for i in range(count)]
    down = [(i, (i - 1) % count) for i in range(count)]
    from_below, from_above = piece, piece
    pieces = [piece]
    for _ in range(count // 2 - 1):
        from_below = lax.ppermute(from_below, "tp", up)
        from_above = lax.ppermute(from_above, "tp", down)
        pieces += [from_below, from_above]
    pieces.append(lax.ppermute(from_below[: toks // 2], "tp", up))
    pieces.append(lax.ppermute(from_above[toks // 2 :], "tp", down))
    return pl.pallas_call(
        order_kernel,
        in_specs=[pl.BlockSpec(memory_space=pltpu.SMEM)]
        + [pl.BlockSpec(memory_space=VMEM)] * len(pieces),
        out_specs=pl.BlockSpec(memory_space=VMEM),
        out_shape=jax.ShapeDtypeStruct((toks, count * wide), BF16),
        scratch_shapes=[VMEM((count, toks, wide), BF16)],
        compiler_params=pltpu.CompilerParams(vmem_limit_bytes=LIMIT),
    )(tp_at, *pieces)


def per_device(activations, out_grad, expert_ids, gate_values, gate_proj, up_proj, down_proj):
    devices = lax.axis_size("exp")
    planes = lax.axis_size("tp")
    experts = devices // 2
    toks, width = activations.shape
    slots = 8 * toks // devices
    half = slots // 2
    tp_at = lax.axis_index("tp").astype(jnp.int32)[None]
    ids_t = expert_ids.T
    gate_t = gate_values.T
    swap = [(i, i ^ 1) for i in range(devices)]

    def trade(v):
        return lax.ppermute(v, "exp", swap)

    sides = [list(range(core, devices, 2)) for core in range(2)]

    def spread(v):
        return lax.all_to_all(
            v, "exp", split_axis=0, concat_axis=0, tiled=True, axis_index_groups=sides
        )

    near = send_near(tp_at, ids_t, gate_t, activations, out_grad, experts, half)
    own = (gate_proj[0], up_proj[0], down_proj[0])
    other = tuple(trade(v) for v in own)
    other, ids_t = lax.optimization_barrier((other, ids_t))
    near = spread(near)
    far = send_far(ids_t, gate_t, activations, out_grad, experts, half)
    near, far = lax.optimization_barrier((near, far))
    near = sort_kinds(near)
    near = lax.all_gather(near, "tp", axis=0, tiled=False)
    far = spread(far.reshape(experts, 2 * half, width)).reshape(far.shape)
    weights = (own[0], own[1], other[0], other[1], own[2], other[2])
    both, side = expert_part(far, near, weights, planes)
    both, side = lax.optimization_barrier((both, side))
    shared = trade(weight_grads(far, near, side, None))
    gate_g, up_g, down_g = weight_grads(far, near, side, shared)
    mine = lax.psum_scatter(both, "tp", scatter_dimension=0, tiled=False)
    mine, gate_g, up_g, down_g = lax.optimization_barrier((mine, gate_g, up_g, down_g))
    returned = spread(mine.reshape(experts, half, -1))
    piece = combine(ids_t, returned)
    in_grad = gather_columns(tp_at, piece, planes)
    return (in_grad, gate_g[None], up_g[None], down_g[None])


def solution(mesh):
    return jax.shard_map(
        per_device,
        mesh=mesh,
        in_specs=(
            P("exp", None),
            P("exp", None),
            P("exp", None),
            P("exp", None),
            P("exp", "tp", None),
            P("exp", "tp", None),
            P("exp", "tp", None),
        ),
        out_specs=(
            P("exp", None),
            P("exp", "tp", None),
            P("exp", "tp", None),
            P("exp", "tp", None),
        ),
        check_vma=False,
    )
```

```python
import functools

import jax
import jax.numpy as jnp
from jax import lax
from jax.experimental import pallas as pl
from jax.experimental.pallas import tpu as pltpu
from jax.sharding import PartitionSpec as P

F32 = jnp.float32
BF16 = jnp.bfloat16
VMEM = pltpu.VMEM
LIMIT = 28 * 1024 * 1024
WHOLE = 60 * 1024 * 1024
PASS = 53 * 1024 * 1024


def table(ids, experts):
    toks = ids.shape[1]
    expert = lax.broadcasted_iota(jnp.int32, (experts, toks), 0)
    first = ids[0:1, :] == expert
    second = ids[1:2, :] == expert
    named = jnp.where(first | second, 1.0, 0.0)
    earlier = lax.broadcasted_iota(jnp.int32, (toks, toks), 0)
    later = lax.broadcasted_iota(jnp.int32, (toks, toks), 1)
    before = jnp.where(earlier < later, 1.0, 0.0).astype(BF16)
    rank = jnp.dot(named.astype(BF16), before, preferred_element_type=F32)
    return first, second, jnp.where(named > 0.0, rank, -1.0)


def choose(ids, gate, slots):
    experts, count, toks = slots.shape
    first, second, rank = table(ids, experts)
    gate = jnp.where(first, gate[0:1, :], 0.0) + jnp.where(second, gate[1:2, :], 0.0)
    hit = (rank[:, None, :] == slots.astype(F32)).reshape(experts * count, toks)
    weight = jnp.broadcast_to(gate[:, None, :], slots.shape).reshape(experts * count, toks)
    scale = jnp.sum(jnp.where(hit, weight, 0.0), axis=1, keepdims=True)
    return jnp.where(hit, 1.0, 0.0), scale


def far_kernel(ids_ref, gate_ref, act_ref, grad_ref, out_ref):
    experts, _, count, tile = out_ref.shape
    toks = ids_ref.shape[1]
    slots = lax.broadcasted_iota(jnp.int32, (experts, count, toks), 1)
    mask, scale = choose(ids_ref[...], gate_ref[...], slots)
    mask = mask.astype(BF16)
    rows = jnp.dot(mask, act_ref[...], preferred_element_type=F32).astype(BF16)
    picked = jnp.dot(mask, grad_ref[...], preferred_element_type=F32)
    out_ref[:, 0] = rows.reshape(experts, count, tile)
    out_ref[:, 1] = (picked * scale).astype(BF16).reshape(experts, count, tile)


def near_kernel(
    half, tp_ref, ids_hbm, gate_hbm, act_hbm, grad_hbm, out_ref, ids_ref, gate_ref, act_ref, grad_ref, sems
):
    pairs = ((ids_hbm, ids_ref), (gate_hbm, gate_ref), (act_hbm, act_ref), (grad_hbm, grad_ref))
    copies = [pltpu.make_async_copy(a, b, sems.at[i]) for i, (a, b) in enumerate(pairs)]
    for copy in copies:
        copy.start()
    experts, toks = out_ref.shape[0], ids_ref.shape[1]
    inner = lax.broadcasted_iota(jnp.int32, (experts, 8, toks), 1)
    slots = jnp.where(inner < 4, half + 2 * tp_ref[0] + inner % 2, -2)
    copies[0].wait()
    copies[1].wait()
    mask, scale = choose(ids_ref[...], gate_ref[...], slots)
    kind = (inner // 2).reshape(mask.shape)
    of_rows = jnp.where(kind == 0, mask, 0.0).astype(BF16)
    of_grads = jnp.where(kind == 1, mask, 0.0).astype(BF16)
    copies[2].wait()
    copies[3].wait()
    rows = jnp.dot(of_rows, act_ref[...], preferred_element_type=F32)
    picked = jnp.dot(of_grads, grad_ref[...], preferred_element_type=F32)
    both = (rows + picked * scale).reshape(experts, 8, -1)
    out_ref[...] = both[:, :4].astype(BF16)


def send_far(ids_t, gate_t, acts, grads, experts, half):
    toks, width = acts.shape
    tile = width // 4
    return pl.pallas_call(
        far_kernel,
        grid=(width // tile,),
        in_specs=[
            pl.BlockSpec((2, toks), lambda i: (0, 0)),
            pl.BlockSpec((2, toks), lambda i: (0, 0)),
            pl.BlockSpec((toks, tile), lambda i: (0, i)),
            pl.BlockSpec((toks, tile), lambda i: (0, i)),
        ],
        out_specs=pl.BlockSpec((experts, 2, half, tile), lambda i: (0, 0, 0, i)),
        out_shape=jax.ShapeDtypeStruct((experts, 2, half, width), BF16),
        compiler_params=pltpu.CompilerParams(vmem_limit_bytes=WHOLE),
        cost_estimate=pl.CostEstimate(
            flops=16 * experts * half * toks * width,
            bytes_accessed=4 * (toks + experts * half) * width,
            transcendentals=0,
        ),
    )(ids_t, gate_t, acts, grads)


def send_near(tp_at, ids_t, gate_t, acts, grads, experts, half):
    toks, width = acts.shape
    return pl.pallas_call(
        functools.partial(near_kernel, half),
        in_specs=[pl.BlockSpec(memory_space=pltpu.SMEM)]
        + [pl.BlockSpec(memory_space=pltpu.HBM)] * 4,
        out_specs=pl.BlockSpec(memory_space=VMEM),
        out_shape=jax.ShapeDtypeStruct((experts, 4, width), BF16),
        scratch_shapes=[
            VMEM((2, toks), ids_t.dtype),
            VMEM((2, toks), gate_t.dtype),
            VMEM((toks, width), acts.dtype),
            VMEM((toks, width), grads.dtype),
            pltpu.SemaphoreType.DMA((4,)),
        ],
        compiler_params=pltpu.CompilerParams(vmem_limit_bytes=WHOLE),
    )(tp_at, ids_t, gate_t, acts, grads)


def sort_kernel(in_ref, out_ref):
    every = in_ref[...].astype(F32)
    for kind in range(2):
        some = every[:, 2 * kind : 2 * kind + 2].reshape(out_ref.shape[1], -1)
        out_ref[kind] = some.astype(BF16)


def sort_kinds(near):
    chips, _, width = near.shape
    tile = width // 2
    return pl.pallas_call(
        sort_kernel,
        grid=(width // tile,),
        in_specs=[pl.BlockSpec((chips, 4, tile), lambda i: (0, 0, i))],
        out_specs=pl.BlockSpec((2, 2 * chips, tile), lambda i: (0, 0, i)),
        out_shape=pltpu.HBM((2, 2 * chips, width), BF16),
        compiler_params=pltpu.CompilerParams(vmem_limit_bytes=LIMIT),
    )(near)


def expert_kernel(
    far_ref, near_ref, g0, u0, g1, u1, d0, d1, part_ref, side_ref, pre_acc, back_acc, both_ref, kept
):
    units = g0.shape[0]
    half = pre_acc.shape[0] // 2
    contract = (((1,), (1,)), ((), ()))
    phase, at = pl.program_id(0), pl.program_id(1)

    @pl.when(phase == 0)
    def _():
        for i, ref in enumerate((g0, u0, g1, u1)):
            kept[at, i * units : (i + 1) * units] = ref[...]
        down = jnp.concatenate([d0[...], d1[...]], axis=0)
        x, g = [
            jnp.concatenate([ref[:, k].reshape(half, -1) for ref in (far_ref, near_ref)], axis=0)
            for k in range(2)
        ]
        pre = lax.dot_general(x, kept[at], contract, preferred_element_type=F32)
        back = lax.dot_general(g, down, contract, preferred_element_type=F32)

        @pl.when(at == 0)
        def _():
            pre_acc[...] = pre
            back_acc[...] = back

        @pl.when(at > 0)
        def _():
            pre_acc[...] += pre
            back_acc[...] += back

    @pl.when((phase == 0) & (at == pl.num_programs(1) - 1))
    def _():
        for i in range(2):
            pre_gate = pre_acc[:, 2 * i * units : (2 * i + 1) * units]
            pre_up = pre_acc[:, (2 * i + 1) * units : (2 * i + 2) * units]
            back = back_acc[:, i * units : (i + 1) * units]
            sig = jax.nn.sigmoid(pre_gate)
            silu = pre_gate * sig
            hidden = (silu * pre_up).astype(BF16)
            d_gate = (back * pre_up * sig * (1.0 + pre_gate * (1.0 - sig))).astype(BF16)
            d_up = (back * silu).astype(BF16)
            base = 3 * i * units
            side_ref[:, base : base + units] = d_gate
            side_ref[:, base + units : base + 2 * units] = d_up
            side_ref[:, base + 2 * units : base + 3 * units] = hidden
            both_ref[:, 2 * i * units : (2 * i + 1) * units] = d_gate
            both_ref[:, (2 * i + 1) * units : (2 * i + 2) * units] = d_up
        outer, inner = near_ref.shape[0], near_ref.shape[2]
        to = lax.broadcasted_iota(jnp.int32, (half, half), 0)
        of = lax.broadcasted_iota(jnp.int32, (half, half), 1)
        chip, place = to // (2 * outer), to % (2 * outer)
        moved = of == (place // 2) * inner + 2 * chip + place % 2
        moved = jnp.where(moved, 1.0, 0.0).astype(BF16)
        both_ref[half:] = jnp.dot(moved, both_ref[half:], preferred_element_type=F32).astype(BF16)

    @pl.when(phase == 1)
    def _():
        part = jnp.dot(both_ref[...], kept[at], preferred_element_type=F32).astype(BF16)
        wide = part_ref.shape[2] // 2
        for j in range(part_ref.shape[0]):
            cut = part[:, j * wide : (j + 1) * wide]
            part_ref[j] = jnp.concatenate([cut[:half], cut[half:]], axis=1)


def expert_part(far, near, weights, pieces):
    width = far.shape[3]
    half = far.shape[0] * far.shape[2]
    units = weights[0].shape[0]
    steps = 2
    tile = width // steps
    last = steps - 1

    def first_phase(p, i):
        return jnp.where(p == 0, i, last)

    return pl.pallas_call(
        expert_kernel,
        grid=(2, steps),
        in_specs=[
            pl.BlockSpec(src.shape[:3] + (tile,), lambda p, i: (0, 0, 0, first_phase(p, i)))
            for src in (far, near)
        ]
        + [pl.BlockSpec((units, tile), lambda p, i: (0, first_phase(p, i)))] * 6,
        out_specs=[
            pl.BlockSpec((pieces // steps, half, 2 * width // pieces), lambda p, i: (p * i, 0, 0)),
            pl.BlockSpec((2 * half, 6 * units), lambda p, i: (0, 0)),
        ],
        out_shape=[
            pltpu.HBM((pieces, half, 2 * width // pieces), BF16),
            jax.ShapeDtypeStruct((2 * half, 6 * units), BF16),
        ],
        scratch_shapes=[
            VMEM((2 * half, 4 * units), F32),
            VMEM((2 * half, 2 * units), F32),
            VMEM((2 * half, 4 * units), BF16),
            VMEM((steps, 4 * units, tile), BF16),
        ],
        compiler_params=pltpu.CompilerParams(vmem_limit_bytes=PASS),
        cost_estimate=pl.CostEstimate(
            flops=40 * half * width * units,
            bytes_accessed=2 * (6 * half * width + 6 * units * width),
            transcendentals=4 * half * units,
        ),
    )(far, near, *weights)


def weight_kernel(base, far_ref, near_ref, side_ref, *refs):
    tile = far_ref.shape[3]
    units = side_ref.shape[1] // 6
    contract = (((0,), (0,)), ((), ()))
    base = base * units

    def stacked(kind):
        return jnp.concatenate(
            [ref[:, kind].reshape(-1, tile) for ref in (far_ref, near_ref)], axis=0
        )

    left = side_ref[:, base : base + 2 * units]
    pair = lax.dot_general(left, stacked(0), contract, preferred_element_type=F32)
    left = side_ref[:, base + 2 * units : base + 3 * units]
    down = lax.dot_general(left, stacked(1), contract, preferred_element_type=F32)
    if len(refs) == 1:
        refs[0][: 2 * units] = pair.astype(BF16)
        refs[0][2 * units :] = down.astype(BF16)
    else:
        more_ref, gate_ref, up_ref, down_ref = refs
        pair += more_ref[: 2 * units].astype(F32)
        down += more_ref[2 * units :].astype(F32)
        gate_ref[...] = pair[:units].astype(BF16)
        up_ref[...] = pair[units:].astype(BF16)
        down_ref[...] = down.astype(BF16)


def weight_grads(far, near, side, more):
    width = far.shape[3]
    units = side.shape[1] // 6
    tile = width // 4
    specs = [
        pl.BlockSpec(far.shape[:3] + (tile,), lambda i: (0, 0, 0, i)),
        pl.BlockSpec(near.shape[:3] + (tile,), lambda i: (0, 0, 0, i)),
        pl.BlockSpec(side.shape, lambda i: (0, 0)),
    ]
    three = pl.BlockSpec((3 * units, tile), lambda i: (0, i))
    one = pl.BlockSpec((units, tile), lambda i: (0, i))
    if more is None:
        base, operands = 3, (far, near, side)
        out_specs, out_shape = three, jax.ShapeDtypeStruct((3 * units, width), BF16)
    else:
        base, operands = 0, (far, near, side, more)
        specs = specs + [three]
        out_specs, out_shape = [one] * 3, [jax.ShapeDtypeStruct((units, width), BF16)] * 3
    return pl.pallas_call(
        functools.partial(weight_kernel, base),
        grid=(width // tile,),
        in_specs=specs,
        out_specs=out_specs,
        out_shape=out_shape,
        compiler_params=pltpu.CompilerParams(vmem_limit_bytes=LIMIT),
        cost_estimate=pl.CostEstimate(
            flops=6 * side.shape[0] * width * units,
            bytes_accessed=2 * (2 * side.shape[0] * width + 6 * units * width),
            transcendentals=0,
        ),
    )(*operands)


def combine_kernel(ids_ref, back_ref, out_ref):
    experts, half = back_ref.shape[0], back_ref.shape[1]
    toks = ids_ref.shape[1]
    wide = out_ref.shape[1]
    _, _, rank = table(ids_ref[...], experts)
    slots = lax.broadcasted_iota(jnp.int32, (experts, half, toks), 1)
    rows = back_ref[...].reshape(experts * half, 2 * wide)
    total = gather_slots(rank, slots.astype(F32), rows)[:, :wide]
    total += gather_slots(rank, (slots + half).astype(F32), rows)[:, wide:]
    out_ref[...] = total.astype(BF16)


def gather_slots(rank, slots, rows):
    hit = jnp.where(rank[:, None, :] == slots, 1.0, 0.0).astype(BF16).reshape(rows.shape[0], -1)
    return lax.dot_general(hit, rows, (((0,), (0,)), ((), ())), preferred_element_type=F32)


def combine(ids_t, returned):
    toks = ids_t.shape[1]
    return pl.pallas_call(
        combine_kernel,
        in_specs=[pl.BlockSpec(memory_space=VMEM)] * 2,
        out_specs=pl.BlockSpec(memory_space=VMEM),
        out_shape=jax.ShapeDtypeStruct((toks, returned.shape[2] // 2), BF16),
        compiler_params=pltpu.CompilerParams(vmem_limit_bytes=LIMIT),
    )(ids_t, returned)


def order_kernel(tp_ref, *refs):
    pieces, out_ref, kept = refs[:-2], refs[-2], refs[-1]
    count, toks, wide = kept.shape
    reach = count // 2 - 1
    me = tp_ref[0]
    kept[me] = pieces[0][...]
    for step in range(1, reach + 1):
        kept[lax.rem(me + count - step, count)] = pieces[2 * step - 1][...]
        kept[lax.rem(me + step, count)] = pieces[2 * step][...]
    kept[lax.rem(me + count // 2, count)] = pieces[-1][...]
    for k in range(0, count, 2):
        out_ref[:, k * wide : (k + 2) * wide] = jnp.concatenate([kept[k], kept[k + 1]], axis=1)


def gather_columns(tp_at, piece, count):
    toks, wide = piece.shape
    up = [(i, (i + 1) % count) for i in range(count)]
    down = [(i, (i - 1) % count) for i in range(count)]
    from_below, from_above = piece, piece
    pieces = [piece]
    for _ in range(count // 2 - 1):
        from_below = lax.ppermute(from_below, "tp", up)
        from_above = lax.ppermute(from_above, "tp", down)
        pieces += [from_below, from_above]
    pieces.append(lax.ppermute(from_below, "tp", up))
    return pl.pallas_call(
        order_kernel,
        in_specs=[pl.BlockSpec(memory_space=pltpu.SMEM)]
        + [pl.BlockSpec(memory_space=VMEM)] * len(pieces),
        out_specs=pl.BlockSpec(memory_space=VMEM),
        out_shape=jax.ShapeDtypeStruct((toks, count * wide), BF16),
        scratch_shapes=[VMEM((count, toks, wide), BF16)],
        compiler_params=pltpu.CompilerParams(vmem_limit_bytes=LIMIT),
    )(tp_at, *pieces)


def per_device(activations, out_grad, expert_ids, gate_values, gate_proj, up_proj, down_proj):
    devices = lax.axis_size("exp")
    planes = lax.axis_size("tp")
    experts = devices // 2
    toks, width = activations.shape
    slots = 8 * toks // devices
    half = slots // 2
    tp_at = lax.axis_index("tp").astype(jnp.int32)[None]
    ids_t = expert_ids.T
    gate_t = gate_values.T
    swap = [(i, i ^ 1) for i in range(devices)]

    def trade(v):
        return lax.ppermute(v, "exp", swap)

    sides = [list(range(core, devices, 2)) for core in range(2)]

    def spread(v):
        return lax.all_to_all(
            v, "exp", split_axis=0, concat_axis=0, tiled=True, axis_index_groups=sides
        )

    near = send_near(tp_at, ids_t, gate_t, activations, out_grad, experts, half)
    own = (gate_proj[0], up_proj[0], down_proj[0])
    other = tuple(trade(v) for v in own)
    other, ids_t = lax.optimization_barrier((other, ids_t))
    near = spread(near)
    far = send_far(ids_t, gate_t, activations, out_grad, experts, half)
    near, far = lax.optimization_barrier((near, far))
    near = sort_kinds(near)
    near = lax.all_gather(near, "tp", axis=0, tiled=False)
    far = spread(far.reshape(experts, 2 * half, width)).reshape(far.shape)
    weights = (own[0], own[1], other[0], other[1], own[2], other[2])
    both, side = expert_part(far, near, weights, planes)
    both, side = lax.optimization_barrier((both, side))
    shared = trade(weight_grads(far, near, side, None))
    gate_g, up_g, down_g = weight_grads(far, near, side, shared)
    mine = lax.psum_scatter(both, "tp", scatter_dimension=0, tiled=False)
    mine, gate_g, up_g, down_g = lax.optimization_barrier((mine, gate_g, up_g, down_g))
    returned = spread(mine.reshape(experts, half, -1))
    piece = combine(ids_t, returned)
    in_grad = gather_columns(tp_at, piece, planes)
    return (in_grad, gate_g[None], up_g[None], down_g[None])


def solution(mesh):
    return jax.shard_map(
        per_device,
        mesh=mesh,
        in_specs=(
            P("exp", None),
            P("exp", None),
            P("exp", None),
            P("exp", None),
            P("exp", "tp", None),
            P("exp", "tp", None),
            P("exp", "tp", None),
        ),
        out_specs=(
            P("exp", None),
            P("exp", "tp", None),
            P("exp", "tp", None),
            P("exp", "tp", None),
        ),
        check_vma=False,
    )
```

```python
import functools

import jax
import jax.numpy as jnp
from jax import lax
from jax.experimental import pallas as pl
from jax.experimental.pallas import tpu as pltpu
from jax.sharding import PartitionSpec as P

F32 = jnp.float32
BF16 = jnp.bfloat16
VMEM = pltpu.VMEM
LIMIT = 28 * 1024 * 1024
WHOLE = 60 * 1024 * 1024
PASS = 53 * 1024 * 1024


def table(ids, experts):
    toks = ids.shape[1]
    expert = lax.broadcasted_iota(jnp.int32, (experts, toks), 0)
    first = ids[0:1, :] == expert
    second = ids[1:2, :] == expert
    named = jnp.where(first | second, 1.0, 0.0)
    earlier = lax.broadcasted_iota(jnp.int32, (toks, toks), 0)
    later = lax.broadcasted_iota(jnp.int32, (toks, toks), 1)
    before = jnp.where(earlier < later, 1.0, 0.0).astype(BF16)
    rank = jnp.dot(named.astype(BF16), before, preferred_element_type=F32)
    return first, second, jnp.where(named > 0.0, rank, -1.0)


def choose(ids, gate, slots):
    experts, count, toks = slots.shape
    first, second, rank = table(ids, experts)
    gate = jnp.where(first, gate[0:1, :], 0.0) + jnp.where(second, gate[1:2, :], 0.0)
    hit = (rank[:, None, :] == slots.astype(F32)).reshape(experts * count, toks)
    weight = jnp.broadcast_to(gate[:, None, :], slots.shape).reshape(experts * count, toks)
    scale = jnp.sum(jnp.where(hit, weight, 0.0), axis=1, keepdims=True)
    return jnp.where(hit, 1.0, 0.0), scale


def far_kernel(ids_ref, gate_ref, act_ref, grad_ref, out_ref):
    experts, _, count, tile = out_ref.shape
    toks = ids_ref.shape[1]
    slots = lax.broadcasted_iota(jnp.int32, (experts, count, toks), 1)
    mask, scale = choose(ids_ref[...], gate_ref[...], slots)
    mask = mask.astype(BF16)
    rows = jnp.dot(mask, act_ref[...], preferred_element_type=F32).astype(BF16)
    picked = jnp.dot(mask, grad_ref[...], preferred_element_type=F32)
    out_ref[:, 0] = rows.reshape(experts, count, tile)
    out_ref[:, 1] = (picked * scale).astype(BF16).reshape(experts, count, tile)


def near_kernel(
    half, tp_ref, ids_hbm, gate_hbm, act_hbm, grad_hbm, out_ref, ids_ref, gate_ref, act_ref, grad_ref, sems
):
    pairs = ((ids_hbm, ids_ref), (gate_hbm, gate_ref), (act_hbm, act_ref), (grad_hbm, grad_ref))
    copies = [pltpu.make_async_copy(a, b, sems.at[i]) for i, (a, b) in enumerate(pairs)]
    for copy in copies:
        copy.start()
    experts, toks = out_ref.shape[0], ids_ref.shape[1]
    inner = lax.broadcasted_iota(jnp.int32, (experts, 8, toks), 1)
    slots = jnp.where(inner < 4, half + 2 * tp_ref[0] + inner % 2, -2)
    copies[0].wait()
    copies[1].wait()
    mask, scale = choose(ids_ref[...], gate_ref[...], slots)
    kind = (inner // 2).reshape(mask.shape)
    of_rows = jnp.where(kind == 0, mask, 0.0).astype(BF16)
    of_grads = jnp.where(kind == 1, mask, 0.0).astype(BF16)
    copies[2].wait()
    copies[3].wait()
    rows = jnp.dot(of_rows, act_ref[...], preferred_element_type=F32)
    picked = jnp.dot(of_grads, grad_ref[...], preferred_element_type=F32)
    both = (rows + picked * scale).reshape(experts, 8, -1)
    out_ref[...] = both[:, :4].astype(BF16)


def send_far(ids_t, gate_t, acts, grads, experts, half):
    toks, width = acts.shape
    tile = width // 4
    return pl.pallas_call(
        far_kernel,
        grid=(width // tile,),
        in_specs=[
            pl.BlockSpec((2, toks), lambda i: (0, 0)),
            pl.BlockSpec((2, toks), lambda i: (0, 0)),
            pl.BlockSpec((toks, tile), lambda i: (0, i)),
            pl.BlockSpec((toks, tile), lambda i: (0, i)),
        ],
        out_specs=pl.BlockSpec((experts, 2, half, tile), lambda i: (0, 0, 0, i)),
        out_shape=jax.ShapeDtypeStruct((experts, 2, half, width), BF16),
        compiler_params=pltpu.CompilerParams(vmem_limit_bytes=WHOLE),
        cost_estimate=pl.CostEstimate(
            flops=16 * experts * half * toks * width,
            bytes_accessed=4 * (toks + experts * half) * width,
            transcendentals=0,
        ),
    )(ids_t, gate_t, acts, grads)


def send_near(tp_at, ids_t, gate_t, acts, grads, experts, half):
    toks, width = acts.shape
    return pl.pallas_call(
        functools.partial(near_kernel, half),
        in_specs=[pl.BlockSpec(memory_space=pltpu.SMEM)]
        + [pl.BlockSpec(memory_space=pltpu.HBM)] * 4,
        out_specs=pl.BlockSpec(memory_space=VMEM),
        out_shape=jax.ShapeDtypeStruct((experts, 4, width), BF16),
        scratch_shapes=[
            VMEM((2, toks), ids_t.dtype),
            VMEM((2, toks), gate_t.dtype),
            VMEM((toks, width), acts.dtype),
            VMEM((toks, width), grads.dtype),
            pltpu.SemaphoreType.DMA((4,)),
        ],
        compiler_params=pltpu.CompilerParams(vmem_limit_bytes=WHOLE),
    )(tp_at, ids_t, gate_t, acts, grads)


def sort_kernel(in_ref, out_ref):
    every = in_ref[...].astype(F32)
    for kind in range(2):
        some = every[:, 2 * kind : 2 * kind + 2].reshape(out_ref.shape[1], -1)
        out_ref[kind] = some.astype(BF16)


def sort_kinds(near):
    chips, _, width = near.shape
    tile = width // 2
    return pl.pallas_call(
        sort_kernel,
        grid=(width // tile,),
        in_specs=[pl.BlockSpec((chips, 4, tile), lambda i: (0, 0, i))],
        out_specs=pl.BlockSpec((2, 2 * chips, tile), lambda i: (0, 0, i)),
        out_shape=pltpu.HBM((2, 2 * chips, width), BF16),
        compiler_params=pltpu.CompilerParams(vmem_limit_bytes=LIMIT),
    )(near)


def expert_kernel(
    far_ref, near_ref, g0, u0, g1, u1, d0, d1, part_ref, side_ref, pre_acc, back_acc, both_ref, kept
):
    units = g0.shape[0]
    half = pre_acc.shape[0] // 2
    contract = (((1,), (1,)), ((), ()))
    phase, at = pl.program_id(0), pl.program_id(1)

    @pl.when(phase == 0)
    def _():
        for i, ref in enumerate((g0, u0, g1, u1)):
            kept[at, i * units : (i + 1) * units] = ref[...]
        down = jnp.concatenate([d0[...], d1[...]], axis=0)
        x, g = [
            jnp.concatenate([ref[:, k].reshape(half, -1) for ref in (far_ref, near_ref)], axis=0)
            for k in range(2)
        ]
        pre = lax.dot_general(x, kept[at], contract, preferred_element_type=F32)
        back = lax.dot_general(g, down, contract, preferred_element_type=F32)

        @pl.when(at == 0)
        def _():
            pre_acc[...] = pre
            back_acc[...] = back

        @pl.when(at > 0)
        def _():
            pre_acc[...] += pre
            back_acc[...] += back

    @pl.when((phase == 0) & (at == pl.num_programs(1) - 1))
    def _():
        for i in range(2):
            pre_gate = pre_acc[:, 2 * i * units : (2 * i + 1) * units]
            pre_up = pre_acc[:, (2 * i + 1) * units : (2 * i + 2) * units]
            back = back_acc[:, i * units : (i + 1) * units]
            sig = jax.nn.sigmoid(pre_gate)
            silu = pre_gate * sig
            hidden = (silu * pre_up).astype(BF16)
            d_gate = (back * pre_up * sig * (1.0 + pre_gate * (1.0 - sig))).astype(BF16)
            d_up = (back * silu).astype(BF16)
            base = 3 * i * units
            side_ref[:, base : base + units] = d_gate
            side_ref[:, base + units : base + 2 * units] = d_up
            side_ref[:, base + 2 * units : base + 3 * units] = hidden
            both_ref[:, 2 * i * units : (2 * i + 1) * units] = d_gate
            both_ref[:, (2 * i + 1) * units : (2 * i + 2) * units] = d_up
        outer, inner = near_ref.shape[0], near_ref.shape[2]
        to = lax.broadcasted_iota(jnp.int32, (half, half), 0)
        of = lax.broadcasted_iota(jnp.int32, (half, half), 1)
        chip, place = to // (2 * outer), to % (2 * outer)
        moved = of == (place // 2) * inner + 2 * chip + place % 2
        moved = jnp.where(moved, 1.0, 0.0).astype(BF16)
        both_ref[half:] = jnp.dot(moved, both_ref[half:], preferred_element_type=F32).astype(BF16)

    @pl.when(phase == 1)
    def _():
        part = jnp.dot(both_ref[...], kept[at], preferred_element_type=F32).astype(BF16)
        wide = part_ref.shape[2] // 2
        for j in range(part_ref.shape[0]):
            cut = part[:, j * wide : (j + 1) * wide]
            part_ref[j] = jnp.concatenate([cut[:half], cut[half:]], axis=1)


def expert_part(far, near, weights, pieces):
    width = far.shape[3]
    half = far.shape[0] * far.shape[2]
    units = weights[0].shape[0]
    steps = 2
    tile = width // steps
    last = steps - 1

    def first_phase(p, i):
        return jnp.where(p == 0, i, last)

    return pl.pallas_call(
        expert_kernel,
        grid=(2, steps),
        in_specs=[
            pl.BlockSpec(src.shape[:3] + (tile,), lambda p, i: (0, 0, 0, first_phase(p, i)))
            for src in (far, near)
        ]
        + [pl.BlockSpec((units, tile), lambda p, i: (0, first_phase(p, i)))] * 6,
        out_specs=[
            pl.BlockSpec((pieces // steps, half, 2 * width // pieces), lambda p, i: (p * i, 0, 0)),
            pl.BlockSpec((2 * half, 6 * units), lambda p, i: (0, 0)),
        ],
        out_shape=[
            pltpu.HBM((pieces, half, 2 * width // pieces), BF16),
            jax.ShapeDtypeStruct((2 * half, 6 * units), BF16),
        ],
        scratch_shapes=[
            VMEM((2 * half, 4 * units), F32),
            VMEM((2 * half, 2 * units), F32),
            VMEM((2 * half, 4 * units), BF16),
            VMEM((steps, 4 * units, tile), BF16),
        ],
        compiler_params=pltpu.CompilerParams(vmem_limit_bytes=PASS),
        cost_estimate=pl.CostEstimate(
            flops=40 * half * width * units,
            bytes_accessed=2 * (6 * half * width + 6 * units * width),
            transcendentals=4 * half * units,
        ),
    )(far, near, *weights)


def weight_kernel(base, far_ref, near_ref, side_ref, *refs):
    tile = far_ref.shape[3]
    units = side_ref.shape[1] // 6
    contract = (((0,), (0,)), ((), ()))
    base = base * units

    def stacked(kind):
        return jnp.concatenate(
            [ref[:, kind].reshape(-1, tile) for ref in (far_ref, near_ref)], axis=0
        )

    left = side_ref[:, base : base + 2 * units]
    pair = lax.dot_general(left, stacked(0), contract, preferred_element_type=F32)
    left = side_ref[:, base + 2 * units : base + 3 * units]
    down = lax.dot_general(left, stacked(1), contract, preferred_element_type=F32)
    if len(refs) == 1:
        refs[0][: 2 * units] = pair.astype(BF16)
        refs[0][2 * units :] = down.astype(BF16)
    else:
        more_ref, gate_ref, up_ref, down_ref = refs
        pair += more_ref[: 2 * units].astype(F32)
        down += more_ref[2 * units :].astype(F32)
        gate_ref[...] = pair[:units].astype(BF16)
        up_ref[...] = pair[units:].astype(BF16)
        down_ref[...] = down.astype(BF16)


def weight_grads(far, near, side, more):
    width = far.shape[3]
    units = side.shape[1] // 6
    tile = width // 4
    specs = [
        pl.BlockSpec(far.shape[:3] + (tile,), lambda i: (0, 0, 0, i)),
        pl.BlockSpec(near.shape[:3] + (tile,), lambda i: (0, 0, 0, i)),
        pl.BlockSpec(side.shape, lambda i: (0, 0)),
    ]
    three = pl.BlockSpec((3 * units, tile), lambda i: (0, i))
    one = pl.BlockSpec((units, tile), lambda i: (0, i))
    if more is None:
        base, operands = 3, (far, near, side)
        out_specs, out_shape = three, jax.ShapeDtypeStruct((3 * units, width), BF16)
    else:
        base, operands = 0, (far, near, side, more)
        specs = specs + [three]
        out_specs, out_shape = [one] * 3, [jax.ShapeDtypeStruct((units, width), BF16)] * 3
    return pl.pallas_call(
        functools.partial(weight_kernel, base),
        grid=(width // tile,),
        in_specs=specs,
        out_specs=out_specs,
        out_shape=out_shape,
        compiler_params=pltpu.CompilerParams(vmem_limit_bytes=LIMIT),
        cost_estimate=pl.CostEstimate(
            flops=6 * side.shape[0] * width * units,
            bytes_accessed=2 * (2 * side.shape[0] * width + 6 * units * width),
            transcendentals=0,
        ),
    )(*operands)


def combine_kernel(ids_ref, back_ref, out_ref):
    experts, half = back_ref.shape[0], back_ref.shape[1]
    toks = ids_ref.shape[1]
    wide = out_ref.shape[1]
    _, _, rank = table(ids_ref[...], experts)
    slots = lax.broadcasted_iota(jnp.int32, (experts, half, toks), 1)
    rows = back_ref[...].reshape(experts * half, 2 * wide)
    total = gather_slots(rank, slots.astype(F32), rows)[:, :wide]
    total += gather_slots(rank, (slots + half).astype(F32), rows)[:, wide:]
    out_ref[...] = total.astype(BF16)


def gather_slots(rank, slots, rows):
    hit = jnp.where(rank[:, None, :] == slots, 1.0, 0.0).astype(BF16).reshape(rows.shape[0], -1)
    return lax.dot_general(hit, rows, (((0,), (0,)), ((), ())), preferred_element_type=F32)


def combine(ids_t, returned):
    toks = ids_t.shape[1]
    return pl.pallas_call(
        combine_kernel,
        in_specs=[pl.BlockSpec(memory_space=VMEM)] * 2,
        out_specs=pl.BlockSpec(memory_space=VMEM),
        out_shape=jax.ShapeDtypeStruct((toks, returned.shape[2] // 2), BF16),
        compiler_params=pltpu.CompilerParams(vmem_limit_bytes=LIMIT),
    )(ids_t, returned)


def order_kernel(tp_ref, *refs):
    pieces, out_ref, kept = refs[:-2], refs[-2], refs[-1]
    count, toks, wide = kept.shape
    reach = count // 2 - 1
    me = tp_ref[0]
    kept[me] = pieces[0][...]
    for step in range(1, reach + 1):
        kept[lax.rem(me + count - step, count)] = pieces[2 * step - 1][...]
        kept[lax.rem(me + step, count)] = pieces[2 * step][...]
    kept[lax.rem(me + count // 2, count)] = pieces[-1][...]
    for k in range(0, count, 2):
        out_ref[:, k * wide : (k + 2) * wide] = jnp.concatenate([kept[k], kept[k + 1]], axis=1)


def gather_columns(tp_at, piece, count):
    toks, wide = piece.shape
    up = [(i, (i + 1) % count) for i in range(count)]
    down = [(i, (i - 1) % count) for i in range(count)]
    from_below, from_above = piece, piece
    pieces = [piece]
    for _ in range(count // 2 - 1):
        from_below = lax.ppermute(from_below, "tp", up)
        from_above = lax.ppermute(from_above, "tp", down)
        pieces += [from_below, from_above]
    across = [(i, (i + count // 2) % count) for i in range(count)]
    pieces.append(lax.ppermute(piece, "tp", across))
    return pl.pallas_call(
        order_kernel,
        in_specs=[pl.BlockSpec(memory_space=pltpu.SMEM)]
        + [pl.BlockSpec(memory_space=VMEM)] * len(pieces),
        out_specs=pl.BlockSpec(memory_space=VMEM),
        out_shape=jax.ShapeDtypeStruct((toks, count * wide), BF16),
        scratch_shapes=[VMEM((count, toks, wide), BF16)],
        compiler_params=pltpu.CompilerParams(vmem_limit_bytes=LIMIT),
    )(tp_at, *pieces)


def per_device(activations, out_grad, expert_ids, gate_values, gate_proj, up_proj, down_proj):
    devices = lax.axis_size("exp")
    planes = lax.axis_size("tp")
    experts = devices // 2
    toks, width = activations.shape
    slots = 8 * toks // devices
    half = slots // 2
    tp_at = lax.axis_index("tp").astype(jnp.int32)[None]
    ids_t = expert_ids.T
    gate_t = gate_values.T
    swap = [(i, i ^ 1) for i in range(devices)]

    def trade(v):
        return lax.ppermute(v, "exp", swap)

    sides = [list(range(core, devices, 2)) for core in range(2)]

    def spread(v):
        return lax.all_to_all(
            v, "exp", split_axis=0, concat_axis=0, tiled=True, axis_index_groups=sides
        )

    near = send_near(tp_at, ids_t, gate_t, activations, out_grad, experts, half)
    own = (gate_proj[0], up_proj[0], down_proj[0])
    other = tuple(trade(v) for v in own)
    other, ids_t = lax.optimization_barrier((other, ids_t))
    near = spread(near)
    far = send_far(ids_t, gate_t, activations, out_grad, experts, half)
    near, far = lax.optimization_barrier((near, far))
    near = sort_kinds(near)
    near = lax.all_gather(near, "tp", axis=0, tiled=False)
    far = spread(far.reshape(experts, 2 * half, width)).reshape(far.shape)
    weights = (own[0], own[1], other[0], other[1], own[2], other[2])
    both, side = expert_part(far, near, weights, planes)
    both, side = lax.optimization_barrier((both, side))
    shared = trade(weight_grads(far, near, side, None))
    gate_g, up_g, down_g = weight_grads(far, near, side, shared)
    mine = lax.psum_scatter(both, "tp", scatter_dimension=0, tiled=False)
    mine, gate_g, up_g, down_g = lax.optimization_barrier((mine, gate_g, up_g, down_g))
    returned = spread(mine.reshape(experts, half, -1))
    piece = combine(ids_t, returned)
    in_grad = gather_columns(tp_at, piece, planes)
    return (in_grad, gate_g[None], up_g[None], down_g[None])


def solution(mesh):
    return jax.shard_map(
        per_device,
        mesh=mesh,
        in_specs=(
            P("exp", None),
            P("exp", None),
            P("exp", None),
            P("exp", None),
            P("exp", "tp", None),
            P("exp", "tp", None),
            P("exp", "tp", None),
        ),
        out_specs=(
            P("exp", None),
            P("exp", "tp", None),
            P("exp", "tp", None),
            P("exp", "tp", None),
        ),
        check_vma=False,
    )
```
